256 devices in a mesh: row: 32 (over y, z), col: 8 (over x, core).
Axes of the slice: x: 4, y: 4, z: 8, core: 2. Of those that a mesh axis runs over, the one named last changes fastest.
Arguments:
- queries: bfloat16 [16384, 1024], P(('row', 'col'))
- passages: bfloat16 [32768, 1024], P(('col', 'row'))
- positives: int32 [16384], P('row'), may hold values from 0 to 32767
Outputs:
- losses: float32 [16384], P('row')
- query_grad: float32 [16384, 1024], P(('row', 'col'))
- passage_grad: float32 [32768, 1024], P(('col', 'row'))
The draws below stay inside these ranges and needn't reach their ends.
All inputs are finite; a program needn't handle non-finite values.
Results may differ from the reference program's by a relative error of at most 0.0022.
Values may be sent and summed in bfloat16 or wider, within the bound.
No kernel may reach another device: no remote copies, remote signals or barrier semaphores. Data moves between devices by JAX's collectives and lax.ppermute only.
A program may use at most 128 MiB of HBM per device.

```python
import math
import jax
import jax.numpy as jnp
from jax import lax

D = 1024
NQ = 16384
NP = 32768


def passage_base(key):
    return jnp.clip(jax.random.normal(jax.random.fold_in(key, 11), (NP, D), jnp.float32), -6.0, 6.0)


def drawn_slots(key):
    slot_key = jax.random.fold_in(key, 13)
    query_offset = jax.random.randint(slot_key, (8,), 0, NQ // 8)
    passage_offset = jax.random.randint(jax.random.fold_in(slot_key, 1), (8,), 0, NP // 8 - 1)
    query_slots = jnp.arange(8, dtype=jnp.int32) * (NQ // 8) + query_offset
    passage_slots = jnp.arange(8, dtype=jnp.int32) * (NP // 8) + passage_offset
    return (query_slots, passage_slots)


def draw_passages(key, part):
    base = passage_base(key)
    query_slots, passage_slots = drawn_slots(key)
    key = jax.random.fold_in(key, 3)
    noise = jnp.clip(jax.random.normal(jax.random.fold_in(key, 17), (8, D), jnp.float32), -6.0, 6.0)
    spread = 0.15 * math.sqrt(D) / 32.0
    base = base.at[passage_slots + 1].set(0.99 * base[passage_slots] + spread * noise)
    return base.astype(jnp.bfloat16)


def draw_queries(key, part):
    base = passage_base(key)
    query_slots, passage_slots = drawn_slots(key)
    key = jax.random.fold_in(key, 5)
    values = jnp.clip(jax.random.normal(key, (NQ, D), jnp.float32), -6.0, 6.0)
    strength = 1.8 + 0.15 * jnp.arange(8, dtype=jnp.float32)
    values = values.at[query_slots].set(strength[:, None] * base[passage_slots])
    return values.astype(jnp.bfloat16)


def set_ends(array, own_key, smallest, largest):
    index_at = [jax.random.randint(jax.random.fold_in(own_key, axis), (), 0, length) for axis, length in enumerate(array.shape)]
    longest = array.shape.index(max(array.shape))
    neighbour = index_at[:longest] + [(index_at[longest] + 1) % array.shape[longest]] + index_at[longest + 1:]
    return array.at[tuple(index_at)].set(smallest).at[tuple(neighbour)].set(largest)


def setup_inputs(seed: int = 0) -> dict:
    streams_of = jax.random.split(jax.random.key(seed), 4)
    return {
        "queries": draw_queries(jax.random.fold_in(streams_of[3], 71), 0),
        "passages": draw_passages(jax.random.fold_in(streams_of[3], 71), 0),
        "positives": set_ends(jax.random.randint(streams_of[2], (NQ,), 0, NP), jax.random.fold_in(streams_of[2], 1), 0, NP - 1).astype(jnp.int32),
    }


def reference(queries, passages, positives):
    scale = 3.0 / math.sqrt(D)
    block = 512 if NQ % 512 == 0 else NQ
    query_blocks = queries.reshape(NQ // block, block, D)
    positive_blocks = positives.reshape(NQ // block, block)

    def one_block(total, item):
        query_rows, positive_rows = item
        scores = jnp.dot(query_rows, passages.T, preferred_element_type=jnp.float32) * scale
        top = lax.optimization_barrier(jnp.max(scores, axis=1, keepdims=True))
        summed = lax.optimization_barrier(jnp.sum(jnp.exp(scores - top), axis=1))
        lse = top[:, 0] + jnp.log(summed)
        column = lax.broadcasted_iota(jnp.int32, scores.shape, 1)
        hit = column == positive_rows[:, None]
        pos_score = lax.optimization_barrier(jnp.sum(jnp.where(hit, scores, 0.0), axis=1))
        losses = lse - pos_score
        weights = ((jnp.exp(scores - lse[:, None]) - hit.astype(jnp.float32)) * scale).astype(jnp.bfloat16)
        query_grad = jnp.dot(weights, passages, preferred_element_type=jnp.float32)
        total = total + jnp.dot(weights.T, query_rows, preferred_element_type=jnp.float32)
        return (total, (losses, query_grad))
    total, (losses, query_grad) = lax.scan(one_block, jnp.zeros((NP, D), jnp.float32), (query_blocks, positive_blocks))
    return (losses.reshape(NQ), query_grad.reshape(NQ, D), total)
```

```python
import functools
import math

import jax
import jax.numpy as jnp
from jax import lax
from jax.experimental import pallas as pl
from jax.experimental.pallas import tpu as pltpu
from jax.sharding import Mesh, PartitionSpec as P

D = 1024
NQ = 16384
SCALE = 3.0 / math.sqrt(D)
X, Y, Z, C = 4, 4, 8, 2
PLANE = ("y", "x", "core")
BF, F32, F16 = jnp.bfloat16, jnp.float32, jnp.float16
MIB = 1 << 20
PIECES = ((4, 0, 64), (4, 64, 64), (0, 0, 128), (-3, 0, 128), (3, 0, 128), (-2, 0, 128), (2, 0, 128), (-1, 0, 128), (1, 0, 128))


def params(mib):
    return pltpu.CompilerParams(vmem_limit_bytes=mib * MIB)


def cost(flops, read):
    return pl.CostEstimate(flops=flops, bytes_accessed=read, transcendentals=0)


def shift_z(v, k):
    return lax.ppermute(v, "z", [(i, (i + k) % Z) for i in range(Z)])


def flip_z(v, k):
    return lax.ppermute(v, "z", [(i, i ^ k) for i in range(Z)])


def shift_x(v, k):
    return lax.ppermute(v, "x", [(i, (i + k) % X) for i in range(X)])


def shift_y(v, k):
    return lax.ppermute(v, "y", [(i, (i + k) % Y) for i in range(Y)])


def swap_core(v):
    return lax.ppermute(v, "core", [(0, 1), (1, 0)])


def shift_plane(v, stage, k):
    pairs = []
    for y in range(Y):
        for x in range(X):
            for c in range(C):
                y2, x2 = (y, (x + k) % X) if c == stage else ((y + k) % Y, x)
                pairs.append(((y * X + x) * C + c, (y2 * X + x2) * C + c))
    return lax.ppermute(v, PLANE, pairs)


def axes_of(where, c):
    x, y = where[0], where[1]
    return jnp.where(c == 0, x, y), jnp.where(c == 0, y, x)


def assemble_kernel(where, own, right, left, right2, left2, out):
    first, second = axes_of(where, where[3])
    for i, (ref, part) in enumerate(((own, 0), (right, 0), (left, 0), (right2, 0), (left2, 2))):
        a = lax.rem(second + (0, 3, 1, 2, 2)[i], 4)
        for j in range(ref.shape[0] // 64):
            b = lax.rem(first + (0, 3, 1, 2)[j + part], 4)
            at = pl.ds(pl.multiple_of((a * 4 + b) * 64, 64), 64)
            out[at, :] = ref[j * 64 : (j + 1) * 64, :]


def assemble(where, pieces):
    vmem = pl.BlockSpec(memory_space=pltpu.VMEM)
    return pl.pallas_call(
        assemble_kernel,
        out_shape=jax.ShapeDtypeStruct((1024, D), BF),
        in_specs=[pl.BlockSpec(memory_space=pltpu.SMEM)] + [vmem] * 5,
        out_specs=vmem,
        compiler_params=params(8),
        cost_estimate=cost(0, 4 * MIB),
        name="assemble",
    )(where, *pieces)


def first_passage(where, offset):
    x, y, z, c = where[0], where[1], where[2], where[3]
    return (((x * C + c) * Y + y) * Z + lax.rem(z + offset + Z, Z)) * 128


def scores_kernel(where, q_own, q_other, positives, largest_q, *refs):
    pieces, (exps, stats, passages, largest_p) = refs[: len(PIECES)], refs[len(PIECES) :]
    i = pl.program_id(0)

    @pl.when(i == 0)
    def _():
        row = 0
        for ref in pieces:
            n = ref.shape[0]
            passages[row : row + n, :] = ref[...]
            row += n
        largest = jnp.max(jnp.abs(passages[...].astype(F32)), axis=0, keepdims=True)
        largest_p[...] = jnp.broadcast_to(jnp.max(largest, axis=1, keepdims=True), largest_p.shape)

    q = jnp.where(i < 4, q_own[...], q_other[...])
    s = lax.dot_general(passages[...], q, (((1,), (1,)), ((), ())), preferred_element_type=F32) * SCALE
    top = jnp.max(s, axis=0, keepdims=True)
    total = jnp.zeros_like(top)
    pos_score = jnp.zeros_like(top)
    row = 0
    for offset, start, n in PIECES:
        part = s[row : row + n, :]
        e = jnp.exp(part - top)
        exps[row : row + n, :] = e
        total += jnp.sum(e, axis=0, keepdims=True)
        index = first_passage(where, offset) + start + lax.broadcasted_iota(jnp.int32, part.shape, 0)
        pos_score += jnp.sum(jnp.where(index == positives[...], part, 0.0), axis=0, keepdims=True)
        row += n
    stats[0:1, :] = top
    stats[1:2, :] = total
    stats[2:3, :] = pos_score
    stats[3:4, :] = jnp.broadcast_to(largest_p[0:1, 0:1], top.shape)
    stats[4:5, :] = jnp.broadcast_to(largest_q[0:1, 0:1], top.shape)
    stats[5:8, :] = jnp.zeros((3, top.shape[1]), F32)


def column_block(i, where):
    c = where[3]
    return jnp.where(i < 4, c * 4 + i, (1 - c) * 4 + i - 4)


def scores(where, q_own, q_other, positives, largest_q, pieces):
    whole = lambda a: pl.BlockSpec(a.shape, lambda i, w: (0, 0))
    return pl.pallas_call(
        scores_kernel,
        out_shape=(
            jax.ShapeDtypeStruct((1024, 2048), F32),
            jax.ShapeDtypeStruct((8, 2048), F32),
            jax.ShapeDtypeStruct((1024, D), BF),
        ),
        grid_spec=pltpu.PrefetchScalarGridSpec(
            num_scalar_prefetch=1,
            grid=(8,),
            in_specs=[
                pl.BlockSpec((256, D), lambda i, w: (jnp.minimum(i, 3), 0)),
                pl.BlockSpec((256, D), lambda i, w: (jnp.maximum(i - 4, 0), 0)),
                pl.BlockSpec((1, 256), lambda i, w: (0, column_block(i, w))),
                whole(largest_q),
            ]
            + [whole(a) for a in pieces],
            out_specs=(
                pl.BlockSpec((1024, 256), lambda i, w: (0, column_block(i, w))),
                pl.BlockSpec((8, 256), lambda i, w: (0, column_block(i, w))),
                pl.BlockSpec((1024, D), lambda i, w: (0, 0)),
            ),
            scratch_shapes=[pltpu.VMEM((8, 128), F32)],
        ),
        compiler_params=params(40),
        cost_estimate=cost(2 * 1024 * 2048 * D, 18 * MIB),
        name="scores",
    )(where, q_own, q_other, positives, largest_q, *pieces)


def merge_rows(parts):
    top = functools.reduce(jnp.maximum, [p[0:1] for p in parts])
    totals = [p[1:2] * jnp.exp(p[0:1] - top) for p in parts]
    scores_ = [p[2:3] for p in parts]
    if len(parts) == 4:
        join = lambda v: (v[0] + v[3]) + (v[1] + v[2])
    else:
        join = lambda v: v[0] + v[1]
    rest = functools.reduce(jnp.maximum, [p[3:8] for p in parts])
    return top, join(totals), join(scores_), rest


def merge_kernel(*refs):
    out = refs[-1]
    top, total, pos_score, rest = merge_rows([r[...] for r in refs[:-1]])
    out[0:1, :] = top
    out[1:2, :] = total
    out[2:3, :] = pos_score
    out[3:8, :] = rest


def merge(parts):
    vmem = pl.BlockSpec(memory_space=pltpu.VMEM)
    return pl.pallas_call(
        merge_kernel,
        out_shape=jax.ShapeDtypeStruct((8, 2048), F32),
        in_specs=[vmem] * len(parts),
        out_specs=vmem,
        compiler_params=params(4),
        cost_estimate=cost(0, 512 * 1024),
        name="merge",
    )(*parts)


def finish_kernel(local, one, two, out):
    top, total, pos_score, rest = merge_rows([one[...], two[...]])
    lse = top + jnp.log(total)
    largest_p = jnp.maximum(rest[0:1], 1e-30)
    largest_q = jnp.maximum(rest[1:2], 1e-30)
    bound_q = (2.0 * SCALE) * largest_p
    bound_p = (NQ * SCALE) * largest_q
    out[0:1, :] = jnp.exp(local[0:1, :] - lse)
    out[1:2, :] = lse - pos_score
    out[2:3, :] = 60000.0 / bound_p
    out[3:4, :] = bound_p / 60000.0
    out[4:5, :] = 60000.0 / bound_q
    out[5:6, :] = bound_q / 60000.0
    out[6:8, :] = jnp.zeros_like(out[6:8, :])


def finish(local, one, two):
    vmem = pl.BlockSpec(memory_space=pltpu.VMEM)
    return pl.pallas_call(
        finish_kernel,
        out_shape=jax.ShapeDtypeStruct((8, 2048), F32),
        in_specs=[vmem] * 3,
        out_specs=vmem,
        compiler_params=params(4),
        cost_estimate=cost(0, 512 * 1024),
        name="finish",
    )(local, one, two)


def passage_kernel(rows, where, exps, q_own, q_other, positives, coef, grad, weights, acc):
    i = pl.program_id(0)
    q = jnp.where(i < 4, q_own[...], q_other[...])
    parts = []
    row = 0
    for offset, start, n in rows:
        index = first_passage(where, offset) + start + lax.broadcasted_iota(jnp.int32, (n, 256), 0)
        hit = (index == positives[...]).astype(F32)
        parts.append(((exps[row : row + n, :] * coef[0:1, :] - hit) * SCALE).astype(BF))
        row += n
    w = jnp.concatenate(parts, axis=0)
    weights[...] = w
    term = jnp.dot(w, q, preferred_element_type=F32)

    @pl.when(i == 0)
    def _():
        acc[...] = term

    @pl.when(i > 0)
    def _():
        acc[...] += term

    @pl.when(i == 7)
    def _():
        grad[...] = (acc[...] * coef[2:3, 0:1])


def passage_term(where, exps, q_own, q_other, positives, coef, rows, block):
    n = sum(r[2] for r in rows)
    return pl.pallas_call(
        functools.partial(passage_kernel, rows),
        out_shape=(jax.ShapeDtypeStruct((n, D), F32), jax.ShapeDtypeStruct((n, 2048), BF)),
        grid_spec=pltpu.PrefetchScalarGridSpec(
            num_scalar_prefetch=1,
            grid=(8,),
            in_specs=[
                pl.BlockSpec((n, 256), lambda i, w: (block, column_block(i, w))),
                pl.BlockSpec((256, D), lambda i, w: (jnp.minimum(i, 3), 0)),
                pl.BlockSpec((256, D), lambda i, w: (jnp.maximum(i - 4, 0), 0)),
                pl.BlockSpec((1, 256), lambda i, w: (0, column_block(i, w))),
                pl.BlockSpec((8, 256), lambda i, w: (0, column_block(i, w))),
            ],
            out_specs=(
                pl.BlockSpec((n, D), lambda i, w: (0, 0)),
                pl.BlockSpec((n, 256), lambda i, w: (0, column_block(i, w))),
            ),
            scratch_shapes=[pltpu.VMEM((n, D), F32)],
        ),
        compiler_params=params(16),
        cost_estimate=cost(2 * n * 2048 * D, 4 * MIB + 13 * n * 1024),
        name="passage_term",
    )(where, exps, q_own, q_other, positives, coef)


def query_kernel(own, where, passages, coef, *refs):
    weights, out = refs[:-1], refs[-1]
    w = jnp.concatenate([r[...] for r in weights], axis=0)
    g = lax.dot_general(w, passages[...], (((0,), (0,)), ((), ())), preferred_element_type=F32)
    g = g * coef[4:5, 0:1]
    first, _ = axes_of(where, where[3] if own else 1 - where[3])
    for b in range(4):
        at = lax.rem(b - first + 4, 4) * 64
        out[pl.ds(pl.multiple_of(at, 64), 64), :] = g[b * 64 : (b + 1) * 64, :]


def query_term(where, passages, coef, weights, own):
    def block(i, w):
        c = w[3] if own else 1 - w[3]
        _, second = axes_of(w, c)
        return (0, c * 4 + lax.rem(second + i, 4))

    return pl.pallas_call(
        functools.partial(query_kernel, own),
        out_shape=jax.ShapeDtypeStruct((1024, D), F32),
        grid_spec=pltpu.PrefetchScalarGridSpec(
            num_scalar_prefetch=1,
            grid=(4,),
            in_specs=[
                pl.BlockSpec((1024, D), lambda i, w: (0, 0)),
                pl.BlockSpec((8, 128), lambda i, w: (0, 0)),
            ]
            + [pl.BlockSpec((a.shape[0], 256), block) for a in weights],
            out_specs=pl.BlockSpec((256, D), lambda i, w: (i, 0)),
        ),
        compiler_params=params(24),
        cost_estimate=cost(2 * 1024 * 1024 * D, 8 * MIB),
        name="query_term",
    )(where, passages, coef, *weights)


def body(queries, passages, positives):
    x, y, z, c = (lax.axis_index(a) for a in ("x", "y", "z", "core"))
    where = jnp.stack([x, y, z, c]).astype(jnp.int32)

    pos = positives.reshape(4, 128)
    near = [pos, shift_y(pos, -1), shift_y(pos, 2), shift_y(pos, 1)]
    twice = jnp.stack(near + near)
    pos = lax.dynamic_slice_in_dim(twice, lax.rem(Y - y, Y), Y, axis=0)
    pos = pos.reshape(Y, X, C, 64)
    pos = jnp.stack([pos[:, :, 0], pos[:, :, 1].transpose(1, 0, 2)]).reshape(1, 2048)

    largest_q = jnp.full((8, 128), jnp.max(jnp.abs(queries.astype(F32))))
    for k in (1, 2, 4):
        largest_q = jnp.maximum(largest_q, flip_z(largest_q, k))

    q = jnp.concatenate([queries] + [shift_plane(queries, 0, k) for k in (1, -1, 2)])
    right, left = shift_z(passages, 1), shift_z(passages, -1)
    ring = [(right, left)]
    q_right, q_left = shift_plane(q, 1, 1), shift_plane(q, 1, -1)
    right, left = shift_z(right, 1), shift_z(left, -1)
    ring.append((right, left))
    q_right2, q_left2 = shift_plane(q_right[:128], 1, 1), shift_plane(q_left[128:], 1, -1)
    right, left = shift_z(right, 1), shift_z(left, -1)
    ring.append((right, left))
    q_own = assemble(where, (q, q_right, q_left, q_right2, q_left2))
    q_other = swap_core(q_own)
    far = (shift_z(right[:64], 1), shift_z(left[64:], -1))
    pieces = (*far, passages, *ring[2], *ring[1], *ring[0])

    exps, stats, p_all = scores(where, q_own, q_other, pos, largest_q, pieces)
    local = stats
    stats = merge([stats] + [shift_x(stats, k) for k in (1, -1, 2)])
    stats = merge([stats] + [shift_y(stats, k) for k in (1, -1, 2)])
    coef = finish(local, stats, swap_core(stats))
    losses = coef[1].reshape(C, 4, 4, 64)
    losses = jnp.stack([losses[0], losses[1].transpose(1, 0, 2)])
    losses = lax.dynamic_index_in_dim(losses, y, axis=1, keepdims=False)
    losses = losses.transpose(1, 0, 2).reshape(512)

    term = functools.partial(passage_term, where, exps, q_own, q_other, pos, coef)
    term4, w4 = term(PIECES[0:2], 0)
    term4 = term4.astype(F16)
    right, left = shift_z(term4[:64], 1), shift_z(term4[64:], -1)
    w = [w4]
    term3, w3 = term_rows(term, 1)
    right = jnp.concatenate([term3[128:192] + right.astype(F32), term3[192:]]).astype(F16)
    left = jnp.concatenate([term3[:64], term3[64:128] + left.astype(F32)]).astype(F16)
    right, left = shift_z(right, 1), shift_z(left, -1)
    w.append(w3)
    for k in (2, 3):
        term_k, w_k = term_rows(term, k)
        right = (term_k[128:] + right.astype(F32)).astype(F16)
        left = (term_k[:128] + left.astype(F32)).astype(F16)
        right, left = shift_z(right, 1), shift_z(left, -1)
        w.append(w_k)
    term0, w0 = term(PIECES[2:3], 1)
    w.insert(1, w0)
    passage_grad = (term0 + (right.astype(F32) + left.astype(F32))) * coef[3, 0]

    other = swap_core(query_term(where, p_all, coef, w, False).astype(F16))
    own = query_term(where, p_all, coef, w, True)
    groups = [(own[g * 256 : g * 256 + 256], other[g * 256 : g * 256 + 256].astype(F32)) for g in range(4)]
    moved = [shift_plane((u + v).astype(F16), 1, k).astype(F32) for k, (u, v) in enumerate(groups) if k]
    total = (sum(groups[0]) + moved[1]) + (moved[0] + moved[2])
    moved = [shift_plane(total[64 * k : 64 * k + 64].astype(F16), 0, k).astype(F32) for k in (1, 2, 3)]
    query_grad = ((total[:64] + moved[1]) + (moved[0] + moved[2])) * coef[5, 0]
    return losses, query_grad, passage_grad


def term_rows(term, k):
    return term(PIECES[2 * k + 1 : 2 * k + 3], k)


def solution(mesh):
    mesh = Mesh(mesh.devices.reshape(Y, Z, X, C), ("y", "z", "x", "core"))
    q_spec = P(("y", "z", "x", "core"), None)
    p_spec = P(("x", "core", "y", "z"), None)
    row_spec = P(("y", "z"))
    return jax.shard_map(
        body,
        mesh=mesh,
        in_specs=(q_spec, p_spec, row_spec),
        out_specs=(row_spec, q_spec, p_spec),
        check_vma=False,
    )
```

```python
import functools
import math

import jax
import jax.numpy as jnp
from jax import lax
from jax.experimental import pallas as pl
from jax.experimental.pallas import tpu as pltpu
from jax.sharding import Mesh, PartitionSpec as P

D = 1024
NQ = 16384
SCALE = 3.0 / math.sqrt(D)
TO_EXP2 = SCALE * math.log2(math.e)
X, Y, Z, C = 4, 4, 8, 2
PLANE = ("y", "x", "core")
BF, F32 = jnp.bfloat16, jnp.float32
MIB = 1 << 20
LARGEST = 46000.0
NEAR = ((0, 0, 128), (-3, 0, 128), (3, 0, 128), (-2, 0, 128), (2, 0, 128), (-1, 0, 128), (1, 0, 128))
FAR = ((4, 0, 64), (4, 64, 64))
N_NEAR, N_FAR = 896, 128
TILE = 16
VMEM = pl.BlockSpec(memory_space=pltpu.VMEM)
SMEM = pl.BlockSpec(memory_space=pltpu.SMEM)


def call(kernel, name, outs, args, scratch=(), mib=8, smem=0, alias=None):
    return pl.pallas_call(
        kernel,
        out_shape=[jax.ShapeDtypeStruct(s, t) for s, t in outs],
        in_specs=[SMEM] * smem + [VMEM] * (len(args) - smem),
        out_specs=[VMEM] * len(outs),
        scratch_shapes=list(scratch),
        input_output_aliases=alias or {},
        compiler_params=pltpu.CompilerParams(vmem_limit_bytes=mib * MIB),
        cost_estimate=pl.CostEstimate(flops=1000, bytes_accessed=1024, transcendentals=0),
        name=name,
    )(*args)


def shift_z(v, k):
    return lax.ppermute(v, "z", [(i, (i + k) % Z) for i in range(Z)])


def shift_x(v, k):
    return lax.ppermute(v, "x", [(i, (i + k) % X) for i in range(X)])


def shift_y(v, k):
    return lax.ppermute(v, "y", [(i, (i + k) % Y) for i in range(Y)])


def swap_core(v):
    return lax.ppermute(v, "core", [(0, 1), (1, 0)])


def shift_plane(v, stage, k):
    pairs = []
    for y in range(Y):
        for x in range(X):
            for c in range(C):
                y2, x2 = (y, (x + k) % X) if c == stage else ((y + k) % Y, x)
                pairs.append(((y * X + x) * C + c, (y2 * X + x2) * C + c))
    return lax.ppermute(v, PLANE, pairs)


def encode(v):
    v2 = v * v
    v4 = v2 * v2
    v8 = v4 * v4
    return jnp.where(v < 0, -v8, v8).astype(BF)


def decode(code):
    y = code.astype(F32)
    size = jnp.abs(y)
    v = jnp.exp2(jnp.log2(jnp.maximum(size, 1e-37)) * 0.125)
    v = jnp.where(size < 1e-37, 0.0, v)
    return jnp.where(y < 0, -v, v)


def axes_of(where, c):
    x, y = where[0], where[1]
    return jnp.where(c == 0, x, y), jnp.where(c == 0, y, x)


def largest(v):
    v = jnp.max(jnp.abs(v).astype(F32), axis=0, keepdims=True)
    return jnp.max(v, axis=1, keepdims=True)


def pack_kernel(passages, queries, out):
    out[:128, :] = passages[...]
    out[128:, :] = jnp.broadcast_to(largest(queries[...]), (TILE, D)).astype(BF)


def sort_positives(where, near, out):
    y, c = where[1], where[3]
    rows = []
    for a in range(4):
        r = near[0][...]
        for j in range(1, 4):
            r = jnp.where(lax.rem(y + j, 4) == a, near[j][...], r)
        rows.append(r)
    for k in range(4):
        for b in range(4):
            at = slice(b * 64, b * 64 + 64)
            core0, core1 = rows[k][b : b + 1, :64], rows[b][k : k + 1, 64:]
            out[k : k + 1, at] = jnp.where(c == 0, core0, core1)
            out[4 + k : 5 + k, at] = jnp.where(c == 0, core1, core0)


def round1_kernel(where, q0, q1, q2, q3, pos0, pos1, pos2, pos3, z_right, z_left, out, positives, *_):
    for i, ref in enumerate((q0, q1, q2, q3)):
        out[i * 64 : (i + 1) * 64, :] = ref[...]
    sort_positives(where, (pos0, pos1, pos2, pos3), positives)


def round2_kernel(q_right, q_left, z_right, z_left, right, left, *_):
    right[...] = q_right[:128, :]
    left[...] = q_left[128:, :]


def round3_kernel(where, own, right, left, right2, left2, z_right, z_left, out, far_right, far_left):
    first, second = axes_of(where, where[3])
    for i, (ref, part) in enumerate(((own, 0), (right, 0), (left, 0), (right2, 0), (left2, 2))):
        a = lax.rem(second + (0, 3, 1, 2, 2)[i], 4)
        for j in range(ref.shape[0] // 64):
            b = lax.rem(first + (0, 3, 1, 2)[j + part], 4)
            at = pl.ds(pl.multiple_of((a * 4 + b) * 64, 64), 64)
            out[at, :] = ref[j * 64 : (j + 1) * 64, :]
    far_right[:64, :] = z_right[:64, :]
    far_right[64:, :] = z_right[128:, :]
    far_left[...] = z_left[64:, :]


def losses_kernel(where, coef, out):
    y, c = where[1], where[3]
    v = coef[:, 512:768]
    core0, core1 = jnp.where(c == 0, v[:4], v[4:]), jnp.where(c == 0, v[4:], v[:4])
    for x in range(4):
        a, b = core0[0:1, x * 64 : x * 64 + 64], core1[x : x + 1, :64]
        for k in range(1, 4):
            a = jnp.where(y == k, core0[k : k + 1, x * 64 : x * 64 + 64], a)
            b = jnp.where(y == k, core1[x : x + 1, k * 64 : k * 64 + 64], b)
        out[x : x + 1, :64] = a
        out[x : x + 1, 64:] = b


def first_passage(where, offset):
    x, y, z, c = where[0], where[1], where[2], where[3]
    return (((x * C + c) * Y + y) * Z + lax.rem(z + offset + Z, Z)) * 128


def softmax(where, rows, raw, positives, exps, at):
    top = jnp.max(raw[...], axis=0, keepdims=True)
    total = jnp.zeros_like(top)
    pos_score = jnp.zeros_like(top)
    row = 0
    for offset, start, n in rows:
        part = raw[row : row + n, :]
        e = jnp.exp2((part - top) * TO_EXP2)
        exps[row : row + n, at] = e
        total += jnp.sum(e, axis=0, keepdims=True)
        hit = lax.broadcasted_iota(jnp.int32, part.shape, 0) == positives - (first_passage(where, offset) + start)
        pos_score += jnp.sum(jnp.where(hit, part, 0.0), axis=0, keepdims=True)
        row += n
    return top * SCALE, total, pos_score * SCALE


def product(p, q):
    return lax.dot_general(p, q, (((1,), (1,)), ((), ())), preferred_element_type=F32)


def near_scores_kernel(where, q, positives, *refs):
    pieces, (exps, stats, passages, raw0, raw1) = refs[: len(NEAR)], refs[len(NEAR) :]
    largest_q = None
    for i, ref in enumerate(pieces):
        passages[i * 128 : (i + 1) * 128, :] = ref[:128, :]
        v = ref[128:129, :128].astype(F32)
        largest_q = v if largest_q is None else jnp.maximum(largest_q, v)
    raws = (raw0, raw1)
    raw0[...] = product(passages[...], q[0:256, :])
    stats[4:8, :] = jnp.zeros((4, 896), F32)
    stats[0:4, 768:] = jnp.broadcast_to(largest_q, (4, 128))
    for i in range(4):
        if i < 3:
            raws[(i + 1) % 2][...] = product(passages[...], q[(i + 1) * 256 : (i + 2) * 256, :])
        at = slice(i * 256, (i + 1) * 256)
        top, total, pos_score = softmax(where, NEAR, raws[i % 2], positives[i : i + 1, :], exps, at)
        stats[i : i + 1, 0:256] = top
        stats[i : i + 1, 256:512] = total
        stats[i : i + 1, 512:768] = pos_score


def other_scores_kernel(
    where, q_own, q_other, positives, near, near_stats, far0, far1,
    far_exps, exps, stats, tops, passages, raw0, raw1, raw2,
):
    passages[:N_NEAR, :] = near[...]
    passages[N_NEAR : N_NEAR + 64, :] = far0[:64, :]
    passages[N_NEAR + 64 :, :] = far1[:64, :]
    largest_q = jnp.maximum(far0[64:65, :128].astype(F32), far1[64:65, :128].astype(F32))
    largest_q = jnp.maximum(largest_q, near_stats[0:1, 768:])
    stats[0:4, 768:] = jnp.broadcast_to(largest_q, (4, 128))
    stats[4:8, 768:] = jnp.broadcast_to(largest(passages[...]), (4, 128))
    raws = (raw0, raw1)
    raw0[...] = product(passages[...], q_other[0:256, :])
    for i in range(4):
        if i < 3:
            raws[(i + 1) % 2][...] = product(passages[...], q_other[(i + 1) * 256 : (i + 2) * 256, :])
        raw2[...] = product(passages[N_NEAR:, :], q_own[i * 256 : (i + 1) * 256, :])
        at = slice(i * 256, (i + 1) * 256)
        own, other = slice(i, i + 1), slice(4 + i, 5 + i)
        top, total, pos_score = softmax(where, NEAR + FAR, raws[i % 2], positives[other, :], exps, at)
        tops[other, 0:256] = top
        tops[other, 256:512] = top
        stats[other, 0:256] = top
        stats[other, 256:512] = total
        stats[other, 512:768] = pos_score
        top, total, pos_score = softmax(where, FAR, raw2, positives[own, :], far_exps, at)
        near_top = near_stats[own, 0:256]
        both = jnp.maximum(top, near_top)
        tops[own, 0:256] = near_top
        tops[own, 256:512] = top
        stats[own, 0:256] = both
        stats[own, 256:512] = total * jnp.exp(top - both) + near_stats[own, 256:512] * jnp.exp(near_top - both)
        stats[own, 512:768] = pos_score + near_stats[own, 512:768]


def merge_stats(parts):
    top = functools.reduce(jnp.maximum, [p[:, 0:256] for p in parts])
    totals = [p[:, 256:512] * jnp.exp(p[:, 0:256] - top) for p in parts]
    pos_scores = [p[:, 512:768] for p in parts]
    if len(parts) == 4:
        join = lambda v: (v[0] + v[3]) + (v[1] + v[2])
    else:
        join = lambda v: v[0] + v[1]
    rest = functools.reduce(jnp.maximum, [p[:, 768:] for p in parts])
    return top, join(totals), join(pos_scores), rest


def merge_kernel(*refs):
    out = refs[-1]
    top, total, pos_score, rest = merge_stats([r[...] for r in refs[:-1]])
    out[:, 0:256] = top
    out[:, 256:512] = total
    out[:, 512:768] = pos_score
    out[:, 768:] = rest


def finish_kernel(tops, one, two, out):
    two = jnp.concatenate(
        [jnp.concatenate([two[4:8, :768], two[0:4, :768]], axis=0), two[:, 768:]], axis=1
    )
    top, total, pos_score, rest = merge_stats([one[...], two])
    lse = top + jnp.log(total)
    out[:, 0:256] = jnp.exp(tops[:, 0:256] - lse)
    out[:, 256:512] = jnp.exp(tops[:, 256:512] - lse)
    out[:, 512:768] = lse - pos_score
    bound_p = (NQ * SCALE) * jnp.maximum(rest[0:1, :], 1e-30)
    bound_q = (2.0 * SCALE) * jnp.maximum(rest[4:5, :], 1e-30)
    out[0:1, 768:] = LARGEST / bound_p
    out[1:2, 768:] = bound_p / LARGEST
    out[2:3, 768:] = LARGEST / bound_q
    out[3:4, 768:] = bound_q / LARGEST
    out[4:8, 768:] = jnp.zeros((4, 128), F32)


def weigh(where, rows, exps, base, positives, coef, first, k, weights):
    for i in range(4):
        at = slice(i * 256, (i + 1) * 256)
        factor = coef[first + i : first + i + 1, k : k + 256]
        pos = positives[first + i : first + i + 1, :]
        row = 0
        for offset, start, n, r in rows:
            hit = lax.broadcasted_iota(jnp.int32, (n, 256), 0) == pos - (first_passage(where, offset) + start)
            e = exps[r - base : r - base + n, at]
            weights[row : row + n, at] = ((e * factor - hit.astype(F32)) * SCALE).astype(BF)
            row += n


def scaled_terms(w_own, w_other, q_own, q_other, scale, at):
    g = jnp.dot(w_own[...], q_own[:, at], preferred_element_type=F32)
    return (g + jnp.dot(w_other[...], q_other[:, at], preferred_element_type=F32)) * scale


BLOCKS = [(o, s, n, 128 * i) for i, (o, s, n) in enumerate(NEAR)]
FAR_BLOCKS = [(o, s, n, N_NEAR + s) for o, s, n in FAR]


def first_terms_kernel(
    where, near_exps, far_exps, other_exps, q_own, q_other, positives, coef,
    right, left, term_left, term_right, w_own, w_other, *_,
):
    weigh(where, FAR_BLOCKS, far_exps, N_NEAR, positives, coef, 0, 256, w_own.at[:128])
    weigh(where, BLOCKS[1:3], near_exps, 0, positives, coef, 0, 0, w_own.at[128:])
    weigh(where, FAR_BLOCKS + BLOCKS[1:3], other_exps, 0, positives, coef, 4, 0, w_other)
    for j in range(4):
        at = slice(j * 256, (j + 1) * 256)
        g = scaled_terms(w_own, w_other, q_own, q_other, coef[0:1, 768:769], at)
        right[:, at] = encode(g[:64])
        left[:, at] = encode(g[64:128])
        term_left[:, at] = g[128:256]
        term_right[:, at] = g[256:]


def other_terms_kernel(
    where, near_exps, other_exps, q_own, q_other, positives, coef, *outs
):
    grads, (w_own, w_other) = outs[:5], outs[5:]
    rows = [BLOCKS[0], *BLOCKS[3:]]
    weigh(where, rows, near_exps, 0, positives, coef, 0, 0, w_own)
    weigh(where, rows, other_exps, 0, positives, coef, 4, 0, w_other)
    for j in range(4):
        at = slice(j * 256, (j + 1) * 256)
        g = scaled_terms(w_own, w_other, q_own, q_other, coef[0:1, 768:769], at)
        for i, ref in enumerate(grads):
            ref[:, at] = g[i * 128 : (i + 1) * 128]


def add_halves_kernel(from_left, from_right, term_left, term_right, other0, other1, right, left, *_):
    right[:64, :] = encode(term_right[:64, :] + decode(from_left[...]))
    right[64:, :] = encode(term_right[64:, :])
    left[:64, :] = encode(term_left[:64, :])
    left[64:, :] = encode(term_left[64:, :] + decode(from_right[...]))


def add_kernel(from_left, from_right, term_left, term_right, right, left):
    right[...] = encode(term_right[...] + decode(from_left[...]))
    left[...] = encode(term_left[...] + decode(from_right[...]))


def last_add_kernel(coef, from_left, from_right, term, out):
    out[...] = (term[...] + (decode(from_left[...]) + decode(from_right[...]))) * coef[1:2, 768:769]


GROUPS = ((1, 0, 128), (0, 128, 384), (1, 128, 640), (0, 0, 128))


def query_terms(own, where, passages, coef, weights, i):
    _, second = axes_of(where, where[3] if own else 1 - where[3])
    at = pl.ds(pl.multiple_of(lax.rem(second + i, 4) * 256, 256), 256)
    w = jnp.concatenate([weights[k][u:v, at] for k, u, v in GROUPS], axis=0)
    g = lax.dot_general(w, passages[...], (((0,), (0,)), ((), ())), preferred_element_type=F32)
    return g * coef[2:3, 768:769]


def row_of(where, b):
    first, _ = axes_of(where, where[3])
    return pl.ds(pl.multiple_of(lax.rem(b - first + 4, 4) * 64, 64), 64)


def send_queries_kernel(where, passages, coef, w0, w1, out0, out1):
    for i in range(4):
        g = encode(query_terms(False, where, passages, coef, (w0, w1), i))
        (out0, out1)[i // 2][i % 2 * 256 : (i % 2 + 1) * 256, :] = g


def keep_queries_kernel(where, passages, coef, w0, w1, other0, other1, keep, *sent):
    for i, ref in enumerate((keep, *sent)):
        g = query_terms(True, where, passages, coef, (w0, w1), i)
        g += decode((other0, other1)[i // 2][i % 2 * 256 : (i % 2 + 1) * 256, :])
        g = g if i == 0 else encode(g)
        for b in range(4):
            ref[row_of(where, b), :] = g[b * 64 : (b + 1) * 64, :]


def add_queries_kernel(own, a, b, c, keep, *sent):
    total = (own[...] + decode(b[...])) + (decode(a[...]) + decode(c[...]))
    keep[...] = total[:64, :]
    for i, ref in enumerate(sent):
        ref[...] = encode(total[(i + 1) * 64 : (i + 2) * 64, :])


def last_queries_kernel(coef, own, a, b, c, out):
    total = (own[...] + decode(b[...])) + (decode(a[...]) + decode(c[...]))
    out[...] = total * coef[3:4, 768:769]


def body(queries, passages, positives):
    x, y, z, c = (lax.axis_index(a) for a in ("x", "y", "z", "core"))
    where = jnp.stack([x, y, z, c]).astype(jnp.int32)
    bf = lambda n: ((n, D), BF)
    f32 = lambda n: ((n, D), F32)

    (packed,) = call(pack_kernel, "pack", [bf(144)], (passages, queries))
    z1r, z1l = shift_z(packed, 1), shift_z(packed, -1)
    pos = positives.reshape(4, 128)
    near = [pos, shift_y(pos, -1), shift_y(pos, 2), shift_y(pos, 1)]
    args = (where, queries, *(shift_plane(queries, 0, k) for k in (1, -1, 2)), *near, z1r, z1l)
    outs = [bf(256), ((8, 256), jnp.int32), bf(144), bf(144)]
    q, pos, z1r, z1l = call(round1_kernel, "round1", outs, args, smem=1, alias={9: 2, 10: 3})
    z2r, z2l = shift_z(z1r, 1), shift_z(z1l, -1)
    q_right, q_left = shift_plane(q, 1, 1), shift_plane(q, 1, -1)
    args = (q_right, q_left, z2r, z2l)
    outs = [bf(128), bf(128), bf(144), bf(144)]
    q_right2, q_left2, z2r, z2l = call(round2_kernel, "round2", outs, args, alias={2: 2, 3: 3})
    z3r, z3l = shift_z(z2r, 1), shift_z(z2l, -1)
    q_right2, q_left2 = shift_plane(q_right2, 1, 1), shift_plane(q_left2, 1, -1)
    args = (where, q, q_right, q_left, q_right2, q_left2, z3r, z3l)
    q_own, far0, far1 = call(round3_kernel, "round3", [bf(1024), bf(80), bf(80)], args, smem=1)
    far0, far1 = shift_z(far0, 1), shift_z(far1, -1)
    q_other = swap_core(q_own)

    raw = pltpu.VMEM((N_NEAR, 256), F32)
    outs = [((N_NEAR, 1024), F32), ((8, 896), F32), bf(N_NEAR)]
    args = (where, q_own, pos, packed, z3r, z3l, z2r, z2l, z1r, z1l)
    near_exps, near_stats, p_near = call(
        near_scores_kernel, "near_scores", outs, args, scratch=[raw] * 2, mib=16, smem=1
    )
    raws = [pltpu.VMEM((1024, 256), F32)] * 2 + [pltpu.VMEM((N_FAR, 256), F32)]
    outs = [((N_FAR, 1024), F32), ((1024, 1024), F32), ((8, 896), F32), ((8, 512), F32), bf(1024)]
    args = (where, q_own, q_other, pos, p_near, near_stats, far0, far1)
    far_exps, other_exps, stats, tops, p_all = call(
        other_scores_kernel, "other_scores", outs, args, scratch=raws, mib=16, smem=1
    )

    for shift in (shift_x, shift_y):
        args = [stats] + [shift(stats, k) for k in (1, -1, 2)]
        (stats,) = call(merge_kernel, "merge", [((8, 896), F32)], args)
    (coef,) = call(finish_kernel, "finish", [((8, 896), F32)], (tops, stats, swap_core(stats)))

    args = (where, near_exps, far_exps, other_exps, q_own, q_other, pos, coef)
    outs = [bf(64), bf(64), f32(128), f32(128), bf(384), bf(384), ((8, 896), F32)]
    right, left, left3, right3, w0_own, w0_other, coef = call(
        first_terms_kernel, "first_terms", outs, args, mib=16, smem=1, alias={7: 6}
    )
    (losses,) = call(losses_kernel, "losses", [((4, 128), F32)], (where, coef), smem=1)
    right, left = shift_z(right, 1), shift_z(left, -1)
    args = (where, near_exps, other_exps, q_own, q_other, pos, coef)
    outs = [f32(128)] * 5 + [bf(640)] * 2
    own, left2, right2, left1, right1, w1_own, w1_other = call(
        other_terms_kernel, "other_terms", outs, args, mib=16, smem=1
    )
    args = (where, p_all, coef, w0_other, w1_other)
    other0, other1 = call(send_queries_kernel, "send_queries", [bf(512)] * 2, args, mib=16, smem=1)
    args = (right, left, left3, right3, other0, other1)
    outs = [bf(128)] * 2 + [bf(512)] * 2
    right, left, other0, other1 = call(add_halves_kernel, "add_halves", outs, args, alias={4: 2, 5: 3})
    right, left = shift_z(right, 1), shift_z(left, -1)
    right, left = call(add_kernel, "add", [bf(128)] * 2, (right, left, left2, right2))
    right, left = shift_z(right, 1), shift_z(left, -1)
    right, left = call(add_kernel, "add", [bf(128)] * 2, (right, left, left1, right1))
    right, left = shift_z(right, 1), shift_z(left, -1)
    (passage_grad,) = call(last_add_kernel, "last_add", [f32(128)], (coef, right, left, own))

    args = (where, p_all, coef, w0_own, w1_own, swap_core(other0), swap_core(other1))
    outs = [f32(256)] + [bf(256)] * 3
    keep, *sent = call(keep_queries_kernel, "keep_queries", outs, args, mib=16, smem=1)
    moved = [shift_plane(v, 1, k + 1) for k, v in enumerate(sent)]
    outs = [f32(64)] + [bf(64)] * 3
    keep, *sent = call(add_queries_kernel, "add_queries", outs, (keep, *moved))
    moved = [shift_plane(v, 0, k + 1) for k, v in enumerate(sent)]
    (query_grad,) = call(last_queries_kernel, "last_queries", [f32(64)], (coef, keep, *moved))
    return losses.reshape(512), query_grad, passage_grad


def solution(mesh):
    mesh = Mesh(mesh.devices.reshape(Y, Z, X, C), ("y", "z", "x", "core"))
    q_spec = P(("y", "z", "x", "core"), None)
    p_spec = P(("x", "core", "y", "z"), None)
    row_spec = P(("y", "z"))
    return jax.shard_map(
        body,
        mesh=mesh,
        in_specs=(q_spec, p_spec, row_spec),
        out_specs=(row_spec, q_spec, p_spec),
        check_vma=False,
    )
```

```python
import functools
import math

import jax
import jax.numpy as jnp
from jax import lax
from jax.experimental import pallas as pl
from jax.experimental.pallas import tpu as pltpu
from jax.sharding import Mesh, PartitionSpec as P

D = 1024
NQ = 16384
SCALE = 3.0 / math.sqrt(D)
TO_EXP2 = SCALE * math.log2(math.e)
X, Y, Z, C = 4, 4, 8, 2
PLANE = ("y", "x", "core")
BF, F32 = jnp.bfloat16, jnp.float32
MIB = 1 << 20
LARGEST = 46000.0
NEAR = ((0, 0, 128), (-3, 0, 128), (3, 0, 128), (-2, 0, 128), (2, 0, 128), (-1, 0, 128), (1, 0, 128))
FAR = ((4, 0, 64), (4, 64, 64))
N_NEAR, N_FAR = 896, 128
TILE = 16
VMEM = pl.BlockSpec(memory_space=pltpu.VMEM)
SMEM = pl.BlockSpec(memory_space=pltpu.SMEM)


def call(kernel, name, outs, args, scratch=(), mib=8, smem=0, alias=None):
    return pl.pallas_call(
        kernel,
        out_shape=[jax.ShapeDtypeStruct(s, t) for s, t in outs],
        in_specs=[SMEM] * smem + [VMEM] * (len(args) - smem),
        out_specs=[VMEM] * len(outs),
        scratch_shapes=list(scratch),
        input_output_aliases=alias or {},
        compiler_params=pltpu.CompilerParams(vmem_limit_bytes=mib * MIB),
        cost_estimate=pl.CostEstimate(flops=1000, bytes_accessed=1024, transcendentals=0),
        name=name,
    )(*args)


def shift_z(v, k):
    return lax.ppermute(v, "z", [(i, (i + k) % Z) for i in range(Z)])


def shift_x(v, k):
    return lax.ppermute(v, "x", [(i, (i + k) % X) for i in range(X)])


def shift_y(v, k):
    return lax.ppermute(v, "y", [(i, (i + k) % Y) for i in range(Y)])


def flip_y(v, k):
    return lax.ppermute(v, "y", [(i, i ^ k) for i in range(Y)])


def swap_core(v):
    return lax.ppermute(v, "core", [(0, 1), (1, 0)])


def shift_plane(v, stage, k):
    pairs = []
    for y in range(Y):
        for x in range(X):
            for c in range(C):
                y2, x2 = (y, (x + k) % X) if c == stage else ((y + k) % Y, x)
                pairs.append(((y * X + x) * C + c, (y2 * X + x2) * C + c))
    return lax.ppermute(v, PLANE, pairs)


def encode(v):
    v2 = v * v
    v4 = v2 * v2
    v8 = v4 * v4
    return jnp.where(v < 0, -v8, v8).astype(BF)


def decode(code):
    y = code.astype(F32)
    size = jnp.abs(y)
    v = jnp.exp2(jnp.log2(jnp.maximum(size, 1e-37)) * 0.125)
    v = jnp.where(size < 1e-37, 0.0, v)
    return jnp.where(y < 0, -v, v)


def axes_of(where, c):
    x, y = where[0], where[1]
    return jnp.where(c == 0, x, y), jnp.where(c == 0, y, x)


def largest(v):
    v = jnp.max(jnp.abs(v).astype(F32), axis=0, keepdims=True)
    return jnp.max(v, axis=1, keepdims=True)


def pack_kernel(passages, queries, out):
    out[:128, :] = passages[...]
    out[128:, :] = jnp.broadcast_to(largest(queries[...]), (TILE, D)).astype(BF)


def sort_positives(where, near, out):
    y, c = where[1], where[3]
    rows = []
    for a in range(4):
        r = near[0]
        for j in range(1, 4):
            r = jnp.where(jnp.bitwise_xor(y, j) == a, near[j], r)
        rows.append(r)
    for k in range(4):
        for b in range(4):
            at = slice(b * 64, b * 64 + 64)
            core0, core1 = rows[k][b : b + 1, :64], rows[b][k : k + 1, 64:]
            out[k : k + 1, at] = jnp.where(c == 0, core0, core1)
            out[4 + k : 5 + k, at] = jnp.where(c == 0, core1, core0)


def round1_kernel(q0, q1, q2, q3, z_right, z_left, out, *_):
    for i, ref in enumerate((q0, q1, q2, q3)):
        out[i * 64 : (i + 1) * 64, :] = ref[...]


def round2_kernel(q_right, q_left, pos0, pos1, z_right, z_left, right, left, pos, *_):
    right[...] = q_right[:128, :]
    left[...] = q_left[128:, :]
    pos[:4, :] = pos0[...]
    pos[4:, :] = pos1[...]


def round3_kernel(
    where, own, right, left, right2, left2, pos0, pos1, z_right, z_left, out, positives, far_right, far_left
):
    first, second = axes_of(where, where[3])
    for i, (ref, part) in enumerate(((own, 0), (right, 0), (left, 0), (right2, 0), (left2, 2))):
        a = lax.rem(second + (0, 3, 1, 2, 2)[i], 4)
        for j in range(ref.shape[0] // 64):
            b = lax.rem(first + (0, 3, 1, 2)[j + part], 4)
            at = pl.ds(pl.multiple_of((a * 4 + b) * 64, 64), 64)
            out[at, :] = ref[j * 64 : (j + 1) * 64, :]
    far_right[:64, :] = z_right[:64, :]
    far_right[64:, :] = z_right[128:, :]
    far_left[...] = z_left[64:, :]
    sort_positives(where, (pos0[:4, :], pos0[4:, :], pos1[:4, :], pos1[4:, :]), positives)


def losses_kernel(where, coef, out):
    y, c = where[1], where[3]
    v = coef[:, 512:768]
    core0, core1 = jnp.where(c == 0, v[:4], v[4:]), jnp.where(c == 0, v[4:], v[:4])
    for x in range(4):
        a, b = core0[0:1, x * 64 : x * 64 + 64], core1[x : x + 1, :64]
        for k in range(1, 4):
            a = jnp.where(y == k, core0[k : k + 1, x * 64 : x * 64 + 64], a)
            b = jnp.where(y == k, core1[x : x + 1, k * 64 : k * 64 + 64], b)
        out[x : x + 1, :64] = a
        out[x : x + 1, 64:] = b


def first_passage(where, offset):
    x, y, z, c = where[0], where[1], where[2], where[3]
    return (((x * C + c) * Y + y) * Z + lax.rem(z + offset + Z, Z)) * 128


def softmax(where, rows, raw, positives, exps, at):
    top = jnp.max(raw[...], axis=0, keepdims=True)
    total = jnp.zeros_like(top)
    pos_score = jnp.zeros_like(top)
    row = 0
    for offset, start, n in rows:
        part = raw[row : row + n, :]
        e = jnp.exp2((part - top) * TO_EXP2)
        exps[row : row + n, at] = e
        total += jnp.sum(e, axis=0, keepdims=True)
        hit = lax.broadcasted_iota(jnp.int32, part.shape, 0) == positives - (first_passage(where, offset) + start)
        pos_score += jnp.sum(jnp.where(hit, part, 0.0), axis=0, keepdims=True)
        row += n
    return top * SCALE, total, pos_score * SCALE


def product(p, q):
    return lax.dot_general(p, q, (((1,), (1,)), ((), ())), preferred_element_type=F32)


def near_scores_kernel(where, q, positives, *refs):
    pieces, (exps, stats, passages, raw0, raw1) = refs[: len(NEAR)], refs[len(NEAR) :]
    largest_q = None
    for i, ref in enumerate(pieces):
        passages[i * 128 : (i + 1) * 128, :] = ref[:128, :]
        v = ref[128:129, :128].astype(F32)
        largest_q = v if largest_q is None else jnp.maximum(largest_q, v)
    raws = (raw0, raw1)
    raw0[...] = product(passages[...], q[0:256, :])
    stats[4:8, :] = jnp.zeros((4, 896), F32)
    stats[0:4, 768:] = jnp.broadcast_to(largest_q, (4, 128))
    for i in range(4):
        if i < 3:
            raws[(i + 1) % 2][...] = product(passages[...], q[(i + 1) * 256 : (i + 2) * 256, :])
        at = slice(i * 256, (i + 1) * 256)
        top, total, pos_score = softmax(where, NEAR, raws[i % 2], positives[i : i + 1, :], exps, at)
        stats[i : i + 1, 0:256] = top
        stats[i : i + 1, 256:512] = total
        stats[i : i + 1, 512:768] = pos_score


def other_scores_kernel(
    where, q_own, q_other, positives, near, near_stats, far0, far1,
    far_exps, exps, stats, tops, passages, raw0, raw1, raw2,
):
    passages[:N_NEAR, :] = near[...]
    passages[N_NEAR : N_NEAR + 64, :] = far0[:64, :]
    passages[N_NEAR + 64 :, :] = far1[:64, :]
    largest_q = jnp.maximum(far0[64:65, :128].astype(F32), far1[64:65, :128].astype(F32))
    largest_q = jnp.maximum(largest_q, near_stats[0:1, 768:])
    stats[0:4, 768:] = jnp.broadcast_to(largest_q, (4, 128))
    stats[4:8, 768:] = jnp.broadcast_to(largest(passages[...]), (4, 128))
    raws = (raw0, raw1)
    raw0[...] = product(passages[...], q_other[0:256, :])
    for i in range(4):
        if i < 3:
            raws[(i + 1) % 2][...] = product(passages[...], q_other[(i + 1) * 256 : (i + 2) * 256, :])
        raw2[...] = product(passages[N_NEAR:, :], q_own[i * 256 : (i + 1) * 256, :])
        at = slice(i * 256, (i + 1) * 256)
        own, other = slice(i, i + 1), slice(4 + i, 5 + i)
        top, total, pos_score = softmax(where, NEAR + FAR, raws[i % 2], positives[other, :], exps, at)
        tops[other, 0:256] = top
        tops[other, 256:512] = top
        stats[other, 0:256] = top
        stats[other, 256:512] = total
        stats[other, 512:768] = pos_score
        top, total, pos_score = softmax(where, FAR, raw2, positives[own, :], far_exps, at)
        near_top = near_stats[own, 0:256]
        both = jnp.maximum(top, near_top)
        tops[own, 0:256] = near_top
        tops[own, 256:512] = top
        stats[own, 0:256] = both
        stats[own, 256:512] = total * jnp.exp(top - both) + near_stats[own, 256:512] * jnp.exp(near_top - both)
        stats[own, 512:768] = pos_score + near_stats[own, 512:768]


def merge_stats(parts):
    top = functools.reduce(jnp.maximum, [p[:, 0:256] for p in parts])
    totals = [p[:, 256:512] * jnp.exp(p[:, 0:256] - top) for p in parts]
    pos_scores = [p[:, 512:768] for p in parts]
    if len(parts) == 4:
        join = lambda v: (v[0] + v[3]) + (v[1] + v[2])
    else:
        join = lambda v: v[0] + v[1]
    rest = functools.reduce(jnp.maximum, [p[:, 768:] for p in parts])
    return top, join(totals), join(pos_scores), rest


def merge_kernel(*refs):
    out = refs[-1]
    top, total, pos_score, rest = merge_stats([r[...] for r in refs[:-1]])
    out[:, 0:256] = top
    out[:, 256:512] = total
    out[:, 512:768] = pos_score
    out[:, 768:] = rest


def finish_kernel(tops, one, two, out):
    two = jnp.concatenate(
        [jnp.concatenate([two[4:8, :768], two[0:4, :768]], axis=0), two[:, 768:]], axis=1
    )
    top, total, pos_score, rest = merge_stats([one[...], two])
    lse = top + jnp.log(total)
    out[:, 0:256] = jnp.exp(tops[:, 0:256] - lse)
    out[:, 256:512] = jnp.exp(tops[:, 256:512] - lse)
    out[:, 512:768] = lse - pos_score
    bound_p = (NQ * SCALE) * jnp.maximum(rest[0:1, :], 1e-30)
    bound_q = (2.0 * SCALE) * jnp.maximum(rest[4:5, :], 1e-30)
    out[0:1, 768:] = LARGEST / bound_p
    out[1:2, 768:] = bound_p / LARGEST
    out[2:3, 768:] = LARGEST / bound_q
    out[3:4, 768:] = bound_q / LARGEST
    out[4:8, 768:] = jnp.zeros((4, 128), F32)


def weigh(where, rows, exps, base, positives, coef, first, k, weights):
    for i in range(4):
        at = slice(i * 256, (i + 1) * 256)
        factor = coef[first + i : first + i + 1, k : k + 256]
        pos = positives[first + i : first + i + 1, :]
        row = 0
        for offset, start, n, r in rows:
            hit = lax.broadcasted_iota(jnp.int32, (n, 256), 0) == pos - (first_passage(where, offset) + start)
            e = exps[r - base : r - base + n, at]
            weights[row : row + n, at] = ((e * factor - hit.astype(F32)) * SCALE).astype(BF)
            row += n


def scaled_terms(w_own, w_other, q_own, q_other, scale, at):
    g = jnp.dot(w_own[...], q_own[:, at], preferred_element_type=F32)
    return (g + jnp.dot(w_other[...], q_other[:, at], preferred_element_type=F32)) * scale


BLOCKS = [(o, s, n, 128 * i) for i, (o, s, n) in enumerate(NEAR)]
FAR_BLOCKS = [(o, s, n, N_NEAR + s) for o, s, n in FAR]


def first_terms_kernel(
    where, near_exps, far_exps, other_exps, q_own, q_other, positives, coef,
    right, left, term_left, term_right, w_own, w_other, *_,
):
    weigh(where, FAR_BLOCKS, far_exps, N_NEAR, positives, coef, 0, 256, w_own.at[:128])
    weigh(where, BLOCKS[1:3], near_exps, 0, positives, coef, 0, 0, w_own.at[128:])
    weigh(where, FAR_BLOCKS + BLOCKS[1:3], other_exps, 0, positives, coef, 4, 0, w_other)
    for j in range(4):
        at = slice(j * 256, (j + 1) * 256)
        g = scaled_terms(w_own, w_other, q_own, q_other, coef[0:1, 768:769], at)
        right[:, at] = encode(g[:64])
        left[:, at] = encode(g[64:128])
        term_left[:, at] = g[128:256]
        term_right[:, at] = g[256:]


def other_terms_kernel(
    where, near_exps, other_exps, q_own, q_other, positives, coef, *outs
):
    grads, (w_own, w_other) = outs[:5], outs[5:]
    rows = [BLOCKS[0], *BLOCKS[3:]]
    weigh(where, rows, near_exps, 0, positives, coef, 0, 0, w_own)
    weigh(where, rows, other_exps, 0, positives, coef, 4, 0, w_other)
    for j in range(4):
        at = slice(j * 256, (j + 1) * 256)
        g = scaled_terms(w_own, w_other, q_own, q_other, coef[0:1, 768:769], at)
        for i, ref in enumerate(grads):
            ref[:, at] = g[i * 128 : (i + 1) * 128]


def add_halves_kernel(from_left, from_right, term_left, term_right, other0, other1, right, left, *_):
    right[:64, :] = encode(term_right[:64, :] + decode(from_left[...]))
    right[64:, :] = encode(term_right[64:, :])
    left[:64, :] = encode(term_left[:64, :])
    left[64:, :] = encode(term_left[64:, :] + decode(from_right[...]))


def add_kernel(received, term, out):
    out[...] = encode(term[...] + decode(received[...]))


def last_add_kernel(coef, from_left, from_right, term, out):
    out[...] = (term[...] + (decode(from_left[...]) + decode(from_right[...]))) * coef[1:2, 768:769]


GROUPS = ((1, 0, 128), (0, 128, 384), (1, 128, 640), (0, 0, 128))


def query_terms(own, where, passages, coef, weights, i):
    _, second = axes_of(where, where[3] if own else 1 - where[3])
    at = pl.ds(pl.multiple_of(lax.rem(second + i, 4) * 256, 256), 256)
    w = jnp.concatenate([weights[k][u:v, at] for k, u, v in GROUPS], axis=0)
    g = lax.dot_general(w, passages[...], (((0,), (0,)), ((), ())), preferred_element_type=F32)
    return g * coef[2:3, 768:769]


def row_of(where, b):
    first, _ = axes_of(where, where[3])
    return pl.ds(pl.multiple_of(lax.rem(b - first + 4, 4) * 64, 64), 64)


def send_queries_kernel(where, passages, coef, w0, w1, out0, out1):
    for i in range(4):
        g = encode(query_terms(False, where, passages, coef, (w0, w1), i))
        (out0, out1)[i // 2][i % 2 * 256 : (i % 2 + 1) * 256, :] = g


def keep_queries_kernel(where, passages, coef, w0, w1, other0, other1, keep, *sent):
    for i, ref in enumerate((keep, *sent)):
        g = query_terms(True, where, passages, coef, (w0, w1), i)
        g += decode((other0, other1)[i // 2][i % 2 * 256 : (i % 2 + 1) * 256, :])
        g = g if i == 0 else encode(g)
        for b in range(4):
            ref[row_of(where, b), :] = g[b * 64 : (b + 1) * 64, :]


def add_queries_kernel(own, a, b, c, keep, *sent):
    total = (own[...] + decode(b[...])) + (decode(a[...]) + decode(c[...]))
    keep[...] = total[:64, :]
    for i, ref in enumerate(sent):
        ref[...] = encode(total[(i + 1) * 64 : (i + 2) * 64, :])


def last_queries_kernel(coef, own, a, b, c, out):
    total = (own[...] + decode(b[...])) + (decode(a[...]) + decode(c[...]))
    out[...] = total * coef[3:4, 768:769]


def body(queries, passages, positives):
    x, y, z, c = (lax.axis_index(a) for a in ("x", "y", "z", "core"))
    where = jnp.stack([x, y, z, c]).astype(jnp.int32)
    bf = lambda n: ((n, D), BF)
    f32 = lambda n: ((n, D), F32)

    (packed,) = call(pack_kernel, "pack", [bf(144)], (passages, queries))
    z1r, z1l = shift_z(packed, 1), shift_z(packed, -1)
    pos = positives.reshape(4, 128)
    args = (queries, *(shift_plane(queries, 0, k) for k in (1, -1, 2)), z1r, z1l)
    q, z1r, z1l = call(round1_kernel, "round1", [bf(256), bf(144), bf(144)], args, alias={4: 1, 5: 2})
    z2r, z2l = shift_z(z1r, 1), shift_z(z1l, -1)
    q_right, q_left = shift_plane(q, 1, 1), shift_plane(q, 1, -1)
    args = (q_right, q_left, pos, flip_y(pos, 1), z2r, z2l)
    outs = [bf(128), bf(128), ((8, 128), jnp.int32), bf(144), bf(144)]
    q_right2, q_left2, pos, z2r, z2l = call(round2_kernel, "round2", outs, args, alias={4: 3, 5: 4})
    z3r, z3l = shift_z(z2r, 1), shift_z(z2l, -1)
    q_right2, q_left2 = shift_plane(q_right2, 1, 1), shift_plane(q_left2, 1, -1)
    args = (where, q, q_right, q_left, q_right2, q_left2, pos, flip_y(pos, 2), z3r, z3l)
    outs = [bf(1024), ((8, 256), jnp.int32), bf(80), bf(80)]
    q_own, pos, far0, far1 = call(round3_kernel, "round3", outs, args, smem=1)
    far0, far1 = shift_z(far0, 1), shift_z(far1, -1)
    q_other = swap_core(q_own)

    raw = pltpu.VMEM((N_NEAR, 256), F32)
    outs = [((N_NEAR, 1024), F32), ((8, 896), F32), bf(N_NEAR)]
    args = (where, q_own, pos, packed, z3r, z3l, z2r, z2l, z1r, z1l)
    near_exps, near_stats, p_near = call(
        near_scores_kernel, "near_scores", outs, args, scratch=[raw] * 2, mib=16, smem=1
    )
    raws = [pltpu.VMEM((1024, 256), F32)] * 2 + [pltpu.VMEM((N_FAR, 256), F32)]
    outs = [((N_FAR, 1024), F32), ((1024, 1024), F32), ((8, 896), F32), ((8, 512), F32), bf(1024)]
    args = (where, q_own, q_other, pos, p_near, near_stats, far0, far1)
    far_exps, other_exps, stats, tops, p_all = call(
        other_scores_kernel, "other_scores", outs, args, scratch=raws, mib=16, smem=1
    )

    for shift in (shift_x, shift_y):
        args = [stats] + [shift(stats, k) for k in (1, -1, 2)]
        (stats,) = call(merge_kernel, "merge", [((8, 896), F32)], args)
    (coef,) = call(finish_kernel, "finish", [((8, 896), F32)], (tops, stats, swap_core(stats)))

    args = (where, near_exps, far_exps, other_exps, q_own, q_other, pos, coef)
    outs = [bf(64), bf(64), f32(128), f32(128), bf(384), bf(384), ((8, 896), F32)]
    right, left, left3, right3, w0_own, w0_other, coef = call(
        first_terms_kernel, "first_terms", outs, args, mib=16, smem=1, alias={7: 6}
    )
    (losses,) = call(losses_kernel, "losses", [((4, 128), F32)], (where, coef), smem=1)
    right, left = shift_z(right, 1), shift_z(left, -1)
    args = (where, near_exps, other_exps, q_own, q_other, pos, coef)
    outs = [f32(128)] * 5 + [bf(640)] * 2
    own, left2, right2, left1, right1, w1_own, w1_other = call(
        other_terms_kernel, "other_terms", outs, args, mib=16, smem=1
    )
    args = (where, p_all, coef, w0_other, w1_other)
    other0, other1 = call(send_queries_kernel, "send_queries", [bf(512)] * 2, args, mib=16, smem=1)
    args = (right, left, left3, right3, other0, other1)
    outs = [bf(128)] * 2 + [bf(512)] * 2
    right, left, other0, other1 = call(add_halves_kernel, "add_halves", outs, args, alias={4: 2, 5: 3})
    right, left = shift_z(right, 1), shift_z(left, -1)
    for to_right, to_left in ((right2, left2), (right1, left1)):
        (right,) = call(add_kernel, "add_right", [bf(128)], (right, to_right))
        right = shift_z(right, 1)
        (left,) = call(add_kernel, "add_left", [bf(128)], (left, to_left))
        left = shift_z(left, -1)
    (passage_grad,) = call(last_add_kernel, "last_add", [f32(128)], (coef, right, left, own))

    args = (where, p_all, coef, w0_own, w1_own, swap_core(other0), swap_core(other1))
    outs = [f32(256)] + [bf(256)] * 3
    keep, *sent = call(keep_queries_kernel, "keep_queries", outs, args, mib=16, smem=1)
    moved = [shift_plane(v, 1, k + 1) for k, v in enumerate(sent)]
    outs = [f32(64)] + [bf(64)] * 3
    keep, *sent = call(add_queries_kernel, "add_queries", outs, (keep, *moved))
    moved = [shift_plane(v, 0, k + 1) for k, v in enumerate(sent)]
    (query_grad,) = call(last_queries_kernel, "last_queries", [f32(64)], (coef, keep, *moved))
    return losses.reshape(512), query_grad, passage_grad


def solution(mesh):
    mesh = Mesh(mesh.devices.reshape(Y, Z, X, C), ("y", "z", "x", "core"))
    q_spec = P(("y", "z", "x", "core"), None)
    p_spec = P(("x", "core", "y", "z"), None)
    row_spec = P(("y", "z"))
    return jax.shard_map(
        body,
        mesh=mesh,
        in_specs=(q_spec, p_spec, row_spec),
        out_specs=(row_spec, q_spec, p_spec),
        check_vma=False,
    )
```

```python
import functools
import math

import jax
import jax.numpy as jnp
from jax import lax
from jax.experimental import pallas as pl
from jax.experimental.pallas import tpu as pltpu
from jax.sharding import Mesh, PartitionSpec as P

D = 1024
NQ = 16384
SCALE = 3.0 / math.sqrt(D)
TO_EXP2 = SCALE * math.log2(math.e)
X, Y, Z, C = 4, 4, 8, 2
PLANE = ("y", "x", "core")
BF, F32 = jnp.bfloat16, jnp.float32
MIB = 1 << 20
LARGEST = 46000.0
NEAR = [(0, 0, 2), (0, 0, 3), (1, 3, 0), (1, 3, 1)]
NEAR += [(sign, k, core) for k in (2, 1) for sign in (1, -1) for core in (0, 1)]
FAR = [(1, 4, 2), (1, 4, 3), (-1, 3, 0), (-1, 3, 1)]
N_NEAR, N_FAR = 1536, 512
TILE = 16
VMEM = pl.BlockSpec(memory_space=pltpu.VMEM)
SMEM = pl.BlockSpec(memory_space=pltpu.SMEM)


def call(kernel, name, outs, args, scratch=(), mib=8, smem=0, alias=None, space=VMEM):
    return pl.pallas_call(
        kernel,
        out_shape=[jax.ShapeDtypeStruct(s, t) for s, t in outs],
        in_specs=[SMEM] * smem + [space] * (len(args) - smem),
        out_specs=[VMEM] * len(outs),
        scratch_shapes=list(scratch),
        input_output_aliases=alias or {},
        compiler_params=pltpu.CompilerParams(vmem_limit_bytes=mib * MIB),
        cost_estimate=pl.CostEstimate(flops=1000, bytes_accessed=1024, transcendentals=0),
        name=name,
    )(*args)


def ring(v, cross=False):
    pairs = []
    for z in range(Z):
        for c in range(C):
            to = ((z + 1) % Z) * C if c == int(cross) else ((z - 1) % Z) * C + 1
            pairs.append((z * C + c, to))
    return lax.ppermute(v, ("z", "core"), pairs)


def ring_cross_out(v):
    pairs = []
    for z in range(Z):
        for c in range(C):
            pairs.append((z * C + c, ((z + 1) % Z) * C + 1 if c == 0 else ((z - 1) % Z) * C))
    return lax.ppermute(v, ("z", "core"), pairs)


def shift_x(v, k):
    return lax.ppermute(v, "x", [(i, (i + k) % X) for i in range(X)])


def shift_y(v, k):
    return lax.ppermute(v, "y", [(i, (i + k) % Y) for i in range(Y)])


def swap_core(v):
    return lax.ppermute(v, "core", [(0, 1), (1, 0)])


def shift_plane(v, stage, k):
    pairs = []
    for y in range(Y):
        for x in range(X):
            for c in range(C):
                y2, x2 = (y, (x + k) % X) if c == stage else ((y + k) % Y, x)
                pairs.append(((y * X + x) * C + c, (y2 * X + x2) * C + c))
    return lax.ppermute(v, PLANE, pairs)


def encode(v):
    v2 = v * v
    v4 = v2 * v2
    v8 = v4 * v4
    return jnp.where(v < 0, -v8, v8).astype(BF)


def decode(code):
    y = code.astype(F32)
    size = jnp.abs(y)
    v = jnp.exp2(jnp.log2(jnp.maximum(size, 1e-37)) * 0.125)
    v = jnp.where(size < 1e-37, 0.0, v)
    return jnp.where(y < 0, -v, v)


def axes_of(where, c):
    x, y = where[0], where[1]
    return jnp.where(c == 0, x, y), jnp.where(c == 0, y, x)


def largest(v):
    v = jnp.max(jnp.abs(v).astype(F32), axis=0, keepdims=True)
    return jnp.max(v, axis=1, keepdims=True)


def rows_like(tile):
    return lax.broadcasted_iota(jnp.int32, tile.shape, 0)


def pack_kernel(where, passages, queries, positives, p_out, q_out, pos_ref, sems):
    copies = [
        pltpu.make_async_copy(src, dst, sems.at[i])
        for i, (src, dst) in enumerate(
            ((queries, q_out.at[pl.ds(0, 64)]), (positives, pos_ref), (passages, p_out.at[pl.ds(0, 128)]))
        )
    ]
    for copy in copies:
        copy.start()
    q_out[64:, :] = jnp.zeros((TILE, D), BF)
    copies[0].wait()
    p_out[128:, :] = jnp.broadcast_to(largest(q_out[:64, :]), (TILE, D)).astype(BF)
    copies[1].wait()
    pos = pos_ref[pl.ds(where[0], 1), :]
    pos = jnp.where(where[3] == 0, pos, jnp.concatenate([pos[:, 64:], pos[:, :64]], axis=1))
    tile = jnp.zeros((TILE, 128), F32)
    for i, part in enumerate((lax.shift_right_logical(pos, 8), jnp.bitwise_and(pos, 255))):
        tile = jnp.where(rows_like(tile) == i, part.astype(F32), tile)
    q_out[64:, :128] = tile.astype(BF)
    copies[2].wait()


def at_core(c):
    return pl.ds(pl.multiple_of(c * 128, 128), 128)


def round1_kernel(where, q0, q1, q2, q3, same, cross, out, chip):
    tile = jnp.zeros((TILE, 128), F32)
    for i, ref in enumerate((q0, q1, q2, q3)):
        out[i * 64 : (i + 1) * 64, :] = ref[:64, :]
        part = ref[64:, :128].astype(F32)
        tile = jnp.where(rows_like(tile) == i, part[0:1, :], tile)
        tile = jnp.where(rows_like(tile) == 4 + i, part[1:2, :], tile)
    out[256:, :] = jnp.zeros((TILE, D), BF)
    out[256:, :128] = tile.astype(BF)
    c = where[3]
    chip[at_core(c), :] = same[:128, :]
    chip[at_core(1 - c), :] = cross[:128, :]
    chip[256:, :] = jnp.maximum(same[128:, :], cross[128:, :])


def round2_kernel(q_right, q_left, chip, right, left, *_):
    right[:128, :] = q_right[:128, :]
    right[128:, :] = q_right[256:, :]
    left[...] = q_left[128:, :]


def round3_kernel(where, own, right, left, right2, left2, chip, *refs):
    out, positives, _, scratch = refs[-4:]
    first, second = axes_of(where, where[3])
    for i, (ref, part, n) in enumerate(((own, 0, 4), (right, 0, 4), (left, 0, 4), (right2, 0, 2), (left2, 2, 2))):
        a = lax.rem(second + (0, 3, 1, 2, 2)[i], 4)
        tile = ref[n * 64 :, :128].astype(F32)
        for j in range(part, part + n):
            b = lax.rem(first + (0, 3, 1, 2)[j], 4)
            at = pl.ds(pl.multiple_of((a * 4 + b) * 64, 64), 64)
            out[at, :] = ref[(j - part) * 64 : (j - part + 1) * 64, :]
            pos = tile[j : j + 1, :] * 256.0 + tile[4 + j : 5 + j, :]
            scratch[pl.ds(a * 4 + b, 1), :] = pos.astype(jnp.int32)
    positives[...] = jnp.zeros((8, 256), jnp.int32)
    for a in range(4):
        for b in range(4):
            positives[a : a + 1, b * 64 : b * 64 + 64] = scratch[a * 4 + b : a * 4 + b + 1, :64]


def losses_kernel(where, coef, out):
    y, c = where[1], where[3]
    for x in range(4):
        a, b = coef[0:1, 512 + x * 64 : 576 + x * 64], coef[x : x + 1, 512:576]
        for k in range(1, 4):
            a = jnp.where(y == k, coef[k : k + 1, 512 + x * 64 : 576 + x * 64], a)
            b = jnp.where(y == k, coef[x : x + 1, 512 + k * 64 : 576 + k * 64], b)
        out[x : x + 1, :] = jnp.where(c == 0, a, b)


def first_passage(where, block):
    x, y, z, c = where[0], where[1], where[2], where[3]
    sign, k, core = block
    core = (0, 1, c, 1 - c)[core]
    return (((x * C + core) * Y + y) * Z + lax.rem(z + sign * k * (2 * c - 1) + Z, Z)) * 128


def softmax(where, blocks, raw, positives, exps, at):
    top = jnp.max(raw[...], axis=0, keepdims=True)
    total = jnp.zeros_like(top)
    pos_score = jnp.zeros_like(top)
    row = 0
    for block in blocks:
        part = raw[row : row + 128, :]
        e = jnp.exp2((part - top) * TO_EXP2)
        exps[row : row + 128, at] = e
        total += jnp.sum(e, axis=0, keepdims=True)
        hit = lax.broadcasted_iota(jnp.int32, part.shape, 0) == positives - first_passage(where, block)
        pos_score += jnp.sum(jnp.where(hit, part, 0.0), axis=0, keepdims=True)
        row += 128
    return top * SCALE, total, pos_score * SCALE


def product(p, q):
    return lax.dot_general(p, q, (((1,), (1,)), ((), ())), preferred_element_type=F32)


def near_scores_kernel(where, q, positives, own, other, *refs):
    pieces, (exps, stats, passages, raw0, raw1) = refs[:5], refs[5:]
    passages[0:128, :] = own[:128, :]
    passages[128:256, :] = other[:128, :]
    tile = jnp.maximum(own[128:, :128], other[128:, :128])
    for i, ref in enumerate(pieces):
        passages[(i + 1) * 256 : (i + 2) * 256, :] = ref[:256, :]
        tile = jnp.maximum(tile, ref[256:, :128])
    raws = (raw0, raw1)
    raw0[...] = product(passages[...], q[0:256, :])
    stats[...] = jnp.ones((8, 896), F32)
    stats[0:4, 768:] = jnp.broadcast_to(tile[0:1, :].astype(F32), (4, 128))
    for i in range(4):
        if i < 3:
            raws[(i + 1) % 2][...] = product(passages[...], q[(i + 1) * 256 : (i + 2) * 256, :])
        at = slice(i * 256, (i + 1) * 256)
        top, total, pos_score = softmax(where, NEAR, raws[i % 2], positives[i : i + 1, :], exps, at)
        stats[i : i + 1, 0:256] = top
        stats[i : i + 1, 256:512] = total
        stats[i : i + 1, 512:768] = pos_score
    stats[4:8, 768:] = jnp.broadcast_to(largest(passages[...]), (4, 128))


def far_scores_kernel(where, q, positives, near_stats, far, third, exps, stats, tops, passages, raw):
    passages[:128, :] = far[at_core(where[3]), :]
    passages[128:256, :] = far[at_core(1 - where[3]), :]
    passages[256:, :] = third[:256, :]
    tile = jnp.maximum(far[256:, :128], third[256:, :128])[0:1, :].astype(F32)
    raw[...] = product(passages[...], q[...])
    stats[...] = near_stats[...]
    tops[...] = jnp.zeros((8, 512), F32)
    for i in range(4):
        at = slice(i * 256, (i + 1) * 256)
        row = slice(i, i + 1)
        top, total, pos_score = softmax(where, FAR, raw.at[:, at], positives[row, :], exps, at)
        near_top = near_stats[row, 0:256]
        both = jnp.maximum(top, near_top)
        tops[row, 0:256] = near_top
        tops[row, 256:512] = top
        stats[row, 0:256] = both
        stats[row, 256:512] = total * jnp.exp(top - both) + near_stats[row, 256:512] * jnp.exp(near_top - both)
        stats[row, 512:768] = pos_score + near_stats[row, 512:768]
    stats[0:4, 768:] = jnp.maximum(near_stats[0:4, 768:], jnp.broadcast_to(tile, (4, 128)))
    stats[4:8, 768:] = jnp.maximum(near_stats[4:8, 768:], jnp.broadcast_to(largest(passages[...]), (4, 128)))


def merge_stats(parts):
    top = functools.reduce(jnp.maximum, [p[:, 0:256] for p in parts])
    totals = [p[:, 256:512] * jnp.exp(p[:, 0:256] - top) for p in parts]
    pos_scores = [p[:, 512:768] for p in parts]
    join = lambda v: (v[0] + v[3]) + (v[1] + v[2])
    rest = functools.reduce(jnp.maximum, [p[:, 768:] for p in parts])
    return top, join(totals), join(pos_scores), rest


def merge_kernel(*refs):
    out = refs[-1]
    top, total, pos_score, rest = merge_stats([r[...] for r in refs[:-1]])
    out[:, 0:256] = top
    out[:, 256:512] = total
    out[:, 512:768] = pos_score
    out[:, 768:] = rest


def finish_kernel(tops, *refs):
    out = refs[-1]
    top, total, pos_score, rest = merge_stats([r[...] for r in refs[:-1]])
    lse = top + jnp.log(total)
    out[:, 0:256] = jnp.exp(tops[:, 0:256] - lse)
    out[:, 256:512] = jnp.exp(tops[:, 256:512] - lse)
    out[:, 512:768] = lse - pos_score
    bound_p = (NQ * SCALE) * jnp.maximum(rest[0:1, :], 1e-30)
    bound_q = (2.0 * SCALE) * jnp.maximum(rest[4:5, :], 1e-30)
    out[0:1, 768:] = LARGEST / bound_p
    out[1:2, 768:] = bound_p / LARGEST
    out[2:3, 768:] = LARGEST / bound_q
    out[3:4, 768:] = bound_q / LARGEST
    out[4:8, 768:] = jnp.zeros((4, 128), F32)


def weigh(where, blocks, exps, row, positives, coef, k, weights):
    for i in range(4):
        at = slice(i * 256, (i + 1) * 256)
        factor = coef[i : i + 1, k : k + 256]
        pos = positives[i : i + 1, :]
        for j, block in enumerate(blocks):
            hit = lax.broadcasted_iota(jnp.int32, (128, 256), 0) == pos - first_passage(where, block)
            e = exps[row + j * 128 : row + (j + 1) * 128, at]
            weights[j * 128 : (j + 1) * 128, at] = ((e * factor - hit.astype(F32)) * SCALE).astype(BF)


def terms(weights, q, coef):
    for j in range(4):
        at = slice(j * 256, (j + 1) * 256)
        yield at, jnp.dot(weights[...], q[:, at], preferred_element_type=F32) * coef[0:1, 768:769]


def far_terms_kernel(where, exps, q, positives, coef, keep, send, weights, *_):
    weigh(where, FAR[:2], exps, 0, positives, coef, 256, weights)
    for at, g in terms(weights, q, coef):
        keep[:, at] = g[:128]
        send[:, at] = encode(g[128:])


def third_terms_kernel(where, exps, far_exps, q, positives, coef, keep, send, weights, *_):
    weigh(where, NEAR[2:4], exps, 256, positives, coef, 0, weights.at[:256])
    weigh(where, FAR[2:], far_exps, 256, positives, coef, 256, weights.at[256:])
    for at, g in terms(weights, q, coef):
        send[:, at] = encode(g[:256])
        keep[:, at] = g[256:]


def other_terms_kernel(where, exps, q, positives, coef, keep0, keep1, keep2, send, weights):
    weigh(where, NEAR[:2], exps, 0, positives, coef, 0, weights.at[:256])
    weigh(where, NEAR[4:], exps, 512, positives, coef, 0, weights.at[256:])
    for at, g in terms(weights, q, coef):
        keep0[:, at] = g[:128]
        send[512:, at] = encode(g[128:256])
        send[:256, at] = encode(g[256:512])
        keep2[:, at] = g[512:768]
        send[256:512, at] = encode(g[768:1024])
        keep1[:, at] = g[1024:]


def add_far_kernel(term, other, send3, out, *_):
    out[...] = encode(term[...] + decode(other[...]))


def add_third_kernel(where, received, term, other, send, coef, out, *_):
    c = where[3]
    both = term[...] + decode(other[...])
    both = jnp.concatenate(
        [both[:128] + jnp.where(c == 0, decode(received[...]), 0.0), both[128:] + jnp.where(c == 1, decode(received[...]), 0.0)],
        axis=0,
    )
    out[...] = encode(both)


def add_second_kernel(received, term, other, *refs):
    refs[-1][...] = encode(term[...] + (decode(received[...]) + decode(other[:256, :])))


def add_first_kernel(where, received, term, other, same, cross):
    for ref, c in ((same, where[3]), (cross, 1 - where[3])):
        at = at_core(c)
        there = pl.ds(pl.multiple_of(256 + c * 128, 128), 128)
        ref[...] = encode(term[at, :] + (decode(received[at, :]) + decode(other[there, :])))


def last_add_kernel(same, cross, term, other, coef, out):
    total = (term[...] + decode(other[512:, :])) + (decode(same[...]) + decode(cross[...]))
    out[...] = total * coef[1:2, 768:769]


def query_terms_kernel(groups, where, near, far, coef, w_far, w_third, w_other, *outs):
    first, second = axes_of(where, where[3])
    for i, out in zip(groups, outs):
        at = pl.ds(pl.multiple_of(lax.rem(second + i, 4) * 256, 256), 256)
        w = jnp.concatenate([w_other[:256, at], w_third[:256, at], w_other[256:, at]], axis=0)
        g = lax.dot_general(w, near[...], (((0,), (0,)), ((), ())), preferred_element_type=F32)
        w = jnp.concatenate([w_far[:, at], w_third[256:, at]], axis=0)
        g += lax.dot_general(w, far[...], (((0,), (0,)), ((), ())), preferred_element_type=F32)
        g = g * coef[2:3, 768:769]
        g = encode(g) if i else g
        for b in range(4):
            to = pl.ds(pl.multiple_of(lax.rem(b - first + 4, 4) * 64, 64), 64)
            out[to, :] = g[b * 64 : (b + 1) * 64, :]


def add_queries_kernel(own, a, b, c, keep, *sent):
    total = (own[...] + decode(b[...])) + (decode(a[...]) + decode(c[...]))
    keep[...] = total[:64, :]
    for i, ref in enumerate(sent):
        ref[...] = encode(total[(i + 1) * 64 : (i + 2) * 64, :])


def last_queries_kernel(coef, own, a, b, c, out):
    total = (own[...] + decode(b[...])) + (decode(a[...]) + decode(c[...]))
    out[...] = total * coef[3:4, 768:769]


def body(queries, passages, positives):
    x, y, z, c = (lax.axis_index(a) for a in ("x", "y", "z", "core"))
    where = jnp.stack([x, y, z, c]).astype(jnp.int32)
    bf = lambda n: ((n, D), BF)
    f32 = lambda n: ((n, D), F32)
    stats_like = ((8, 896), F32)

    args = (where, passages, queries, positives.reshape(4, 128))
    scratch = [pltpu.VMEM((4, 128), jnp.int32), pltpu.SemaphoreType.DMA((3,))]
    packed, q = call(
        pack_kernel, "pack", [bf(144), bf(80)], args, scratch=scratch, smem=1, space=pl.BlockSpec(memory_space=pltpu.HBM)
    )
    same, cross = ring(packed), ring(packed, cross=True)
    args = (where, q, *(shift_plane(q, 0, k) for k in (1, -1, 2)), same, cross)
    q, m1 = call(round1_kernel, "round1", [bf(272), bf(272)], args, smem=1)
    m2 = ring(m1)
    q_right, q_left = shift_plane(q, 1, 1), shift_plane(q, 1, -1)
    outs = [bf(144), bf(144), bf(272)]
    q_right2, q_left2, m2 = call(round2_kernel, "round2", outs, (q_right, q_left, m2), alias={2: 2})
    m3 = ring(m2)
    q_right2, q_left2 = shift_plane(q_right2, 1, 1), shift_plane(q_left2, 1, -1)
    other, t1, t2 = swap_core(packed), swap_core(m1), swap_core(m2)
    args = (where, q, q_right, q_left, q_right2, q_left2, m3, other, t1, t2)
    outs = [bf(1024), ((8, 256), jnp.int32), bf(272)]
    scratch = [pltpu.VMEM((16, 128), jnp.int32)]
    q, pos, m3 = call(round3_kernel, "round3", outs, args, scratch=scratch, smem=1, alias={6: 2})
    far, t3 = ring(m3), swap_core(m3)

    raw = pltpu.VMEM((N_NEAR, 256), F32)
    outs = [((N_NEAR, 1024), F32), stats_like, bf(N_NEAR)]
    args = (where, q, pos, packed, other, m3, m2, t2, m1, t1)
    exps, near_stats, p_near = call(
        near_scores_kernel, "near_scores", outs, args, scratch=[raw] * 2, mib=16, smem=1
    )
    outs = [((N_FAR, 1024), F32), stats_like, ((8, 512), F32), bf(N_FAR)]
    args = (where, q, pos, near_stats, far, t3)
    far_exps, stats, tops, p_far = call(
        far_scores_kernel, "far_scores", outs, args, scratch=[pltpu.VMEM((N_FAR, 1024), F32)], smem=1
    )

    parts = [stats] + [shift_x(stats, k) for k in (1, -1, 2)]
    (stats,) = call(merge_kernel, "merge", [stats_like], parts)
    parts = [stats] + [shift_y(stats, k) for k in (1, -1, 2)]
    (coef,) = call(finish_kernel, "finish", [stats_like], (tops, *parts))

    args = (where, far_exps, q, pos, coef)
    outs = [f32(128), bf(128), bf(256), stats_like]
    far_keep, far_send, w_far, coef = call(
        far_terms_kernel, "far_terms", outs, args, mib=12, smem=1, alias={4: 3}
    )
    args = (where, exps, far_exps, q, pos, coef)
    outs = [f32(256), bf(256), bf(512), stats_like]
    keep3, send3, w_third, coef = call(
        third_terms_kernel, "third_terms", outs, args, mib=12, smem=1, alias={5: 3}
    )
    args = (far_keep, swap_core(far_send), send3)
    sent, send3 = call(add_far_kernel, "add_far", [bf(128), bf(256)], args, alias={2: 1})
    received = ring(sent)
    args = (where, exps, q, pos, coef)
    outs = [f32(128), f32(256), f32(256), bf(640), bf(1280)]
    keep0, keep1, keep2, send, w_other = call(
        other_terms_kernel, "other_terms", outs, args, mib=16, smem=1
    )
    (losses,) = call(losses_kernel, "losses", [((4, 64), F32)], (where, coef), smem=1)
    args = (where, received, keep3, swap_core(send3), send, coef)
    outs = [bf(256), bf(640), stats_like]
    sent, send, coef = call(add_third_kernel, "add_third", outs, args, smem=1, alias={4: 1, 5: 2})
    received = ring(sent)
    other = swap_core(send)

    args = (where, p_near, p_far, coef, w_far, w_third, w_other)
    kernel = functools.partial(query_terms_kernel, (2, 1))
    sent2, sent1 = call(kernel, "query_terms", [bf(256)] * 2, args, mib=16, smem=1)
    kernel = functools.partial(query_terms_kernel, (3, 0))
    sent3, keep = call(kernel, "query_terms", [bf(256), f32(256)], args, mib=16, smem=1)
    moved = [shift_plane(v, 1, k + 1) for k, v in enumerate((sent1, sent2, sent3))]

    args = (received, keep2, other, sent1, sent2, sent3)
    (sent,) = call(add_second_kernel, "add_second", [bf(256)], args)
    received = ring(sent)
    same, cross = call(add_first_kernel, "add_first", [bf(128)] * 2, (where, received, keep1, other), smem=1)
    args = (ring(same), ring_cross_out(cross), keep0, other, coef)
    (passage_grad,) = call(last_add_kernel, "last_add", [f32(128)], args)

    outs = [f32(64)] + [bf(64)] * 3
    keep, *sent = call(add_queries_kernel, "add_queries", outs, (keep, *moved))
    moved = [shift_plane(v, 0, k + 1) for k, v in enumerate(sent)]
    (query_grad,) = call(last_queries_kernel, "last_queries", [f32(64)], (coef, keep, *moved))

    others = swap_core(losses)
    losses = jnp.where(c == 0, jnp.stack([losses, others], axis=1), jnp.stack([others, losses], axis=1))
    return losses.reshape(512), query_grad, passage_grad


def solution(mesh):
    mesh = Mesh(mesh.devices.reshape(Y, Z, X, C), ("y", "z", "x", "core"))
    q_spec = P(("y", "z", "x", "core"), None)
    p_spec = P(("x", "core", "y", "z"), None)
    row_spec = P(("y", "z"))
    return jax.shard_map(
        body,
        mesh=mesh,
        in_specs=(q_spec, p_spec, row_spec),
        out_specs=(row_spec, q_spec, p_spec),
        check_vma=False,
    )
```

```python
import functools
import math

import jax
import jax.numpy as jnp
from jax import lax
from jax.experimental import pallas as pl
from jax.experimental.pallas import tpu as pltpu
from jax.sharding import Mesh, PartitionSpec as P

D = 1024
NQ = 16384
SCALE = 3.0 / math.sqrt(D)
TO_EXP2 = SCALE * math.log2(math.e)
X, Y, Z, C = 4, 4, 8, 2
PLANE = ("y", "x", "core")
BF, F32 = jnp.bfloat16, jnp.float32
MIB = 1 << 20
LARGEST = 46000.0
NEAR = [(0, 0, 2), (0, 0, 3), (1, 3, 0), (1, 3, 1)]
NEAR += [(sign, k, core) for k in (2, 1) for sign in (1, -1) for core in (0, 1)]
FAR = [(1, 4, 2), (1, 4, 3), (-1, 3, 0), (-1, 3, 1)]
N_NEAR, N_FAR = 1536, 512
TILE = 16
VMEM = pl.BlockSpec(memory_space=pltpu.VMEM)
SMEM = pl.BlockSpec(memory_space=pltpu.SMEM)
HBM = pl.BlockSpec(memory_space=pltpu.HBM)


def call(kernel, name, outs, args, scratch=(), mib=8, smem=0, alias=None, space=VMEM):
    return pl.pallas_call(
        kernel,
        out_shape=[jax.ShapeDtypeStruct(s, t) for s, t in outs],
        in_specs=[SMEM] * smem + [space] * (len(args) - smem),
        out_specs=[VMEM] * len(outs),
        scratch_shapes=list(scratch),
        input_output_aliases=alias or {},
        compiler_params=pltpu.CompilerParams(vmem_limit_bytes=mib * MIB),
        cost_estimate=pl.CostEstimate(flops=1000, bytes_accessed=1024, transcendentals=0),
        name=name,
    )(*args)


def ring(v, cross=False):
    pairs = []
    for z in range(Z):
        for c in range(C):
            to = ((z + 1) % Z) * C if c == int(cross) else ((z - 1) % Z) * C + 1
            pairs.append((z * C + c, to))
    return lax.ppermute(v, ("z", "core"), pairs)


def ring_cross_out(v):
    pairs = []
    for z in range(Z):
        for c in range(C):
            pairs.append((z * C + c, ((z + 1) % Z) * C + 1 if c == 0 else ((z - 1) % Z) * C))
    return lax.ppermute(v, ("z", "core"), pairs)


def shift_x(v, k):
    return lax.ppermute(v, "x", [(i, (i + k) % X) for i in range(X)])


def shift_y(v, k):
    return lax.ppermute(v, "y", [(i, (i + k) % Y) for i in range(Y)])


def swap_core(v):
    return lax.ppermute(v, "core", [(0, 1), (1, 0)])


def shift_plane(v, stage, k):
    pairs = []
    for y in range(Y):
        for x in range(X):
            for c in range(C):
                y2, x2 = (y, (x + k) % X) if c == stage else ((y + k) % Y, x)
                pairs.append(((y * X + x) * C + c, (y2 * X + x2) * C + c))
    return lax.ppermute(v, PLANE, pairs)


def encode(v):
    v2 = v * v
    v4 = v2 * v2
    v8 = v4 * v4
    return jnp.where(v < 0, -v8, v8).astype(BF)


def decode(code):
    y = code.astype(F32)
    size = jnp.abs(y)
    v = jnp.exp2(jnp.log2(jnp.maximum(size, 1e-37)) * 0.125)
    v = jnp.where(size < 1e-37, 0.0, v)
    return jnp.where(y < 0, -v, v)


def axes_of(where, c):
    x, y = where[0], where[1]
    return jnp.where(c == 0, x, y), jnp.where(c == 0, y, x)


def largest(v):
    v = jnp.max(jnp.abs(v).astype(F32), axis=0, keepdims=True)
    return jnp.max(v, axis=1, keepdims=True)


def rows_like(tile):
    return lax.broadcasted_iota(jnp.int32, tile.shape, 0)


def pack_kernel(where, passages, queries, positives, p_out, q_out, pos_ref, sems):
    copies = [
        pltpu.make_async_copy(src, dst, sems.at[i])
        for i, (src, dst) in enumerate(
            ((queries, q_out.at[pl.ds(0, 64)]), (positives, pos_ref), (passages, p_out.at[pl.ds(0, 128)]))
        )
    ]
    for copy in copies:
        copy.start()
    q_out[64:, :] = jnp.zeros((TILE, D), BF)
    copies[0].wait()
    p_out[128:, :] = jnp.broadcast_to(largest(q_out[:64, :]), (TILE, D)).astype(BF)
    copies[1].wait()
    pos = pos_ref[pl.ds(where[0], 1), :]
    pos = jnp.where(where[3] == 0, pos, jnp.concatenate([pos[:, 64:], pos[:, :64]], axis=1))
    tile = jnp.zeros((TILE, 128), F32)
    for i, part in enumerate((lax.shift_right_logical(pos, 8), jnp.bitwise_and(pos, 255))):
        tile = jnp.where(rows_like(tile) == i, part.astype(F32), tile)
    q_out[64:, :128] = tile.astype(BF)
    copies[2].wait()


def at_core(c):
    return pl.ds(pl.multiple_of(c * 128, 128), 128)


def round1_kernel(q0, q1, q2, q3, out):
    tile = jnp.zeros((TILE, 128), F32)
    for i, ref in enumerate((q0, q1, q2, q3)):
        out[i * 64 : (i + 1) * 64, :] = ref[:64, :]
        part = ref[64:, :128].astype(F32)
        tile = jnp.where(rows_like(tile) == i, part[0:1, :], tile)
        tile = jnp.where(rows_like(tile) == 4 + i, part[1:2, :], tile)
    out[256:, :] = jnp.zeros((TILE, D), BF)
    out[256:, :128] = tile.astype(BF)


def chip_kernel(where, same, cross, chip):
    c = where[3]
    chip[at_core(c), :] = same[:128, :]
    chip[at_core(1 - c), :] = cross[:128, :]
    chip[256:, :] = jnp.maximum(same[128:, :], cross[128:, :])


def round2_kernel(q_right, q_left, chip, right, left, *_):
    right[:128, :] = q_right[:128, :]
    right[128:, :] = q_right[256:, :]
    left[...] = q_left[128:, :]


def round3_kernel(where, own, right, left, right2, left2, chip, *refs):
    out, positives, _, scratch = refs[-4:]
    first, second = axes_of(where, where[3])
    for i, (ref, part, n) in enumerate(((own, 0, 4), (right, 0, 4), (left, 0, 4), (right2, 0, 2), (left2, 2, 2))):
        a = lax.rem(second + (0, 3, 1, 2, 2)[i], 4)
        tile = ref[n * 64 :, :128].astype(F32)
        for j in range(part, part + n):
            b = lax.rem(first + (0, 3, 1, 2)[j], 4)
            at = pl.ds(pl.multiple_of((a * 4 + b) * 64, 64), 64)
            out[at, :] = ref[(j - part) * 64 : (j - part + 1) * 64, :]
            pos = tile[j : j + 1, :] * 256.0 + tile[4 + j : 5 + j, :]
            scratch[pl.ds(a * 4 + b, 1), :] = pos.astype(jnp.int32)
    positives[...] = jnp.zeros((8, 256), jnp.int32)
    for a in range(4):
        for b in range(4):
            positives[a : a + 1, b * 64 : b * 64 + 64] = scratch[a * 4 + b : a * 4 + b + 1, :64]


def losses_kernel(where, coef, out):
    y, c = where[1], where[3]
    for x in range(4):
        a, b = coef[0:1, 512 + x * 64 : 576 + x * 64], coef[x : x + 1, 512:576]
        for k in range(1, 4):
            a = jnp.where(y == k, coef[k : k + 1, 512 + x * 64 : 576 + x * 64], a)
            b = jnp.where(y == k, coef[x : x + 1, 512 + k * 64 : 576 + k * 64], b)
        out[x : x + 1, :] = jnp.where(c == 0, a, b)


def first_passage(where, block):
    x, y, z, c = where[0], where[1], where[2], where[3]
    sign, k, core = block
    core = (0, 1, c, 1 - c)[core]
    return (((x * C + core) * Y + y) * Z + lax.rem(z + sign * k * (2 * c - 1) + Z, Z)) * 128


def softmax(where, blocks, raw, positives, exps, at):
    top = jnp.max(raw[...], axis=0, keepdims=True)
    total = jnp.zeros_like(top)
    pos_score = jnp.zeros_like(top)
    row = 0
    for block in blocks:
        part = raw[row : row + 128, :]
        e = jnp.exp2((part - top) * TO_EXP2)
        exps[row : row + 128, at] = e
        total += jnp.sum(e, axis=0, keepdims=True)
        hit = lax.broadcasted_iota(jnp.int32, part.shape, 0) == positives - first_passage(where, block)
        pos_score += jnp.sum(jnp.where(hit, part, 0.0), axis=0, keepdims=True)
        row += 128
    return top * SCALE, total, pos_score * SCALE


def product(p, q):
    return lax.dot_general(p, q, (((1,), (1,)), ((), ())), preferred_element_type=F32)


def near_scores_kernel(where, q, positives, own, other, *refs):
    pieces, (exps, stats, passages, raw0, raw1) = refs[:5], refs[5:]
    passages[0:128, :] = own[:128, :]
    passages[128:256, :] = other[:128, :]
    tile = jnp.maximum(own[128:, :128], other[128:, :128])
    for i, ref in enumerate(pieces):
        passages[(i + 1) * 256 : (i + 2) * 256, :] = ref[:256, :]
        tile = jnp.maximum(tile, ref[256:, :128])
    raws = (raw0, raw1)
    raw0[...] = product(passages[...], q[0:256, :])
    stats[...] = jnp.ones((8, 896), F32)
    stats[0:4, 768:] = jnp.broadcast_to(tile[0:1, :].astype(F32), (4, 128))
    for i in range(4):
        if i < 3:
            raws[(i + 1) % 2][...] = product(passages[...], q[(i + 1) * 256 : (i + 2) * 256, :])
        at = slice(i * 256, (i + 1) * 256)
        top, total, pos_score = softmax(where, NEAR, raws[i % 2], positives[i : i + 1, :], exps, at)
        stats[i : i + 1, 0:256] = top
        stats[i : i + 1, 256:512] = total
        stats[i : i + 1, 512:768] = pos_score
    stats[4:8, 768:] = jnp.broadcast_to(largest(passages[...]), (4, 128))


def far_scores_kernel(where, q, positives, near_stats, far, third, exps, stats, tops, passages, raw):
    passages[:128, :] = far[at_core(where[3]), :]
    passages[128:256, :] = far[at_core(1 - where[3]), :]
    passages[256:, :] = third[:256, :]
    tile = jnp.maximum(far[256:, :128], third[256:, :128])[0:1, :].astype(F32)
    raw[...] = product(passages[...], q[...])
    stats[...] = near_stats[...]
    tops[...] = jnp.zeros((8, 512), F32)
    for i in range(4):
        at = slice(i * 256, (i + 1) * 256)
        row = slice(i, i + 1)
        top, total, pos_score = softmax(where, FAR, raw.at[:, at], positives[row, :], exps, at)
        near_top = near_stats[row, 0:256]
        both = jnp.maximum(top, near_top)
        tops[row, 0:256] = near_top
        tops[row, 256:512] = top
        stats[row, 0:256] = both
        stats[row, 256:512] = total * jnp.exp(top - both) + near_stats[row, 256:512] * jnp.exp(near_top - both)
        stats[row, 512:768] = pos_score + near_stats[row, 512:768]
    stats[0:4, 768:] = jnp.maximum(near_stats[0:4, 768:], jnp.broadcast_to(tile, (4, 128)))
    stats[4:8, 768:] = jnp.maximum(near_stats[4:8, 768:], jnp.broadcast_to(largest(passages[...]), (4, 128)))


def merge_stats(parts):
    top = functools.reduce(jnp.maximum, [p[:, 0:256] for p in parts])
    totals = [p[:, 256:512] * jnp.exp(p[:, 0:256] - top) for p in parts]
    pos_scores = [p[:, 512:768] for p in parts]
    join = lambda v: (v[0] + v[3]) + (v[1] + v[2])
    rest = functools.reduce(jnp.maximum, [p[:, 768:] for p in parts])
    return top, join(totals), join(pos_scores), rest


def merge_kernel(*refs):
    out = refs[-1]
    top, total, pos_score, rest = merge_stats([r[...] for r in refs[:-1]])
    out[:, 0:256] = top
    out[:, 256:512] = total
    out[:, 512:768] = pos_score
    out[:, 768:] = rest


def finish_kernel(tops, *refs):
    out = refs[-1]
    top, total, pos_score, rest = merge_stats([r[...] for r in refs[:-1]])
    lse = top + jnp.log(total)
    out[:, 0:256] = jnp.exp(tops[:, 0:256] - lse)
    out[:, 256:512] = jnp.exp(tops[:, 256:512] - lse)
    out[:, 512:768] = lse - pos_score
    bound_p = (NQ * SCALE) * jnp.maximum(rest[0:1, :], 1e-30)
    bound_q = (2.0 * SCALE) * jnp.maximum(rest[4:5, :], 1e-30)
    out[0:1, 768:] = LARGEST / bound_p
    out[1:2, 768:] = bound_p / LARGEST
    out[2:3, 768:] = LARGEST / bound_q
    out[3:4, 768:] = bound_q / LARGEST
    out[4:8, 768:] = jnp.zeros((4, 128), F32)


def weigh(where, blocks, exps, row, positives, coef, k, weights):
    for i in range(4):
        at = slice(i * 256, (i + 1) * 256)
        factor = coef[i : i + 1, k : k + 256]
        pos = positives[i : i + 1, :]
        for j, block in enumerate(blocks):
            hit = lax.broadcasted_iota(jnp.int32, (128, 256), 0) == pos - first_passage(where, block)
            e = exps[row + j * 128 : row + (j + 1) * 128, at]
            weights[j * 128 : (j + 1) * 128, at] = ((e * factor - hit.astype(F32)) * SCALE).astype(BF)


def terms(weights, q, coef):
    for j in range(4):
        at = slice(j * 256, (j + 1) * 256)
        yield at, jnp.dot(weights[...], q[:, at], preferred_element_type=F32) * coef[0:1, 768:769]


def far_terms_kernel(where, exps, q, positives, coef, keep, send, weights, *_):
    weigh(where, FAR[:2], exps, 0, positives, coef, 256, weights)
    for at, g in terms(weights, q, coef):
        keep[:, at] = encode(g[:128])
        send[:, at] = encode(g[128:])


def third_terms_kernel(where, exps, far_exps, q, positives, coef, keep, send, weights, *_):
    weigh(where, NEAR[2:4], exps, 256, positives, coef, 0, weights.at[:256])
    weigh(where, FAR[2:], far_exps, 256, positives, coef, 256, weights.at[256:])
    for at, g in terms(weights, q, coef):
        send[:, at] = g[:256]
        keep[:, at] = g[256:]


def other_terms_kernel(where, exps, q, positives, coef, keep0, keep1, keep2, send, weights):
    weigh(where, NEAR[:2], exps, 0, positives, coef, 0, weights.at[:256])
    weigh(where, NEAR[4:], exps, 512, positives, coef, 0, weights.at[256:])
    for at, g in terms(weights, q, coef):
        keep0[:, at] = g[:128]
        send[512:, at] = g[128:256]
        send[:256, at] = g[256:512]
        keep2[:, at] = g[512:768]
        send[256:512, at] = g[768:1024]
        keep1[:, at] = g[1024:]


def add_third_kernel(where, same, cross, term, other, send, coef, out, *_):
    at, rest = at_core(where[3]), at_core(1 - where[3])
    out[at, :] = encode((term[at, :] + other[at, :]) + (decode(same[...]) + decode(cross[...])))
    out[rest, :] = encode(term[rest, :] + other[rest, :])


def add_second_kernel(received, term, other, *refs):
    refs[-1][...] = encode((term[...] + other[:256, :]) + decode(received[...]))


def add_first_kernel(where, received, term, other, same, cross):
    for ref, c in ((same, where[3]), (cross, 1 - where[3])):
        at = at_core(c)
        there = pl.ds(pl.multiple_of(256 + c * 128, 128), 128)
        ref[...] = encode((term[at, :] + other[there, :]) + decode(received[at, :]))


def last_add_kernel(same, cross, term, other, coef, out, done):
    total = (term[...] + other[512:, :]) + (decode(same[...]) + decode(cross[...]))
    out[...] = total * coef[1:2, 768:769]
    done[...] = jnp.zeros((8, 128), F32)


def query_terms_kernel(groups, where, near, far, coef, w_far, w_third, w_other, *outs):
    first, second = axes_of(where, where[3])
    for i, out in zip(groups, outs):
        at = pl.ds(pl.multiple_of(lax.rem(second + i, 4) * 256, 256), 256)
        w = jnp.concatenate([w_other[:256, at], w_third[:256, at], w_other[256:, at]], axis=0)
        g = lax.dot_general(w, near[...], (((0,), (0,)), ((), ())), preferred_element_type=F32)
        w = jnp.concatenate([w_far[:, at], w_third[256:, at]], axis=0)
        g += lax.dot_general(w, far[...], (((0,), (0,)), ((), ())), preferred_element_type=F32)
        g = g * coef[2:3, 768:769]
        g = encode(g) if i else g
        for b in range(4):
            to = pl.ds(pl.multiple_of(lax.rem(b - first + 4, 4) * 64, 64), 64)
            out[to, :] = g[b * 64 : (b + 1) * 64, :]


def add_queries_kernel(own, a, b, c, keep, *sent):
    total = (own[...] + decode(b[...])) + (decode(a[...]) + decode(c[...]))
    keep[...] = total[:64, :]
    for i, ref in enumerate(sent):
        ref[...] = encode(total[(i + 1) * 64 : (i + 2) * 64, :])


def last_queries_kernel(coef, own, a, b, c, done, out):
    total = (own[...] + decode(b[...])) + (decode(a[...]) + decode(c[...]))
    out[...] = total * coef[3:4, 768:769]


def body(queries, passages, positives):
    x, y, z, c = (lax.axis_index(a) for a in ("x", "y", "z", "core"))
    where = jnp.stack([x, y, z, c]).astype(jnp.int32)
    bf = lambda n: ((n, D), BF)
    f32 = lambda n: ((n, D), F32)
    stats_like = ((8, 896), F32)

    args = (where, passages, queries, positives.reshape(4, 128))
    scratch = [pltpu.VMEM((4, 128), jnp.int32), pltpu.SemaphoreType.DMA((3,))]
    packed, q = call(
        pack_kernel, "pack", [bf(144), bf(80)], args, scratch=scratch, mib=56, smem=1, space=HBM
    )
    same, cross = ring(packed), ring(packed, cross=True)
    (q,) = call(round1_kernel, "round1", [bf(272)], (q, *(shift_plane(q, 0, k) for k in (1, -1, 2))))
    (m1,) = call(chip_kernel, "chip", [bf(272)], (where, same, cross), smem=1)
    m2 = ring(m1)
    q_right, q_left = shift_plane(q, 1, 1), shift_plane(q, 1, -1)
    outs = [bf(144), bf(144), bf(272)]
    q_right2, q_left2, m2 = call(round2_kernel, "round2", outs, (q_right, q_left, m2), alias={2: 2})
    m3 = ring(m2)
    q_right2, q_left2 = shift_plane(q_right2, 1, 1), shift_plane(q_left2, 1, -1)
    other, t1, t2 = swap_core(packed), swap_core(m1), swap_core(m2)
    args = (where, q, q_right, q_left, q_right2, q_left2, m3, other, t1, t2)
    outs = [bf(1024), ((8, 256), jnp.int32), bf(272)]
    scratch = [pltpu.VMEM((16, 128), jnp.int32)]
    q, pos, m3 = call(round3_kernel, "round3", outs, args, scratch=scratch, smem=1, alias={6: 2})
    far, t3 = ring(m3), swap_core(m3)

    raw = pltpu.VMEM((N_NEAR, 256), F32)
    outs = [((N_NEAR, 1024), F32), stats_like, bf(N_NEAR)]
    args = (where, q, pos, packed, other, m3, m2, t2, m1, t1)
    exps, near_stats, p_near = call(
        near_scores_kernel, "near_scores", outs, args, scratch=[raw] * 2, mib=16, smem=1
    )
    outs = [((N_FAR, 1024), F32), stats_like, ((8, 512), F32), bf(N_FAR)]
    args = (where, q, pos, near_stats, far, t3)
    far_exps, stats, tops, p_far = call(
        far_scores_kernel, "far_scores", outs, args, scratch=[pltpu.VMEM((N_FAR, 1024), F32)], smem=1
    )

    parts = [stats] + [shift_x(stats, k) for k in (1, -1, 2)]
    (stats,) = call(merge_kernel, "merge", [stats_like], parts)
    parts = [stats] + [shift_y(stats, k) for k in (1, -1, 2)]
    (coef,) = call(finish_kernel, "finish", [stats_like], (tops, *parts))

    args = (where, far_exps, q, pos, coef)
    outs = [bf(128), bf(128), bf(256), stats_like]
    far_keep, far_send, w_far, coef = call(
        far_terms_kernel, "far_terms", outs, args, mib=12, smem=1, alias={4: 3}
    )
    args = (where, exps, far_exps, q, pos, coef)
    same, cross = ring(far_keep), ring(far_send, cross=True)
    outs = [f32(256), f32(256), bf(512), stats_like]
    keep3, send3, w_third, coef = call(
        third_terms_kernel, "third_terms", outs, args, mib=12, smem=1, alias={5: 3}
    )
    args = (where, exps, q, pos, coef)
    outs = [f32(128), f32(256), f32(256), f32(640), bf(1280)]
    keep0, keep1, keep2, send, w_other = call(
        other_terms_kernel, "other_terms", outs, args, mib=16, smem=1
    )
    (losses,) = call(losses_kernel, "losses", [((4, 64), F32)], (where, coef), smem=1)
    args = (where, same, cross, keep3, swap_core(send3), send, coef)
    outs = [bf(256), f32(640), stats_like]
    sent, send, coef = call(add_third_kernel, "add_third", outs, args, smem=1, alias={5: 1, 6: 2})
    received = ring(sent)
    other = swap_core(send)

    args = (where, p_near, p_far, coef, w_far, w_third, w_other)
    kernel = functools.partial(query_terms_kernel, (2, 1))
    sent2, sent1 = call(kernel, "query_terms", [bf(256)] * 2, args, mib=16, smem=1)
    kernel = functools.partial(query_terms_kernel, (3, 0))
    sent3, keep = call(kernel, "query_terms", [bf(256), f32(256)], args, mib=16, smem=1)
    moved = [shift_plane(v, 1, k + 1) for k, v in enumerate((sent1, sent2, sent3))]

    args = (received, keep2, other, sent1, sent2, sent3)
    (sent,) = call(add_second_kernel, "add_second", [bf(256)], args)
    received = ring(sent)
    same, cross = call(add_first_kernel, "add_first", [bf(128)] * 2, (where, received, keep1, other), smem=1)
    args = (ring(same), ring_cross_out(cross), keep0, other, coef)
    passage_grad, done = call(last_add_kernel, "last_add", [f32(128), ((8, 128), F32)], args)

    outs = [f32(64)] + [bf(64)] * 3
    keep, *sent = call(add_queries_kernel, "add_queries", outs, (keep, *moved))
    moved = [shift_plane(v, 0, k + 1) for k, v in enumerate(sent)]
    (query_grad,) = call(last_queries_kernel, "last_queries", [f32(64)], (coef, keep, *moved, done))

    others = swap_core(losses)
    losses = jnp.where(c == 0, jnp.stack([losses, others], axis=1), jnp.stack([others, losses], axis=1))
    return losses.reshape(512), query_grad, passage_grad


def solution(mesh):
    mesh = Mesh(mesh.devices.reshape(Y, Z, X, C), ("y", "z", "x", "core"))
    q_spec = P(("y", "z", "x", "core"), None)
    p_spec = P(("x", "core", "y", "z"), None)
    row_spec = P(("y", "z"))
    return jax.shard_map(
        body,
        mesh=mesh,
        in_specs=(q_spec, p_spec, row_spec),
        out_specs=(row_spec, q_spec, p_spec),
        check_vma=False,
    )
```

```python
import functools
import math

import jax
import jax.numpy as jnp
from jax import lax
from jax.experimental import pallas as pl
from jax.experimental.pallas import tpu as pltpu
from jax.sharding import Mesh, PartitionSpec as P

D = 1024
NQ = 16384
SCALE = 3.0 / math.sqrt(D)
TO_EXP2 = SCALE * math.log2(math.e)
X, Y, Z, C = 4, 4, 8, 2
PLANE = ("y", "x", "core")
BF, F32 = jnp.bfloat16, jnp.float32
MIB = 1 << 20
LARGEST = 46000.0
VMEM = pl.BlockSpec(memory_space=pltpu.VMEM)
SMEM = pl.BlockSpec(memory_space=pltpu.SMEM)


def call(kernel, name, outs, args, scratch=(), mib=8, smem=0, alias=None):
    return pl.pallas_call(
        kernel,
        out_shape=[jax.ShapeDtypeStruct(s, t) for s, t in outs],
        in_specs=[SMEM] * smem + [VMEM] * (len(args) - smem),
        out_specs=[VMEM] * len(outs),
        scratch_shapes=list(scratch),
        input_output_aliases=alias or {},
        compiler_params=pltpu.CompilerParams(vmem_limit_bytes=mib * MIB),
        cost_estimate=pl.CostEstimate(flops=1000, bytes_accessed=1024, transcendentals=0),
        name=name,
    )(*args)


def shift_z(v, k):
    return lax.ppermute(v, "z", [(i, (i + k) % Z) for i in range(Z)])


def flip_z(v, k):
    return lax.ppermute(v, "z", [(i, i ^ k) for i in range(Z)])


def shift_x(v, k):
    return lax.ppermute(v, "x", [(i, (i + k) % X) for i in range(X)])


def shift_y(v, k):
    return lax.ppermute(v, "y", [(i, (i + k) % Y) for i in range(Y)])


def flip_y(v, k):
    return lax.ppermute(v, "y", [(i, i ^ k) for i in range(Y)])


def swap_core(v):
    return lax.ppermute(v, "core", [(0, 1), (1, 0)])


def shift_plane(v, stage, k):
    pairs = []
    for y in range(Y):
        for x in range(X):
            for c in range(C):
                y2, x2 = (y, (x + k) % X) if c == stage else ((y + k) % Y, x)
                pairs.append(((y * X + x) * C + c, (y2 * X + x2) * C + c))
    return lax.ppermute(v, PLANE, pairs)


def encode(v):
    v2 = v * v
    v4 = v2 * v2
    v8 = v4 * v4
    return jnp.where(v < 0, -v8, v8).astype(BF)


def decode(code):
    y = code.astype(F32)
    size = jnp.abs(y)
    v = jnp.exp2(jnp.log2(jnp.maximum(size, 1e-37)) * 0.125)
    v = jnp.where(size < 1e-37, 0.0, v)
    return jnp.where(y < 0, -v, v)


def axes_of(where, c):
    x, y = where[0], where[1]
    return jnp.where(c == 0, x, y), jnp.where(c == 0, y, x)


def largest(v):
    v = jnp.max(jnp.abs(v).astype(F32), axis=0, keepdims=True)
    return jnp.max(v, axis=1, keepdims=True)


def sort_positives(where, near, out):
    y, c = where[1], where[3]
    rows = []
    for a in range(4):
        r = near[0]
        for j in range(1, 4):
            r = jnp.where(jnp.bitwise_xor(y, j) == a, near[j], r)
        rows.append(r)
    for k in range(4):
        for b in range(4):
            at = slice(b * 64, b * 64 + 64)
            core0, core1 = rows[k][b : b + 1, :64], rows[b][k : k + 1, 64:]
            out[k : k + 1, at] = jnp.where(c == 0, core0, core1)
            out[4 + k : 5 + k, at] = jnp.where(c == 0, core1, core0)


def round1_kernel(q0, q1, q2, q3, out, top):
    for i, ref in enumerate((q0, q1, q2, q3)):
        out[i * 64 : (i + 1) * 64, :] = ref[...]
    top[...] = jnp.broadcast_to(largest(q0[...]), (8, 128))


def round2_kernel(q_right, q_left, pos0, pos1, top0, top1, right, left, pos, top):
    right[...] = q_right[:128, :]
    left[...] = q_left[128:, :]
    pos[:4, :] = pos0[...]
    pos[4:, :] = pos1[...]
    top[...] = jnp.maximum(top0[...], top1[...])


def round3_kernel(where, own, right, left, right2, left2, pos0, pos1, top0, top1, out, positives, top):
    first, second = axes_of(where, where[3])
    for i, (ref, part) in enumerate(((own, 0), (right, 0), (left, 0), (right2, 0), (left2, 2))):
        a = lax.rem(second + (0, 3, 1, 2, 2)[i], 4)
        for j in range(ref.shape[0] // 64):
            b = lax.rem(first + (0, 3, 1, 2)[j + part], 4)
            at = pl.ds(pl.multiple_of((a * 4 + b) * 64, 64), 64)
            out[at, :] = ref[j * 64 : (j + 1) * 64, :]
    sort_positives(where, (pos0[:4, :], pos0[4:, :], pos1[:4, :], pos1[4:, :]), positives)
    top[...] = jnp.maximum(top0[...], top1[...])


def losses_kernel(where, coef, out):
    y, c = where[1], where[3]
    v = coef[:, 512:768]
    core0, core1 = jnp.where(c == 0, v[:4], v[4:]), jnp.where(c == 0, v[4:], v[:4])
    for x in range(4):
        a, b = core0[0:1, x * 64 : x * 64 + 64], core1[x : x + 1, :64]
        for k in range(1, 4):
            a = jnp.where(y == k, core0[k : k + 1, x * 64 : x * 64 + 64], a)
            b = jnp.where(y == k, core1[x : x + 1, k * 64 : k * 64 + 64], b)
        out[x : x + 1, :64] = a
        out[x : x + 1, 64:] = b


def first_passage(where):
    x, y, c = where[0], where[1], where[3]
    return ((x * C + c) * Y + y) * (Z * 128)


def rows_of(where, offset):
    return pl.ds(pl.multiple_of(lax.rem(where[2] + offset + Z, Z) * 128, 128), 128)


def softmax(where, raw, positives, exps, at):
    top = jnp.max(raw[...], axis=0, keepdims=True)
    total = jnp.zeros_like(top)
    pos_score = jnp.zeros_like(top)
    for row in range(0, 1024, 128):
        part = raw[row : row + 128, :]
        e = jnp.exp2((part - top) * TO_EXP2)
        exps[row : row + 128, at] = e
        total += jnp.sum(e, axis=0, keepdims=True)
        hit = lax.broadcasted_iota(jnp.int32, part.shape, 0) == positives - (first_passage(where) + row)
        pos_score += jnp.sum(jnp.where(hit, part, 0.0), axis=0, keepdims=True)
    return top * SCALE, total, pos_score * SCALE


def product(p, q):
    return lax.dot_general(p, q, (((1,), (1,)), ((), ())), preferred_element_type=F32)


def scores_kernel(where, q_own, q_other, positives, passages, top0, top1, exps, stats, raw0, raw1):
    blocks = [q.at[i * 256 : (i + 1) * 256] for q in (q_own, q_other) for i in range(4)]
    raws = (raw0, raw1)
    raw0[...] = product(passages[...], blocks[0][...])
    largest_q = jnp.maximum(top0[0:1, :], top1[0:1, :])
    stats[0:4, 768:] = jnp.broadcast_to(largest_q, (4, 128))
    stats[4:8, 768:] = jnp.broadcast_to(largest(passages[...]), (4, 128))
    for i in range(8):
        if i < 7:
            raws[(i + 1) % 2][...] = product(passages[...], blocks[i + 1][...])
        row, at = slice(i, i + 1), slice(i * 256, (i + 1) * 256)
        top, total, pos_score = softmax(where, raws[i % 2], positives[row, :], exps, at)
        stats[row, 0:256] = top
        stats[row, 256:512] = total
        stats[row, 512:768] = pos_score


def merge_stats(parts):
    top = functools.reduce(jnp.maximum, [p[:, 0:256] for p in parts])
    totals = [p[:, 256:512] * jnp.exp(p[:, 0:256] - top) for p in parts]
    pos_scores = [p[:, 512:768] for p in parts]
    if len(parts) == 4:
        join = lambda v: (v[0] + v[3]) + (v[1] + v[2])
    else:
        join = lambda v: v[0] + v[1]
    rest = functools.reduce(jnp.maximum, [p[:, 768:] for p in parts])
    return top, join(totals), join(pos_scores), rest


def merge_kernel(*refs):
    out = refs[-1]
    top, total, pos_score, rest = merge_stats([r[...] for r in refs[:-1]])
    out[:, 0:256] = top
    out[:, 256:512] = total
    out[:, 512:768] = pos_score
    out[:, 768:] = rest


def finish_kernel(local, one, two, out):
    two = jnp.concatenate(
        [jnp.concatenate([two[4:8, :768], two[0:4, :768]], axis=0), two[:, 768:]], axis=1
    )
    top, total, pos_score, rest = merge_stats([one[...], two])
    lse = top + jnp.log(total)
    out[:, 0:256] = jnp.exp(local[:, 0:256] - lse)
    out[:, 256:512] = jnp.zeros_like(lse)
    out[:, 512:768] = lse - pos_score
    bound_p = (NQ * SCALE) * jnp.maximum(rest[0:1, :], 1e-30)
    bound_q = (2.0 * SCALE) * jnp.maximum(rest[4:5, :], 1e-30)
    out[0:1, 768:] = LARGEST / bound_p
    out[1:2, 768:] = bound_p / LARGEST
    out[2:3, 768:] = LARGEST / bound_q
    out[3:4, 768:] = bound_q / LARGEST
    out[4:8, 768:] = jnp.zeros((4, 128), F32)


def weigh(where, offsets, exps, positives, coef, weights):
    rows = [rows_of(where, offset) for offset in offsets]
    first = first_passage(where)
    for i in range(8):
        at = slice(i * 256, (i + 1) * 256)
        factor = coef[i : i + 1, 0:256]
        for row, offset in zip(rows, offsets):
            start = first + lax.rem(where[2] + offset + Z, Z) * 128
            hit = lax.broadcasted_iota(jnp.int32, (128, 256), 0) == positives[i : i + 1, :] - start
            weights[row, at] = ((exps[row, at] * factor - hit.astype(F32)) * SCALE).astype(BF)
    return rows


def terms(rows, weights, q_own, q_other, coef):
    w_own = jnp.concatenate([weights[row, :1024] for row in rows], axis=0)
    w_other = jnp.concatenate([weights[row, 1024:] for row in rows], axis=0)
    for j in range(4):
        at = slice(j * 256, (j + 1) * 256)
        g = jnp.dot(w_own, q_own[:, at], preferred_element_type=F32)
        g += jnp.dot(w_other, q_other[:, at], preferred_element_type=F32)
        yield at, g * coef[0:1, 768:769]


def first_terms_kernel(
    where, exps, q_own, q_other, positives, coef, right, left, term_left, term_right, weights, *_
):
    rows = weigh(where, (4, -3, 3), exps, positives, coef, weights)
    for at, g in terms(rows, weights, q_own, q_other, coef):
        right[:, at] = encode(g[:64])
        left[:, at] = encode(g[64:128])
        term_left[:, at] = g[128:256]
        term_right[:, at] = g[256:]


def other_terms_kernel(where, exps, q_own, q_other, positives, coef, _, *outs):
    grads, weights = outs[:5], outs[5]
    rows = weigh(where, (0, -2, 2, -1, 1), exps, positives, coef, weights)
    for at, g in terms(rows, weights, q_own, q_other, coef):
        for i, ref in enumerate(grads):
            ref[:, at] = g[i * 128 : (i + 1) * 128]


def add_halves_kernel(from_left, from_right, term_left, term_right, other0, other1, right, left, *_):
    right[:64, :] = encode(term_right[:64, :] + decode(from_left[...]))
    right[64:, :] = encode(term_right[64:, :])
    left[:64, :] = encode(term_left[:64, :])
    left[64:, :] = encode(term_left[64:, :] + decode(from_right[...]))


def add_kernel(received, term, *refs):
    out = refs[-1]
    out[...] = encode(term[...] + decode(received[...]))


def last_add_kernel(coef, from_left, from_right, term, out):
    out[...] = (term[...] + (decode(from_left[...]) + decode(from_right[...]))) * coef[1:2, 768:769]


def query_terms(own, where, passages, coef, weights, i):
    _, second = axes_of(where, where[3] if own else 1 - where[3])
    at = pl.ds(pl.multiple_of((0 if own else 1024) + lax.rem(second + i, 4) * 256, 256), 256)
    g = lax.dot_general(weights[:, at], passages[...], (((0,), (0,)), ((), ())), preferred_element_type=F32)
    return g * coef[2:3, 768:769]


def row_of(where, b):
    first, _ = axes_of(where, where[3])
    return pl.ds(pl.multiple_of(lax.rem(b - first + 4, 4) * 64, 64), 64)


def send_queries_kernel(where, passages, coef, weights, out0, out1):
    for i in range(4):
        g = encode(query_terms(False, where, passages, coef, weights, i))
        (out0, out1)[i // 2][i % 2 * 256 : (i % 2 + 1) * 256, :] = g


def keep_queries_kernel(where, passages, coef, weights, other0, other1, keep, *sent):
    for i, ref in enumerate((keep, *sent)):
        g = query_terms(True, where, passages, coef, weights, i)
        g += decode((other0, other1)[i // 2][i % 2 * 256 : (i % 2 + 1) * 256, :])
        g = g if i == 0 else encode(g)
        for b in range(4):
            ref[row_of(where, b), :] = g[b * 64 : (b + 1) * 64, :]


def add_queries_kernel(own, a, b, c, keep, *sent):
    total = (own[...] + decode(b[...])) + (decode(a[...]) + decode(c[...]))
    keep[...] = total[:64, :]
    for i, ref in enumerate(sent):
        ref[...] = encode(total[(i + 1) * 64 : (i + 2) * 64, :])


def last_queries_kernel(coef, own, a, b, c, out):
    total = (own[...] + decode(b[...])) + (decode(a[...]) + decode(c[...]))
    out[...] = total * coef[3:4, 768:769]


def body(queries, passages, positives):
    x, y, z, c = (lax.axis_index(a) for a in ("x", "y", "z", "core"))
    where = jnp.stack([x, y, z, c]).astype(jnp.int32)
    bf = lambda n: ((n, D), BF)
    f32 = lambda n: ((n, D), F32)

    p_all = lax.all_gather(passages, "z", axis=0, tiled=True)
    args = (queries, *(shift_plane(queries, 0, k) for k in (1, -1, 2)))
    q, top = call(round1_kernel, "round1", [bf(256), ((8, 128), F32)], args)
    q_right, q_left = shift_plane(q, 1, 1), shift_plane(q, 1, -1)
    pos = positives.reshape(4, 128)
    args = (q_right, q_left, pos, flip_y(pos, 1), top, flip_z(top, 1))
    outs = [bf(128), bf(128), ((8, 128), jnp.int32), ((8, 128), F32)]
    q_right2, q_left2, pos, top = call(round2_kernel, "round2", outs, args)
    q_right2, q_left2 = shift_plane(q_right2, 1, 1), shift_plane(q_left2, 1, -1)
    args = (where, q, q_right, q_left, q_right2, q_left2, pos, flip_y(pos, 2), top, flip_z(top, 2))
    outs = [bf(1024), ((8, 256), jnp.int32), ((8, 128), F32)]
    q_own, pos, top = call(round3_kernel, "round3", outs, args, smem=1)
    q_other = swap_core(q_own)

    raws = [pltpu.VMEM((1024, 256), F32)] * 2
    outs = [((1024, 2048), F32), ((8, 896), F32)]
    args = (where, q_own, q_other, pos, p_all, top, flip_z(top, 4))
    exps, stats = call(scores_kernel, "scores", outs, args, scratch=raws, mib=16, smem=1)
    local = stats

    for shift in (shift_x, shift_y):
        args = [stats] + [shift(stats, k) for k in (1, -1, 2)]
        (stats,) = call(merge_kernel, "merge", [((8, 896), F32)], args)
    (coef,) = call(finish_kernel, "finish", [((8, 896), F32)], (local, stats, swap_core(stats)))

    args = (where, exps, q_own, q_other, pos, coef)
    outs = [bf(64), bf(64), f32(128), f32(128), ((1024, 2048), BF), ((8, 896), F32)]
    right, left, left3, right3, weights, coef = call(
        first_terms_kernel, "first_terms", outs, args, mib=16, smem=1, alias={5: 5}
    )
    (losses,) = call(losses_kernel, "losses", [((4, 128), F32)], (where, coef), smem=1)
    right, left = shift_z(right, 1), shift_z(left, -1)
    args = (where, exps, q_own, q_other, pos, coef, weights)
    outs = [f32(128)] * 5 + [((1024, 2048), BF)]
    own, left2, right2, left1, right1, weights = call(
        other_terms_kernel, "other_terms", outs, args, mib=16, smem=1, alias={6: 5}
    )
    args = (where, p_all, coef, weights)
    other0, other1 = call(send_queries_kernel, "send_queries", [bf(512)] * 2, args, mib=16, smem=1)
    args = (right, left, left3, right3, other0, other1)
    outs = [bf(128)] * 2 + [bf(512)] * 2
    right, left, other0, other1 = call(add_halves_kernel, "add_halves", outs, args, alias={4: 2, 5: 3})
    right, left = shift_z(right, 1), shift_z(left, -1)
    for to_right, to_left, done in ((right2, left2, ()), (right1, left1, (losses,))):
        (right,) = call(add_kernel, "add_right", [bf(128)], (right, to_right, *done))
        right = shift_z(right, 1)
        (left,) = call(add_kernel, "add_left", [bf(128)], (left, to_left))
        left = shift_z(left, -1)
    (passage_grad,) = call(last_add_kernel, "last_add", [f32(128)], (coef, right, left, own))

    args = (where, p_all, coef, weights, swap_core(other0), swap_core(other1))
    outs = [f32(256)] + [bf(256)] * 3
    keep, *sent = call(keep_queries_kernel, "keep_queries", outs, args, mib=16, smem=1)
    moved = [shift_plane(v, 1, k + 1) for k, v in enumerate(sent)]
    outs = [f32(64)] + [bf(64)] * 3
    keep, *sent = call(add_queries_kernel, "add_queries", outs, (keep, *moved))
    moved = [shift_plane(v, 0, k + 1) for k, v in enumerate(sent)]
    (query_grad,) = call(last_queries_kernel, "last_queries", [f32(64)], (coef, keep, *moved))
    return losses.reshape(512), query_grad, passage_grad


def solution(mesh):
    mesh = Mesh(mesh.devices.reshape(Y, Z, X, C), ("y", "z", "x", "core"))
    q_spec = P(("y", "z", "x", "core"), None)
    p_spec = P(("x", "core", "y", "z"), None)
    row_spec = P(("y", "z"))
    return jax.shard_map(
        body,
        mesh=mesh,
        in_specs=(q_spec, p_spec, row_spec),
        out_specs=(row_spec, q_spec, p_spec),
        check_vma=False,
    )
```

```python
import functools
import math

import jax
import jax.numpy as jnp
from jax import lax
from jax.experimental import pallas as pl
from jax.experimental.pallas import tpu as pltpu
from jax.sharding import Mesh, PartitionSpec as P

D = 1024
NQ = 16384
SCALE = 3.0 / math.sqrt(D)
TO_EXP2 = SCALE * math.log2(math.e)
X, Y, Z, C = 4, 4, 8, 2
PLANE = ("y", "x", "core")
BF, F32 = jnp.bfloat16, jnp.float32
MIB = 1 << 20
LARGEST = 46000.0
NEAR = ((0, 0, 128), (-3, 0, 128), (3, 0, 128), (-2, 0, 128), (2, 0, 128), (-1, 0, 128), (1, 0, 128))
FAR = ((4, 0, 64), (4, 64, 64))
N_NEAR, N_FAR = 896, 128
TILE = 16
VMEM = pl.BlockSpec(memory_space=pltpu.VMEM)
SMEM = pl.BlockSpec(memory_space=pltpu.SMEM)


def call(kernel, name, outs, args, scratch=(), mib=8, smem=0, alias=None):
    return pl.pallas_call(
        kernel,
        out_shape=[jax.ShapeDtypeStruct(s, t) for s, t in outs],
        in_specs=[SMEM] * smem + [VMEM] * (len(args) - smem),
        out_specs=[VMEM] * len(outs),
        scratch_shapes=list(scratch),
        input_output_aliases=alias or {},
        compiler_params=pltpu.CompilerParams(vmem_limit_bytes=mib * MIB),
        cost_estimate=pl.CostEstimate(flops=1000, bytes_accessed=1024, transcendentals=0),
        name=name,
    )(*args)


def shift_z(v, k):
    return lax.ppermute(v, "z", [(i, (i + k) % Z) for i in range(Z)])


def shift_x(v, k):
    return lax.ppermute(v, "x", [(i, (i + k) % X) for i in range(X)])


def shift_y(v, k):
    return lax.ppermute(v, "y", [(i, (i + k) % Y) for i in range(Y)])


def swap_core(v):
    return lax.ppermute(v, "core", [(0, 1), (1, 0)])


def shift_plane(v, stage, k):
    pairs = []
    for y in range(Y):
        for x in range(X):
            for c in range(C):
                y2, x2 = (y, (x + k) % X) if c == stage else ((y + k) % Y, x)
                pairs.append(((y * X + x) * C + c, (y2 * X + x2) * C + c))
    return lax.ppermute(v, PLANE, pairs)


def encode(v):
    v2 = v * v
    v4 = v2 * v2
    v8 = v4 * v4
    return jnp.where(v < 0, -v8, v8).astype(BF)


def decode(code):
    y = code.astype(F32)
    size = jnp.abs(y)
    v = jnp.exp2(jnp.log2(jnp.maximum(size, 1e-37)) * 0.125)
    v = jnp.where(size < 1e-37, 0.0, v)
    return jnp.where(y < 0, -v, v)


def axes_of(where, c):
    x, y = where[0], where[1]
    return jnp.where(c == 0, x, y), jnp.where(c == 0, y, x)


def largest(v):
    v = jnp.max(jnp.abs(v).astype(F32), axis=0, keepdims=True)
    return jnp.max(v, axis=1, keepdims=True)


def rows_like(tile):
    return lax.broadcasted_iota(jnp.int32, tile.shape, 0)


def pack_passages_kernel(passages, queries, out):
    out[:128, :] = passages[...]
    out[128:, :] = jnp.broadcast_to(largest(queries[...]), (TILE, D)).astype(BF)


def pack_queries_kernel(where, queries, positives, out):
    out[:64, :] = queries[...]
    out[64:, :] = jnp.zeros((TILE, D), BF)
    pos = positives[pl.ds(where[0], 1), :]
    pos = jnp.where(where[3] == 0, pos, jnp.concatenate([pos[:, 64:], pos[:, :64]], axis=1))
    tile = jnp.zeros((TILE, 128), F32)
    for i, part in enumerate((lax.shift_right_logical(pos, 8), jnp.bitwise_and(pos, 255))):
        tile = jnp.where(rows_like(tile) == i, part.astype(F32), tile)
    out[64:, :128] = tile.astype(BF)


def round1_kernel(q0, q1, q2, q3, out):
    tile = jnp.zeros((TILE, 128), F32)
    for i, ref in enumerate((q0, q1, q2, q3)):
        out[i * 64 : (i + 1) * 64, :] = ref[:64, :]
        part = ref[64:, :128].astype(F32)
        tile = jnp.where(rows_like(tile) == i, part[0:1, :], tile)
        tile = jnp.where(rows_like(tile) == 4 + i, part[1:2, :], tile)
    out[256:, :] = jnp.zeros((TILE, D), BF)
    out[256:, :128] = tile.astype(BF)


def cut_kernel(z_right, z_left, far_right, far_left):
    far_right[:64, :] = z_right[:64, :]
    far_right[64:, :] = z_right[128:, :]
    far_left[...] = z_left[64:, :]


def round2_kernel(q_right, q_left, z_right, z_left, right, left):
    right[:128, :] = q_right[:128, :]
    right[128:, :] = q_right[256:, :]
    left[...] = q_left[128:, :]


def round3_kernel(where, own, right, left, right2, left2, far0, far1, out, positives, scratch):
    first, second = axes_of(where, where[3])
    for i, (ref, part, n) in enumerate(((own, 0, 4), (right, 0, 4), (left, 0, 4), (right2, 0, 2), (left2, 2, 2))):
        a = lax.rem(second + (0, 3, 1, 2, 2)[i], 4)
        tile = ref[n * 64 :, :128].astype(F32)
        for j in range(part, part + n):
            b = lax.rem(first + (0, 3, 1, 2)[j], 4)
            at = pl.ds(pl.multiple_of((a * 4 + b) * 64, 64), 64)
            out[at, :] = ref[(j - part) * 64 : (j - part + 1) * 64, :]
            pos = tile[j : j + 1, :] * 256.0 + tile[4 + j : 5 + j, :]
            scratch[pl.ds(a * 4 + b, 1), :] = pos.astype(jnp.int32)
    positives[...] = jnp.zeros((8, 256), jnp.int32)
    for a in range(4):
        for b in range(4):
            positives[a : a + 1, b * 64 : b * 64 + 64] = scratch[a * 4 + b : a * 4 + b + 1, :64]


def losses_kernel(where, coef, out, done):
    done[...] = jnp.zeros((8, 128), F32)
    y, c = where[1], where[3]
    v = coef[:, 512:768]
    core0, core1 = jnp.where(c == 0, v[:4], v[4:]), jnp.where(c == 0, v[4:], v[:4])
    for x in range(4):
        a, b = core0[0:1, x * 64 : x * 64 + 64], core1[x : x + 1, :64]
        for k in range(1, 4):
            a = jnp.where(y == k, core0[k : k + 1, x * 64 : x * 64 + 64], a)
            b = jnp.where(y == k, core1[x : x + 1, k * 64 : k * 64 + 64], b)
        out[x : x + 1, :64] = a
        out[x : x + 1, 64:] = b


def first_passage(where, offset):
    x, y, z, c = where[0], where[1], where[2], where[3]
    return (((x * C + c) * Y + y) * Z + lax.rem(z + offset + Z, Z)) * 128


def softmax(where, rows, raw, positives, exps, at):
    top = jnp.max(raw[...], axis=0, keepdims=True)
    total = jnp.zeros_like(top)
    pos_score = jnp.zeros_like(top)
    row = 0
    for offset, start, n in rows:
        part = raw[row : row + n, :]
        e = jnp.exp2((part - top) * TO_EXP2)
        exps[row : row + n, at] = e
        total += jnp.sum(e, axis=0, keepdims=True)
        hit = lax.broadcasted_iota(jnp.int32, part.shape, 0) == positives - (first_passage(where, offset) + start)
        pos_score += jnp.sum(jnp.where(hit, part, 0.0), axis=0, keepdims=True)
        row += n
    return top * SCALE, total, pos_score * SCALE


def product(p, q):
    return lax.dot_general(p, q, (((1,), (1,)), ((), ())), preferred_element_type=F32)


def score_blocks(where, q, passages, positives, first, raws, exps, stats):
    raws[0][...] = product(passages[...], q[0:256, :])
    for i in range(4):
        if i < 3:
            raws[(i + 1) % 2][...] = product(passages[...], q[(i + 1) * 256 : (i + 2) * 256, :])
        at, row = slice(i * 256, (i + 1) * 256), slice(first + i, first + i + 1)
        top, total, pos_score = softmax(where, NEAR + FAR, raws[i % 2], positives[row, :], exps, at)
        stats[row, 0:256] = top
        stats[row, 256:512] = total
        stats[row, 512:768] = pos_score


def own_scores_kernel(where, q, positives, *refs):
    pieces, (exps, stats, passages, *raws) = refs[: len(NEAR) + 2], refs[len(NEAR) + 2 :]
    largest_q, row = None, 0
    for ref in pieces:
        n = ref.shape[0] - TILE
        passages[row : row + n, :] = ref[:n, :]
        v = ref[n : n + 1, :128].astype(F32)
        largest_q = v if largest_q is None else jnp.maximum(largest_q, v)
        row += n
    stats[0:4, 768:] = jnp.broadcast_to(largest_q, (4, 128))
    stats[4:8, 768:] = jnp.broadcast_to(largest(passages[...]), (4, 128))
    score_blocks(where, q, passages, positives, 0, raws, exps, stats)


def other_scores_kernel(where, q, pos_own, pos_other, passages, own_stats, exps, stats, positives, *raws):
    positives[:4, :] = pos_own[:4, :]
    positives[4:, :] = pos_other[:4, :]
    stats[0:4, :] = own_stats[0:4, :]
    stats[4:8, 768:] = own_stats[4:8, 768:]
    score_blocks(where, q, passages, positives, 4, raws, exps, stats)


def merge_stats(parts):
    top = functools.reduce(jnp.maximum, [p[:, 0:256] for p in parts])
    totals = [p[:, 256:512] * jnp.exp(p[:, 0:256] - top) for p in parts]
    pos_scores = [p[:, 512:768] for p in parts]
    if len(parts) == 4:
        join = lambda v: (v[0] + v[3]) + (v[1] + v[2])
    else:
        join = lambda v: v[0] + v[1]
    rest = functools.reduce(jnp.maximum, [p[:, 768:] for p in parts])
    return top, join(totals), join(pos_scores), rest


def merge_kernel(*refs):
    out = refs[-1]
    top, total, pos_score, rest = merge_stats([r[...] for r in refs[:-1]])
    out[:, 0:256] = top
    out[:, 256:512] = total
    out[:, 512:768] = pos_score
    out[:, 768:] = rest


def finish_kernel(local, one, two, out):
    two = jnp.concatenate(
        [jnp.concatenate([two[4:8, :768], two[0:4, :768]], axis=0), two[:, 768:]], axis=1
    )
    top, total, pos_score, rest = merge_stats([one[...], two])
    lse = top + jnp.log(total)
    out[:, 0:256] = jnp.exp(local[:, 0:256] - lse)
    out[:, 256:512] = jnp.zeros_like(lse)
    out[:, 512:768] = lse - pos_score
    bound_p = (NQ * SCALE) * jnp.maximum(rest[0:1, :], 1e-30)
    bound_q = (2.0 * SCALE) * jnp.maximum(rest[4:5, :], 1e-30)
    out[0:1, 768:] = LARGEST / bound_p
    out[1:2, 768:] = bound_p / LARGEST
    out[2:3, 768:] = LARGEST / bound_q
    out[3:4, 768:] = bound_q / LARGEST
    out[4:8, 768:] = jnp.zeros((4, 128), F32)


def weigh(where, rows, exps, positives, coef, first, weights):
    for i in range(4):
        at = slice(i * 256, (i + 1) * 256)
        factor = coef[first + i : first + i + 1, 0:256]
        pos = positives[first + i : first + i + 1, :]
        row = 0
        for offset, start, n, r in rows:
            hit = lax.broadcasted_iota(jnp.int32, (n, 256), 0) == pos - (first_passage(where, offset) + start)
            weights[row : row + n, at] = ((exps[r : r + n, at] * factor - hit.astype(F32)) * SCALE).astype(BF)
            row += n


def scaled_terms(w_own, w_other, q_own, q_other, scale, at):
    g = jnp.dot(w_own[...], q_own[:, at], preferred_element_type=F32)
    return (g + jnp.dot(w_other[...], q_other[:, at], preferred_element_type=F32)) * scale


BLOCKS = [(o, s, n, 128 * i) for i, (o, s, n) in enumerate(NEAR)]
FAR_BLOCKS = [(o, s, n, N_NEAR + s) for o, s, n in FAR]


def first_terms_kernel(
    where, own_exps, other_exps, q_own, q_other, positives, coef,
    right, left, term_left, term_right, w_own, w_other, *_,
):
    rows = FAR_BLOCKS + BLOCKS[1:3]
    weigh(where, rows, own_exps, positives, coef, 0, w_own)
    weigh(where, rows, other_exps, positives, coef, 4, w_other)
    for j in range(4):
        at = slice(j * 256, (j + 1) * 256)
        g = scaled_terms(w_own, w_other, q_own, q_other, coef[0:1, 768:769], at)
        right[:, at] = encode(g[:64])
        left[:, at] = encode(g[64:128])
        term_left[:, at] = g[128:256]
        term_right[:, at] = g[256:]


def other_terms_kernel(
    where, own_exps, other_exps, q_own, q_other, positives, coef, *outs
):
    grads, (w_own, w_other) = outs[:5], outs[5:]
    rows = [BLOCKS[0], *BLOCKS[3:]]
    weigh(where, rows, own_exps, positives, coef, 0, w_own)
    weigh(where, rows, other_exps, positives, coef, 4, w_other)
    for j in range(4):
        at = slice(j * 256, (j + 1) * 256)
        g = scaled_terms(w_own, w_other, q_own, q_other, coef[0:1, 768:769], at)
        for i, ref in enumerate(grads):
            ref[:, at] = g[i * 128 : (i + 1) * 128]


def add_halves_kernel(from_left, from_right, term_left, term_right, other0, other1, right, left, *_):
    right[:64, :] = encode(term_right[:64, :] + decode(from_left[...]))
    right[64:, :] = encode(term_right[64:, :])
    left[:64, :] = encode(term_left[:64, :])
    left[64:, :] = encode(term_left[64:, :] + decode(from_right[...]))


def add_kernel(received, term, *refs):
    out = refs[-1]
    out[...] = encode(term[...] + decode(received[...]))


def last_add_kernel(coef, from_left, from_right, term, out):
    out[...] = (term[...] + (decode(from_left[...]) + decode(from_right[...]))) * coef[1:2, 768:769]


GROUPS = ((1, 0, 128), (0, 128, 384), (1, 128, 640), (0, 0, 128))


def query_terms(own, where, passages, coef, weights, i):
    _, second = axes_of(where, where[3] if own else 1 - where[3])
    at = pl.ds(pl.multiple_of(lax.rem(second + i, 4) * 256, 256), 256)
    w = jnp.concatenate([weights[k][u:v, at] for k, u, v in GROUPS], axis=0)
    g = lax.dot_general(w, passages[...], (((0,), (0,)), ((), ())), preferred_element_type=F32)
    return g * coef[2:3, 768:769]


def row_of(where, b):
    first, _ = axes_of(where, where[3])
    return pl.ds(pl.multiple_of(lax.rem(b - first + 4, 4) * 64, 64), 64)


def send_queries_kernel(where, passages, coef, w0, w1, out0, out1):
    for i in range(4):
        g = encode(query_terms(False, where, passages, coef, (w0, w1), i))
        (out0, out1)[i // 2][i % 2 * 256 : (i % 2 + 1) * 256, :] = g


def keep_queries_kernel(where, passages, coef, w0, w1, other0, other1, keep, *sent):
    for i, ref in enumerate((keep, *sent)):
        g = query_terms(True, where, passages, coef, (w0, w1), i)
        g += decode((other0, other1)[i // 2][i % 2 * 256 : (i % 2 + 1) * 256, :])
        g = g if i == 0 else encode(g)
        for b in range(4):
            ref[row_of(where, b), :] = g[b * 64 : (b + 1) * 64, :]


def add_queries_kernel(own, a, b, c, keep, *sent):
    total = (own[...] + decode(b[...])) + (decode(a[...]) + decode(c[...]))
    keep[...] = total[:64, :]
    for i, ref in enumerate(sent):
        ref[...] = encode(total[(i + 1) * 64 : (i + 2) * 64, :])


def last_queries_kernel(coef, own, a, b, c, out):
    total = (own[...] + decode(b[...])) + (decode(a[...]) + decode(c[...]))
    out[...] = total * coef[3:4, 768:769]


def body(queries, passages, positives):
    x, y, z, c = (lax.axis_index(a) for a in ("x", "y", "z", "core"))
    where = jnp.stack([x, y, z, c]).astype(jnp.int32)
    bf = lambda n: ((n, D), BF)
    f32 = lambda n: ((n, D), F32)

    (packed,) = call(pack_passages_kernel, "pack_passages", [bf(144)], (passages, queries))
    z1r, z1l = shift_z(packed, 1), shift_z(packed, -1)
    z2r, z2l = shift_z(z1r, 1), shift_z(z1l, -1)
    z3r, z3l = shift_z(z2r, 1), shift_z(z2l, -1)
    far0, far1 = call(cut_kernel, "cut", [bf(80)] * 2, (z3r, z3l))
    far0, far1 = shift_z(far0, 1), shift_z(far1, -1)
    args = (where, queries, positives.reshape(4, 128))
    (q,) = call(pack_queries_kernel, "pack_queries", [bf(80)], args, smem=1)
    (q,) = call(round1_kernel, "round1", [bf(272)], (q, *(shift_plane(q, 0, k) for k in (1, -1, 2))))
    q_right, q_left = shift_plane(q, 1, 1), shift_plane(q, 1, -1)
    q_right2, q_left2 = call(round2_kernel, "round2", [bf(144)] * 2, (q_right, q_left, z3r, z3l))
    q_right2, q_left2 = shift_plane(q_right2, 1, 1), shift_plane(q_left2, 1, -1)
    args = (where, q, q_right, q_left, q_right2, q_left2, far0, far1)
    outs = [bf(1024), ((8, 256), jnp.int32)]
    scratch = [pltpu.VMEM((16, 128), jnp.int32)]
    q_own, pos_own = call(round3_kernel, "round3", outs, args, scratch=scratch, smem=1)
    q_other, pos_other = swap_core(q_own), swap_core(pos_own)

    raws = [pltpu.VMEM((1024, 256), F32)] * 2
    outs = [((1024, 1024), F32), ((8, 896), F32), bf(1024)]
    args = (where, q_own, pos_own, packed, z3r, z3l, z2r, z2l, z1r, z1l, far0, far1)
    own_exps, stats, p_all = call(own_scores_kernel, "own_scores", outs, args, scratch=raws, mib=16, smem=1)
    outs = [((1024, 1024), F32), ((8, 896), F32), ((8, 256), jnp.int32)]
    args = (where, q_other, pos_own, pos_other, p_all, stats)
    other_exps, stats, pos = call(other_scores_kernel, "other_scores", outs, args, scratch=raws, mib=16, smem=1)
    local = stats

    for shift in (shift_x, shift_y):
        args = [stats] + [shift(stats, k) for k in (1, -1, 2)]
        (stats,) = call(merge_kernel, "merge", [((8, 896), F32)], args)
    (coef,) = call(finish_kernel, "finish", [((8, 896), F32)], (local, stats, swap_core(stats)))

    args = (where, own_exps, other_exps, q_own, q_other, pos, coef)
    outs = [bf(64), bf(64), f32(128), f32(128), bf(384), bf(384), ((8, 896), F32)]
    right, left, left3, right3, w0_own, w0_other, coef = call(
        first_terms_kernel, "first_terms", outs, args, mib=16, smem=1, alias={6: 6}
    )
    losses, done = call(losses_kernel, "losses", [((4, 128), F32), ((8, 128), F32)], (where, coef), smem=1)
    right, left = shift_z(right, 1), shift_z(left, -1)
    args = (where, own_exps, other_exps, q_own, q_other, pos, coef)
    outs = [f32(128)] * 5 + [bf(640)] * 2
    own, left2, right2, left1, right1, w1_own, w1_other = call(
        other_terms_kernel, "other_terms", outs, args, mib=16, smem=1
    )
    args = (where, p_all, coef, w0_other, w1_other)
    other0, other1 = call(send_queries_kernel, "send_queries", [bf(512)] * 2, args, mib=16, smem=1)
    args = (right, left, left3, right3, other0, other1)
    outs = [bf(128)] * 2 + [bf(512)] * 2
    right, left, other0, other1 = call(add_halves_kernel, "add_halves", outs, args, alias={4: 2, 5: 3})
    right, left = shift_z(right, 1), shift_z(left, -1)
    for to_right, to_left, before in ((right2, left2, ()), (right1, left1, (done,))):
        (right,) = call(add_kernel, "add_right", [bf(128)], (right, to_right, *before))
        right = shift_z(right, 1)
        (left,) = call(add_kernel, "add_left", [bf(128)], (left, to_left))
        left = shift_z(left, -1)
    (passage_grad,) = call(last_add_kernel, "last_add", [f32(128)], (coef, right, left, own))

    args = (where, p_all, coef, w0_own, w1_own, swap_core(other0), swap_core(other1))
    outs = [f32(256)] + [bf(256)] * 3
    keep, *sent = call(keep_queries_kernel, "keep_queries", outs, args, mib=16, smem=1)
    moved = [shift_plane(v, 1, k + 1) for k, v in enumerate(sent)]
    outs = [f32(64)] + [bf(64)] * 3
    keep, *sent = call(add_queries_kernel, "add_queries", outs, (keep, *moved))
    moved = [shift_plane(v, 0, k + 1) for k, v in enumerate(sent)]
    (query_grad,) = call(last_queries_kernel, "last_queries", [f32(64)], (coef, keep, *moved))
    return losses.reshape(512), query_grad, passage_grad


def solution(mesh):
    mesh = Mesh(mesh.devices.reshape(Y, Z, X, C), ("y", "z", "x", "core"))
    q_spec = P(("y", "z", "x", "core"), None)
    p_spec = P(("x", "core", "y", "z"), None)
    row_spec = P(("y", "z"))
    return jax.shard_map(
        body,
        mesh=mesh,
        in_specs=(q_spec, p_spec, row_spec),
        out_specs=(row_spec, q_spec, p_spec),
        check_vma=False,
    )
```

```python
import functools
import math

import jax
import jax.numpy as jnp
from jax import lax
from jax.experimental import pallas as pl
from jax.experimental.pallas import tpu as pltpu
from jax.sharding import Mesh, PartitionSpec as P

D = 1024
NQ = 16384
SCALE = 3.0 / math.sqrt(D)
TO_EXP2 = SCALE * math.log2(math.e)
X, Y, Z, C = 4, 4, 8, 2
PLANE = ("y", "x", "core")
BF, F32 = jnp.bfloat16, jnp.float32
MIB = 1 << 20
LARGEST = 46000.0
NEAR = ((0, 0, 128), (-3, 0, 128), (3, 0, 128), (-2, 0, 128), (2, 0, 128), (-1, 0, 128), (1, 0, 128))
FAR = ((4, 0, 64), (4, 64, 64))
N_NEAR, N_FAR = 896, 128
TILE = 16
VMEM = pl.BlockSpec(memory_space=pltpu.VMEM)
SMEM = pl.BlockSpec(memory_space=pltpu.SMEM)


def call(kernel, name, outs, args, scratch=(), mib=8, smem=0, alias=None):
    return pl.pallas_call(
        kernel,
        out_shape=[jax.ShapeDtypeStruct(s, t) for s, t in outs],
        in_specs=[SMEM] * smem + [VMEM] * (len(args) - smem),
        out_specs=[VMEM] * len(outs),
        scratch_shapes=list(scratch),
        input_output_aliases=alias or {},
        compiler_params=pltpu.CompilerParams(vmem_limit_bytes=mib * MIB),
        cost_estimate=pl.CostEstimate(flops=1000, bytes_accessed=1024, transcendentals=0),
        name=name,
    )(*args)


def shift_z(v, k):
    return lax.ppermute(v, "z", [(i, (i + k) % Z) for i in range(Z)])


def shift_x(v, k):
    return lax.ppermute(v, "x", [(i, (i + k) % X) for i in range(X)])


def shift_y(v, k):
    return lax.ppermute(v, "y", [(i, (i + k) % Y) for i in range(Y)])


def swap_core(v):
    return lax.ppermute(v, "core", [(0, 1), (1, 0)])


def shift_plane(v, stage, k):
    pairs = []
    for y in range(Y):
        for x in range(X):
            for c in range(C):
                y2, x2 = (y, (x + k) % X) if c == stage else ((y + k) % Y, x)
                pairs.append(((y * X + x) * C + c, (y2 * X + x2) * C + c))
    return lax.ppermute(v, PLANE, pairs)


def encode(v):
    v2 = v * v
    v4 = v2 * v2
    v8 = v4 * v4
    return jnp.where(v < 0, -v8, v8).astype(BF)


def decode(code):
    y = code.astype(F32)
    size = jnp.abs(y)
    v = jnp.exp2(jnp.log2(jnp.maximum(size, 1e-37)) * 0.125)
    v = jnp.where(size < 1e-37, 0.0, v)
    return jnp.where(y < 0, -v, v)


def axes_of(where, c):
    x, y = where[0], where[1]
    return jnp.where(c == 0, x, y), jnp.where(c == 0, y, x)


def largest(v):
    v = jnp.max(jnp.abs(v).astype(F32), axis=0, keepdims=True)
    return jnp.max(v, axis=1, keepdims=True)


def rows_like(tile):
    return lax.broadcasted_iota(jnp.int32, tile.shape, 0)


def pack_passages_kernel(passages, queries, out):
    out[:128, :] = passages[...]
    out[128:, :] = jnp.broadcast_to(largest(queries[...]), (TILE, D)).astype(BF)


def pack_queries_kernel(where, queries, positives, out):
    out[:64, :] = queries[...]
    out[64:, :] = jnp.zeros((TILE, D), BF)
    pos = positives[pl.ds(where[0], 1), :]
    pos = jnp.where(where[3] == 0, pos, jnp.concatenate([pos[:, 64:], pos[:, :64]], axis=1))
    tile = jnp.zeros((TILE, 128), F32)
    for i, part in enumerate((lax.shift_right_logical(pos, 8), jnp.bitwise_and(pos, 255))):
        tile = jnp.where(rows_like(tile) == i, part.astype(F32), tile)
    out[64:, :128] = tile.astype(BF)


def round1_kernel(q0, q1, q2, q3, out):
    tile = jnp.zeros((TILE, 128), F32)
    for i, ref in enumerate((q0, q1, q2, q3)):
        out[i * 64 : (i + 1) * 64, :] = ref[:64, :]
        part = ref[64:, :128].astype(F32)
        tile = jnp.where(rows_like(tile) == i, part[0:1, :], tile)
        tile = jnp.where(rows_like(tile) == 4 + i, part[1:2, :], tile)
    out[256:, :] = jnp.zeros((TILE, D), BF)
    out[256:, :128] = tile.astype(BF)


def cut_kernel(z_right, z_left, far_right, far_left):
    far_right[:64, :] = z_right[:64, :]
    far_right[64:, :] = z_right[128:, :]
    far_left[...] = z_left[64:, :]


def round2_kernel(q_right, q_left, z_right, z_left, right, left):
    right[:128, :] = q_right[:128, :]
    right[128:, :] = q_right[256:, :]
    left[...] = q_left[128:, :]


def round3_kernel(where, own, right, left, right2, left2, far0, far1, out, positives, scratch):
    first, second = axes_of(where, where[3])
    for i, (ref, part, n) in enumerate(((own, 0, 4), (right, 0, 4), (left, 0, 4), (right2, 0, 2), (left2, 2, 2))):
        a = lax.rem(second + (0, 3, 1, 2, 2)[i], 4)
        tile = ref[n * 64 :, :128].astype(F32)
        for j in range(part, part + n):
            b = lax.rem(first + (0, 3, 1, 2)[j], 4)
            at = pl.ds(pl.multiple_of((a * 4 + b) * 64, 64), 64)
            out[at, :] = ref[(j - part) * 64 : (j - part + 1) * 64, :]
            pos = tile[j : j + 1, :] * 256.0 + tile[4 + j : 5 + j, :]
            scratch[pl.ds(a * 4 + b, 1), :] = pos.astype(jnp.int32)
    positives[...] = jnp.zeros((8, 256), jnp.int32)
    for a in range(4):
        for b in range(4):
            positives[a : a + 1, b * 64 : b * 64 + 64] = scratch[a * 4 + b : a * 4 + b + 1, :64]


def losses_kernel(where, coef, out, done):
    done[...] = jnp.zeros((8, 128), F32)
    y, c = where[1], where[3]
    v = coef[:, 512:768]
    core0, core1 = jnp.where(c == 0, v[:4], v[4:]), jnp.where(c == 0, v[4:], v[:4])
    for x in range(4):
        a, b = core0[0:1, x * 64 : x * 64 + 64], core1[x : x + 1, :64]
        for k in range(1, 4):
            a = jnp.where(y == k, core0[k : k + 1, x * 64 : x * 64 + 64], a)
            b = jnp.where(y == k, core1[x : x + 1, k * 64 : k * 64 + 64], b)
        out[x : x + 1, :64] = a
        out[x : x + 1, 64:] = b


def first_passage(where, offset):
    x, y, z, c = where[0], where[1], where[2], where[3]
    return (((x * C + c) * Y + y) * Z + lax.rem(z + offset + Z, Z)) * 128


def softmax(where, rows, raw, positives, exps, at):
    top = jnp.max(raw[...], axis=0, keepdims=True)
    total = jnp.zeros_like(top)
    pos_score = jnp.zeros_like(top)
    row = 0
    for offset, start, n in rows:
        part = raw[row : row + n, :]
        e = jnp.exp2((part - top) * TO_EXP2)
        exps[row : row + n, at] = e
        total += jnp.sum(e, axis=0, keepdims=True)
        hit = lax.broadcasted_iota(jnp.int32, part.shape, 0) == positives - (first_passage(where, offset) + start)
        pos_score += jnp.sum(jnp.where(hit, part, 0.0), axis=0, keepdims=True)
        row += n
    return top * SCALE, total, pos_score * SCALE


def product(p, q):
    return lax.dot_general(p, q, (((1,), (1,)), ((), ())), preferred_element_type=F32)


def score_blocks(where, q, passages, positives, first, raws, exps, stats):
    raws[0][...] = product(passages[...], q[0:256, :])
    for i in range(4):
        if i < 3:
            raws[(i + 1) % 2][...] = product(passages[...], q[(i + 1) * 256 : (i + 2) * 256, :])
        at, row = slice(i * 256, (i + 1) * 256), slice(first + i, first + i + 1)
        top, total, pos_score = softmax(where, NEAR + FAR, raws[i % 2], positives[row, :], exps, at)
        stats[row, 0:256] = top
        stats[row, 256:512] = total
        stats[row, 512:768] = pos_score


def own_scores_kernel(where, q, positives, *refs):
    pieces, (exps, stats, passages, *raws) = refs[: len(NEAR) + 2], refs[len(NEAR) + 2 :]
    largest_q, row = None, 0
    for ref in pieces:
        n = ref.shape[0] - TILE
        passages[row : row + n, :] = ref[:n, :]
        v = ref[n : n + 1, :128].astype(F32)
        largest_q = v if largest_q is None else jnp.maximum(largest_q, v)
        row += n
    stats[0:4, 768:] = jnp.broadcast_to(largest_q, (4, 128))
    stats[4:8, 768:] = jnp.broadcast_to(largest(passages[...]), (4, 128))
    score_blocks(where, q, passages, positives, 0, raws, exps, stats)


def other_scores_kernel(where, q, pos_own, pos_other, passages, own_stats, exps, stats, positives, *raws):
    positives[:4, :] = pos_own[:4, :]
    positives[4:, :] = pos_other[:4, :]
    stats[0:4, :] = own_stats[0:4, :]
    stats[4:8, 768:] = own_stats[4:8, 768:]
    score_blocks(where, q, passages, positives, 4, raws, exps, stats)


def merge_stats(parts):
    top = functools.reduce(jnp.maximum, [p[:, 0:256] for p in parts])
    totals = [p[:, 256:512] * jnp.exp(p[:, 0:256] - top) for p in parts]
    pos_scores = [p[:, 512:768] for p in parts]
    if len(parts) == 4:
        join = lambda v: (v[0] + v[3]) + (v[1] + v[2])
    else:
        join = lambda v: v[0] + v[1]
    rest = functools.reduce(jnp.maximum, [p[:, 768:] for p in parts])
    return top, join(totals), join(pos_scores), rest


def merge_kernel(*refs):
    out = refs[-1]
    top, total, pos_score, rest = merge_stats([r[...] for r in refs[:-1]])
    out[:, 0:256] = top
    out[:, 256:512] = total
    out[:, 512:768] = pos_score
    out[:, 768:] = rest


def finish_kernel(local, one, two, out):
    two = jnp.concatenate(
        [jnp.concatenate([two[4:8, :768], two[0:4, :768]], axis=0), two[:, 768:]], axis=1
    )
    top, total, pos_score, rest = merge_stats([one[...], two])
    lse = top + jnp.log(total)
    out[:, 0:256] = jnp.exp(local[:, 0:256] - lse)
    out[:, 256:512] = jnp.zeros_like(lse)
    out[:, 512:768] = lse - pos_score
    bound_p = (NQ * SCALE) * jnp.maximum(rest[0:1, :], 1e-30)
    bound_q = (2.0 * SCALE) * jnp.maximum(rest[4:5, :], 1e-30)
    out[0:1, 768:] = LARGEST / bound_p
    out[1:2, 768:] = bound_p / LARGEST
    out[2:3, 768:] = LARGEST / bound_q
    out[3:4, 768:] = bound_q / LARGEST
    out[4:8, 768:] = jnp.zeros((4, 128), F32)


def weigh(where, rows, exps, positives, coef, first, weights):
    for i in range(4):
        at = slice(i * 256, (i + 1) * 256)
        factor = coef[first + i : first + i + 1, 0:256]
        pos = positives[first + i : first + i + 1, :]
        row = 0
        for offset, start, n, r in rows:
            hit = lax.broadcasted_iota(jnp.int32, (n, 256), 0) == pos - (first_passage(where, offset) + start)
            weights[row : row + n, at] = ((exps[r : r + n, at] * factor - hit.astype(F32)) * SCALE).astype(BF)
            row += n


def scaled_terms(w_own, w_other, q_own, q_other, scale, at):
    g = jnp.dot(w_own[...], q_own[:, at], preferred_element_type=F32)
    return (g + jnp.dot(w_other[...], q_other[:, at], preferred_element_type=F32)) * scale


BLOCKS = [(o, s, n, 128 * i) for i, (o, s, n) in enumerate(NEAR)]
FAR_BLOCKS = [(o, s, n, N_NEAR + s) for o, s, n in FAR]


def first_terms_kernel(
    where, own_exps, other_exps, q_own, q_other, positives, coef,
    right, left, term_right, w_own, w_other, *_,
):
    rows = FAR_BLOCKS + BLOCKS[1:3]
    weigh(where, rows, own_exps, positives, coef, 0, w_own)
    weigh(where, rows, other_exps, positives, coef, 4, w_other)
    for j in range(4):
        at = slice(j * 256, (j + 1) * 256)
        g = scaled_terms(w_own, w_other, q_own, q_other, coef[0:1, 768:769], at)
        right[:, at] = encode(g[:128])
        left[:, at] = encode(g[128:256])
        term_right[:, at] = g[256:]


def other_terms_kernel(
    where, own_exps, other_exps, q_own, q_other, positives, coef, *outs
):
    grads, (w_own, w_other) = outs[:5], outs[5:]
    rows = [BLOCKS[0], *BLOCKS[3:]]
    weigh(where, rows, own_exps, positives, coef, 0, w_own)
    weigh(where, rows, other_exps, positives, coef, 4, w_other)
    for j in range(4):
        at = slice(j * 256, (j + 1) * 256)
        g = scaled_terms(w_own, w_other, q_own, q_other, coef[0:1, 768:769], at)
        for i, ref in enumerate(grads):
            ref[:, at] = g[i * 128 : (i + 1) * 128]


def add_both_kernel(from_left, from_right, term_right, term_left, other0, other1, right, left, *_):
    right[...] = encode(term_right[...] + decode(from_left[...]))
    left[...] = encode(term_left[...] + decode(from_right[...]))


def add_kernel(received, term, *refs):
    out = refs[-1]
    out[...] = encode(term[...] + decode(received[...]))


def last_add_kernel(coef, from_left, from_right, term, out):
    out[...] = (term[...] + (decode(from_left[...]) + decode(from_right[...]))) * coef[1:2, 768:769]


GROUPS = ((1, 0, 128), (0, 128, 384), (1, 128, 640), (0, 0, 128))


def query_terms(own, where, passages, coef, w0, w1, w):
    _, second = axes_of(where, where[3] if own else 1 - where[3])
    for i in range(4):
        at = pl.ds(pl.multiple_of(lax.rem(second + i, 4) * 256, 256), 256)
        row = 0
        for k, u, v in GROUPS:
            w[row : row + v - u, i * 256 : (i + 1) * 256] = (w0, w1)[k][u:v, at]
            row += v - u
    g = lax.dot_general(w[...], passages[...], (((0,), (0,)), ((), ())), preferred_element_type=F32)
    return g * coef[2:3, 768:769]


def row_of(where, b):
    first, _ = axes_of(where, where[3])
    return pl.ds(pl.multiple_of(lax.rem(b - first + 4, 4) * 64, 64), 64)


def send_queries_kernel(where, passages, coef, w0, w1, out0, out1, w):
    g = encode(query_terms(False, where, passages, coef, w0, w1, w))
    out0[...] = g[:512, :]
    out1[...] = g[512:, :]


def keep_queries_kernel(where, passages, coef, w0, w1, other0, other1, keep, *refs):
    sent, w = refs[:-1], refs[-1]
    terms = query_terms(True, where, passages, coef, w0, w1, w)
    for i, ref in enumerate((keep, *sent)):
        g = terms[i * 256 : (i + 1) * 256, :] + decode((other0, other1)[i // 2][i % 2 * 256 : (i % 2 + 1) * 256, :])
        g = g if i == 0 else encode(g)
        for b in range(4):
            ref[row_of(where, b), :] = g[b * 64 : (b + 1) * 64, :]


def add_queries_kernel(own, a, b, c, keep, *sent):
    total = (own[...] + decode(b[...])) + (decode(a[...]) + decode(c[...]))
    keep[...] = total[:64, :]
    for i, ref in enumerate(sent):
        ref[...] = encode(total[(i + 1) * 64 : (i + 2) * 64, :])


def last_queries_kernel(coef, own, a, b, c, out):
    total = (own[...] + decode(b[...])) + (decode(a[...]) + decode(c[...]))
    out[...] = total * coef[3:4, 768:769]


def body(queries, passages, positives):
    x, y, z, c = (lax.axis_index(a) for a in ("x", "y", "z", "core"))
    where = jnp.stack([x, y, z, c]).astype(jnp.int32)
    bf = lambda n: ((n, D), BF)
    f32 = lambda n: ((n, D), F32)

    (packed,) = call(pack_passages_kernel, "pack_passages", [bf(144)], (passages, queries))
    z1r, z1l = shift_z(packed, 1), shift_z(packed, -1)
    z2r, z2l = shift_z(z1r, 1), shift_z(z1l, -1)
    z3r, z3l = shift_z(z2r, 1), shift_z(z2l, -1)
    far0, far1 = call(cut_kernel, "cut", [bf(80)] * 2, (z3r, z3l))
    far0, far1 = shift_z(far0, 1), shift_z(far1, -1)
    args = (where, queries, positives.reshape(4, 128))
    (q,) = call(pack_queries_kernel, "pack_queries", [bf(80)], args, smem=1)
    (q,) = call(round1_kernel, "round1", [bf(272)], (q, *(shift_plane(q, 0, k) for k in (1, -1, 2))))
    q_right, q_left = shift_plane(q, 1, 1), shift_plane(q, 1, -1)
    q_right2, q_left2 = call(round2_kernel, "round2", [bf(144)] * 2, (q_right, q_left, z3r, z3l))
    q_right2, q_left2 = shift_plane(q_right2, 1, 1), shift_plane(q_left2, 1, -1)
    args = (where, q, q_right, q_left, q_right2, q_left2, far0, far1)
    outs = [bf(1024), ((8, 256), jnp.int32)]
    scratch = [pltpu.VMEM((16, 128), jnp.int32)]
    q_own, pos_own = call(round3_kernel, "round3", outs, args, scratch=scratch, smem=1)
    q_other, pos_other = swap_core(q_own), swap_core(pos_own)

    raws = [pltpu.VMEM((1024, 256), F32)] * 2
    outs = [((1024, 1024), F32), ((8, 896), F32), bf(1024)]
    args = (where, q_own, pos_own, packed, z3r, z3l, z2r, z2l, z1r, z1l, far0, far1)
    own_exps, stats, p_all = call(own_scores_kernel, "own_scores", outs, args, scratch=raws, mib=16, smem=1)
    outs = [((1024, 1024), F32), ((8, 896), F32), ((8, 256), jnp.int32)]
    args = (where, q_other, pos_own, pos_other, p_all, stats)
    other_exps, stats, pos = call(other_scores_kernel, "other_scores", outs, args, scratch=raws, mib=16, smem=1)
    local = stats

    for shift in (shift_x, shift_y):
        args = [stats] + [shift(stats, k) for k in (1, -1, 2)]
        (stats,) = call(merge_kernel, "merge", [((8, 896), F32)], args)
    (coef,) = call(finish_kernel, "finish", [((8, 896), F32)], (local, stats, swap_core(stats)))

    args = (where, own_exps, other_exps, q_own, q_other, pos, coef)
    outs = [bf(128), bf(128), f32(128), bf(384), bf(384), ((8, 896), F32)]
    right, left, right3, w0_own, w0_other, coef = call(
        first_terms_kernel, "first_terms", outs, args, mib=16, smem=1, alias={6: 5}
    )
    losses, done = call(losses_kernel, "losses", [((4, 128), F32), ((8, 128), F32)], (where, coef), smem=1)
    right, left = shift_z(right, 1), shift_z(left, -1)
    args = (where, own_exps, other_exps, q_own, q_other, pos, coef)
    outs = [f32(128)] * 5 + [bf(640)] * 2
    own, left2, right2, left1, right1, w1_own, w1_other = call(
        other_terms_kernel, "other_terms", outs, args, mib=16, smem=1
    )
    args = (where, p_all, coef, w0_other, w1_other)
    other0, other1 = call(
        send_queries_kernel, "send_queries", [bf(512)] * 2, args, scratch=[pltpu.VMEM((1024, 1024), BF)], mib=20, smem=1
    )
    args = (right, left, right3, left2, other0, other1)
    outs = [bf(128)] * 2 + [bf(512)] * 2
    right, left, other0, other1 = call(add_both_kernel, "add_both", outs, args, alias={4: 2, 5: 3})
    right, left = shift_z(right, 1), shift_z(left, -1)
    (right,) = call(add_kernel, "add_right", [bf(128)], (right, right2))
    right = shift_z(right, 1)
    (left,) = call(add_kernel, "add_left", [bf(128)], (left, left1))
    left = shift_z(left, -1)
    (right,) = call(add_kernel, "add_right", [bf(128)], (right, right1, done))
    right = shift_z(right, 1)
    (passage_grad,) = call(last_add_kernel, "last_add", [f32(128)], (coef, right, left, own))

    args = (where, p_all, coef, w0_own, w1_own, swap_core(other0), swap_core(other1))
    outs = [f32(256)] + [bf(256)] * 3
    keep, *sent = call(
        keep_queries_kernel, "keep_queries", outs, args, scratch=[pltpu.VMEM((1024, 1024), BF)], mib=20, smem=1
    )
    moved = [shift_plane(v, 1, k + 1) for k, v in enumerate(sent)]
    outs = [f32(64)] + [bf(64)] * 3
    keep, *sent = call(add_queries_kernel, "add_queries", outs, (keep, *moved))
    moved = [shift_plane(v, 0, k + 1) for k, v in enumerate(sent)]
    (query_grad,) = call(last_queries_kernel, "last_queries", [f32(64)], (coef, keep, *moved))
    return losses.reshape(512), query_grad, passage_grad


def solution(mesh):
    mesh = Mesh(mesh.devices.reshape(Y, Z, X, C), ("y", "z", "x", "core"))
    q_spec = P(("y", "z", "x", "core"), None)
    p_spec = P(("x", "core", "y", "z"), None)
    row_spec = P(("y", "z"))
    return jax.shard_map(
        body,
        mesh=mesh,
        in_specs=(q_spec, p_spec, row_spec),
        out_specs=(row_spec, q_spec, p_spec),
        check_vma=False,
    )
```

```python
import functools
import math

import jax
import jax.numpy as jnp
from jax import lax
from jax.experimental import pallas as pl
from jax.experimental.pallas import tpu as pltpu
from jax.sharding import Mesh, PartitionSpec as P

D = 1024
NQ = 16384
SCALE = 3.0 / math.sqrt(D)
TO_EXP2 = SCALE * math.log2(math.e)
X, Y, Z, C = 4, 4, 8, 2
PLANE = ("y", "x", "core")
BF, F32 = jnp.bfloat16, jnp.float32
MIB = 1 << 20
LARGEST = 46000.0
NEAR = ((0, 0, 128), (-3, 0, 128), (3, 0, 128), (-2, 0, 128), (2, 0, 128), (-1, 0, 128), (1, 0, 128))
FAR = ((4, 0, 64), (4, 64, 64))
N_NEAR, N_FAR = 896, 128
TILE = 16
VMEM = pl.BlockSpec(memory_space=pltpu.VMEM)
SMEM = pl.BlockSpec(memory_space=pltpu.SMEM)


def call(kernel, name, outs, args, scratch=(), mib=8, smem=0, alias=None):
    return pl.pallas_call(
        kernel,
        out_shape=[jax.ShapeDtypeStruct(s, t) for s, t in outs],
        in_specs=[SMEM] * smem + [VMEM] * (len(args) - smem),
        out_specs=[VMEM] * len(outs),
        scratch_shapes=list(scratch),
        input_output_aliases=alias or {},
        compiler_params=pltpu.CompilerParams(vmem_limit_bytes=mib * MIB),
        cost_estimate=pl.CostEstimate(flops=1000, bytes_accessed=1024, transcendentals=0),
        name=name,
    )(*args)


def shift_z(v, k):
    return lax.ppermute(v, "z", [(i, (i + k) % Z) for i in range(Z)])


def shift_x(v, k):
    return lax.ppermute(v, "x", [(i, (i + k) % X) for i in range(X)])


def shift_y(v, k):
    return lax.ppermute(v, "y", [(i, (i + k) % Y) for i in range(Y)])


def swap_core(v):
    return lax.ppermute(v, "core", [(0, 1), (1, 0)])


def shift_plane(v, stage, k):
    pairs = []
    for y in range(Y):
        for x in range(X):
            for c in range(C):
                y2, x2 = (y, (x + k) % X) if c == stage else ((y + k) % Y, x)
                pairs.append(((y * X + x) * C + c, (y2 * X + x2) * C + c))
    return lax.ppermute(v, PLANE, pairs)


def encode(v):
    v2 = v * v
    v4 = v2 * v2
    v8 = v4 * v4
    return jnp.where(v < 0, -v8, v8).astype(BF)


def decode(code):
    y = code.astype(F32)
    size = jnp.abs(y)
    v = jnp.exp2(jnp.log2(jnp.maximum(size, 1e-37)) * 0.125)
    v = jnp.where(size < 1e-37, 0.0, v)
    return jnp.where(y < 0, -v, v)


def axes_of(where, c):
    x, y = where[0], where[1]
    return jnp.where(c == 0, x, y), jnp.where(c == 0, y, x)


def largest(v):
    v = jnp.max(jnp.abs(v).astype(F32), axis=0, keepdims=True)
    return jnp.max(v, axis=1, keepdims=True)


def rows_like(tile):
    return lax.broadcasted_iota(jnp.int32, tile.shape, 0)


def pack_passages_kernel(passages, queries, out):
    out[:128, :] = passages[...]
    out[128:, :] = jnp.broadcast_to(largest(queries[...]), (TILE, D)).astype(BF)


def pack_queries_kernel(where, queries, positives, out):
    out[:64, :] = queries[...]
    out[64:, :] = jnp.zeros((TILE, D), BF)
    pos = positives[pl.ds(where[0], 1), :]
    pos = jnp.where(where[3] == 0, pos, jnp.concatenate([pos[:, 64:], pos[:, :64]], axis=1))
    tile = jnp.zeros((TILE, 128), F32)
    for i, part in enumerate((lax.shift_right_logical(pos, 8), jnp.bitwise_and(pos, 255))):
        tile = jnp.where(rows_like(tile) == i, part.astype(F32), tile)
    out[64:, :128] = tile.astype(BF)


def round1_kernel(q0, q1, q2, q3, out):
    tile = jnp.zeros((TILE, 128), F32)
    for i, ref in enumerate((q0, q1, q2, q3)):
        out[i * 64 : (i + 1) * 64, :] = ref[:64, :]
        part = ref[64:, :128].astype(F32)
        tile = jnp.where(rows_like(tile) == i, part[0:1, :], tile)
        tile = jnp.where(rows_like(tile) == 4 + i, part[1:2, :], tile)
    out[256:, :] = jnp.zeros((TILE, D), BF)
    out[256:, :128] = tile.astype(BF)


def cut_kernel(z_right, z_left, far_right, far_left):
    far_right[:64, :] = z_right[:64, :]
    far_right[64:, :] = z_right[128:, :]
    far_left[...] = z_left[64:, :]


def round2_kernel(q_right, q_left, z_right, z_left, right, left):
    right[:128, :] = q_right[:128, :]
    right[128:, :] = q_right[256:, :]
    left[...] = q_left[128:, :]


def round3_kernel(where, own, right, left, right2, left2, far0, far1, out, positives, scratch):
    first, second = axes_of(where, where[3])
    for i, (ref, part, n) in enumerate(((own, 0, 4), (right, 0, 4), (left, 0, 4), (right2, 0, 2), (left2, 2, 2))):
        a = lax.rem(second + (0, 3, 1, 2, 2)[i], 4)
        tile = ref[n * 64 :, :128].astype(F32)
        for j in range(part, part + n):
            b = lax.rem(first + (0, 3, 1, 2)[j], 4)
            at = pl.ds(pl.multiple_of((a * 4 + b) * 64, 64), 64)
            out[at, :] = ref[(j - part) * 64 : (j - part + 1) * 64, :]
            pos = tile[j : j + 1, :] * 256.0 + tile[4 + j : 5 + j, :]
            scratch[pl.ds(a * 4 + b, 1), :] = pos.astype(jnp.int32)
    positives[...] = jnp.zeros((8, 256), jnp.int32)
    for a in range(4):
        for b in range(4):
            positives[a : a + 1, b * 64 : b * 64 + 64] = scratch[a * 4 + b : a * 4 + b + 1, :64]


def losses_kernel(where, coef, out, done):
    done[...] = jnp.zeros((8, 128), F32)
    y, c = where[1], where[3]
    v = coef[:, 512:768]
    core0, core1 = jnp.where(c == 0, v[:4], v[4:]), jnp.where(c == 0, v[4:], v[:4])
    for x in range(4):
        a, b = core0[0:1, x * 64 : x * 64 + 64], core1[x : x + 1, :64]
        for k in range(1, 4):
            a = jnp.where(y == k, core0[k : k + 1, x * 64 : x * 64 + 64], a)
            b = jnp.where(y == k, core1[x : x + 1, k * 64 : k * 64 + 64], b)
        out[x : x + 1, :64] = a
        out[x : x + 1, 64:] = b


def first_passage(where, offset):
    x, y, z, c = where[0], where[1], where[2], where[3]
    return (((x * C + c) * Y + y) * Z + lax.rem(z + offset + Z, Z)) * 128


def softmax(where, rows, raw, positives, exps, at):
    top = jnp.max(raw[...], axis=0, keepdims=True)
    total = jnp.zeros_like(top)
    pos_score = jnp.zeros_like(top)
    row = 0
    for offset, start, n in rows:
        part = raw[row : row + n, :]
        e = jnp.exp2((part - top) * TO_EXP2)
        exps[row : row + n, at] = e
        total += jnp.sum(e, axis=0, keepdims=True)
        hit = lax.broadcasted_iota(jnp.int32, part.shape, 0) == positives - (first_passage(where, offset) + start)
        pos_score += jnp.sum(jnp.where(hit, part, 0.0), axis=0, keepdims=True)
        row += n
    return top * SCALE, total, pos_score * SCALE


def product(p, q):
    return lax.dot_general(p, q, (((1,), (1,)), ((), ())), preferred_element_type=F32)


def score_blocks(where, q, passages, positives, first, raws, exps, stats):
    raws[0][...] = product(passages[...], q[0:256, :])
    for i in range(4):
        if i < 3:
            raws[(i + 1) % 2][...] = product(passages[...], q[(i + 1) * 256 : (i + 2) * 256, :])
        at, row = slice(i * 256, (i + 1) * 256), slice(first + i, first + i + 1)
        top, total, pos_score = softmax(where, NEAR + FAR, raws[i % 2], positives[row, :], exps, at)
        stats[row, 0:256] = top
        stats[row, 256:512] = total
        stats[row, 512:768] = pos_score


def own_scores_kernel(where, q, positives, *refs):
    pieces, (exps, stats, passages, *raws) = refs[: len(NEAR) + 2], refs[len(NEAR) + 2 :]
    largest_q, row = None, 0
    for ref in pieces:
        n = ref.shape[0] - TILE
        passages[row : row + n, :] = ref[:n, :]
        v = ref[n : n + 1, :128].astype(F32)
        largest_q = v if largest_q is None else jnp.maximum(largest_q, v)
        row += n
    stats[0:4, 768:] = jnp.broadcast_to(largest_q, (4, 128))
    stats[4:8, 768:] = jnp.broadcast_to(largest(passages[...]), (4, 128))
    score_blocks(where, q, passages, positives, 0, raws, exps, stats)


def other_scores_kernel(where, q, pos_own, pos_other, passages, own_stats, exps, stats, positives, *raws):
    positives[:4, :] = pos_own[:4, :]
    positives[4:, :] = pos_other[:4, :]
    stats[0:4, :] = own_stats[0:4, :]
    stats[4:8, 768:] = own_stats[4:8, 768:]
    score_blocks(where, q, passages, positives, 4, raws, exps, stats)


def merge_stats(parts):
    top = functools.reduce(jnp.maximum, [p[:, 0:256] for p in parts])
    totals = [p[:, 256:512] * jnp.exp(p[:, 0:256] - top) for p in parts]
    pos_scores = [p[:, 512:768] for p in parts]
    if len(parts) == 4:
        join = lambda v: (v[0] + v[3]) + (v[1] + v[2])
    else:
        join = lambda v: v[0] + v[1]
    rest = functools.reduce(jnp.maximum, [p[:, 768:] for p in parts])
    return top, join(totals), join(pos_scores), rest


def merge_kernel(*refs):
    out = refs[-1]
    top, total, pos_score, rest = merge_stats([r[...] for r in refs[:-1]])
    out[:, 0:256] = top
    out[:, 256:512] = total
    out[:, 512:768] = pos_score
    out[:, 768:] = rest


def finish_kernel(local, one, two, out):
    two = jnp.concatenate(
        [jnp.concatenate([two[4:8, :768], two[0:4, :768]], axis=0), two[:, 768:]], axis=1
    )
    top, total, pos_score, rest = merge_stats([one[...], two])
    lse = top + jnp.log(total)
    out[:, 0:256] = jnp.exp(local[:, 0:256] - lse)
    out[:, 256:512] = jnp.zeros_like(lse)
    out[:, 512:768] = lse - pos_score
    bound_p = (NQ * SCALE) * jnp.maximum(rest[0:1, :], 1e-30)
    bound_q = (2.0 * SCALE) * jnp.maximum(rest[4:5, :], 1e-30)
    out[0:1, 768:] = LARGEST / bound_p
    out[1:2, 768:] = bound_p / LARGEST
    out[2:3, 768:] = LARGEST / bound_q
    out[3:4, 768:] = bound_q / LARGEST
    out[4:8, 768:] = jnp.zeros((4, 128), F32)


def weigh(where, rows, exps, positives, coef, first, weights):
    for i in range(4):
        at = slice(i * 256, (i + 1) * 256)
        factor = coef[first + i : first + i + 1, 0:256]
        pos = positives[first + i : first + i + 1, :]
        row = 0
        for offset, start, n, r in rows:
            hit = lax.broadcasted_iota(jnp.int32, (n, 256), 0) == pos - (first_passage(where, offset) + start)
            weights[row : row + n, at] = ((exps[r : r + n, at] * factor - hit.astype(F32)) * SCALE).astype(BF)
            row += n


def scaled_terms(w_own, w_other, q_own, q_other, scale, at):
    g = jnp.dot(w_own[...], q_own[:, at], preferred_element_type=F32)
    return (g + jnp.dot(w_other[...], q_other[:, at], preferred_element_type=F32)) * scale


BLOCKS = [(o, s, n, 128 * i) for i, (o, s, n) in enumerate(NEAR)]
FAR_BLOCKS = [(o, s, n, N_NEAR + s) for o, s, n in FAR]


def first_terms_kernel(
    where, own_exps, other_exps, q_own, q_other, positives, coef,
    right, left, term_right, w_own, w_other, *_,
):
    rows = FAR_BLOCKS + BLOCKS[1:3]
    weigh(where, rows, own_exps, positives, coef, 0, w_own)
    weigh(where, rows, other_exps, positives, coef, 4, w_other)
    for j in range(4):
        at = slice(j * 256, (j + 1) * 256)
        g = scaled_terms(w_own, w_other, q_own, q_other, coef[0:1, 768:769], at)
        right[:, at] = encode(g[:128])
        left[:, at] = encode(g[128:256])
        term_right[:, at] = g[256:]


def other_terms_kernel(
    where, own_exps, other_exps, q_own, q_other, positives, coef, *outs
):
    grads, (w_own, w_other) = outs[:5], outs[5:]
    rows = [BLOCKS[0], *BLOCKS[3:]]
    weigh(where, rows, own_exps, positives, coef, 0, w_own)
    weigh(where, rows, other_exps, positives, coef, 4, w_other)
    for j in range(4):
        at = slice(j * 256, (j + 1) * 256)
        g = scaled_terms(w_own, w_other, q_own, q_other, coef[0:1, 768:769], at)
        for i, ref in enumerate(grads):
            ref[:, at] = g[i * 128 : (i + 1) * 128]


def add_first_kernel(received, term, other0, other1, out, *_):
    out[...] = encode(term[...] + decode(received[...]))


def add_kernel(received, term, *refs):
    out = refs[-1]
    out[...] = encode(term[...] + decode(received[...]))


def last_add_kernel(coef, from_left, from_right, term, out):
    out[...] = (term[...] + (decode(from_left[...]) + decode(from_right[...]))) * coef[1:2, 768:769]


GROUPS = ((1, 0, 128), (0, 128, 384), (1, 128, 640), (0, 0, 128))


def query_terms(own, where, passages, coef, w0, w1, w):
    _, second = axes_of(where, where[3] if own else 1 - where[3])
    for i in range(4):
        at = pl.ds(pl.multiple_of(lax.rem(second + i, 4) * 256, 256), 256)
        row = 0
        for k, u, v in GROUPS:
            w[row : row + v - u, i * 256 : (i + 1) * 256] = (w0, w1)[k][u:v, at]
            row += v - u
    g = lax.dot_general(w[...], passages[...], (((0,), (0,)), ((), ())), preferred_element_type=F32)
    return g * coef[2:3, 768:769]


def row_of(where, b):
    first, _ = axes_of(where, where[3])
    return pl.ds(pl.multiple_of(lax.rem(b - first + 4, 4) * 64, 64), 64)


def send_queries_kernel(where, passages, coef, w0, w1, out0, out1, w):
    g = encode(query_terms(False, where, passages, coef, w0, w1, w))
    out0[...] = g[:512, :]
    out1[...] = g[512:, :]


def keep_queries_kernel(where, passages, coef, w0, w1, other0, other1, keep, *refs):
    sent, w = refs[:-1], refs[-1]
    terms = query_terms(True, where, passages, coef, w0, w1, w)
    for i, ref in enumerate((keep, *sent)):
        g = terms[i * 256 : (i + 1) * 256, :] + decode((other0, other1)[i // 2][i % 2 * 256 : (i % 2 + 1) * 256, :])
        g = g if i == 0 else encode(g)
        for b in range(4):
            ref[row_of(where, b), :] = g[b * 64 : (b + 1) * 64, :]


def add_queries_kernel(own, a, b, c, keep, *sent):
    total = (own[...] + decode(b[...])) + (decode(a[...]) + decode(c[...]))
    keep[...] = total[:64, :]
    for i, ref in enumerate(sent):
        ref[...] = encode(total[(i + 1) * 64 : (i + 2) * 64, :])


def last_queries_kernel(coef, own, a, b, c, out):
    total = (own[...] + decode(b[...])) + (decode(a[...]) + decode(c[...]))
    out[...] = total * coef[3:4, 768:769]


def body(queries, passages, positives):
    x, y, z, c = (lax.axis_index(a) for a in ("x", "y", "z", "core"))
    where = jnp.stack([x, y, z, c]).astype(jnp.int32)
    bf = lambda n: ((n, D), BF)
    f32 = lambda n: ((n, D), F32)

    (packed,) = call(pack_passages_kernel, "pack_passages", [bf(144)], (passages, queries))
    z1r, z1l = shift_z(packed, 1), shift_z(packed, -1)
    z2r, z2l = shift_z(z1r, 1), shift_z(z1l, -1)
    z3r, z3l = shift_z(z2r, 1), shift_z(z2l, -1)
    far0, far1 = call(cut_kernel, "cut", [bf(80)] * 2, (z3r, z3l))
    far0, far1 = shift_z(far0, 1), shift_z(far1, -1)
    args = (where, queries, positives.reshape(4, 128))
    (q,) = call(pack_queries_kernel, "pack_queries", [bf(80)], args, smem=1)
    (q,) = call(round1_kernel, "round1", [bf(272)], (q, *(shift_plane(q, 0, k) for k in (1, -1, 2))))
    q_right, q_left = shift_plane(q, 1, 1), shift_plane(q, 1, -1)
    q_right2, q_left2 = call(round2_kernel, "round2", [bf(144)] * 2, (q_right, q_left, z3r, z3l))
    q_right2, q_left2 = shift_plane(q_right2, 1, 1), shift_plane(q_left2, 1, -1)
    args = (where, q, q_right, q_left, q_right2, q_left2, far0, far1)
    outs = [bf(1024), ((8, 256), jnp.int32)]
    scratch = [pltpu.VMEM((16, 128), jnp.int32)]
    q_own, pos_own = call(round3_kernel, "round3", outs, args, scratch=scratch, smem=1)
    q_other, pos_other = swap_core(q_own), swap_core(pos_own)

    raws = [pltpu.VMEM((1024, 256), F32)] * 2
    outs = [((1024, 1024), F32), ((8, 896), F32), bf(1024)]
    args = (where, q_own, pos_own, packed, z3r, z3l, z2r, z2l, z1r, z1l, far0, far1)
    own_exps, stats, p_all = call(own_scores_kernel, "own_scores", outs, args, scratch=raws, mib=16, smem=1)
    outs = [((1024, 1024), F32), ((8, 896), F32), ((8, 256), jnp.int32)]
    args = (where, q_other, pos_own, pos_other, p_all, stats)
    other_exps, stats, pos = call(other_scores_kernel, "other_scores", outs, args, scratch=raws, mib=16, smem=1)
    local = stats

    for shift in (shift_x, shift_y):
        args = [stats] + [shift(stats, k) for k in (1, -1, 2)]
        (stats,) = call(merge_kernel, "merge", [((8, 896), F32)], args)
    (coef,) = call(finish_kernel, "finish", [((8, 896), F32)], (local, stats, swap_core(stats)))

    args = (where, own_exps, other_exps, q_own, q_other, pos, coef)
    outs = [bf(128), bf(128), f32(128), bf(384), bf(384), ((8, 896), F32)]
    right, left, right3, w0_own, w0_other, coef = call(
        first_terms_kernel, "first_terms", outs, args, mib=16, smem=1, alias={6: 5}
    )
    losses, done = call(losses_kernel, "losses", [((4, 128), F32), ((8, 128), F32)], (where, coef), smem=1)
    right, left = shift_z(right, 1), shift_z(left, -1)
    args = (where, own_exps, other_exps, q_own, q_other, pos, coef)
    outs = [f32(128)] * 5 + [bf(640)] * 2
    own, left2, right2, left1, right1, w1_own, w1_other = call(
        other_terms_kernel, "other_terms", outs, args, mib=16, smem=1
    )
    args = (where, p_all, coef, w0_other, w1_other)
    other0, other1 = call(
        send_queries_kernel, "send_queries", [bf(512)] * 2, args, scratch=[pltpu.VMEM((1024, 1024), BF)], mib=20, smem=1
    )
    outs = [bf(128), bf(512), bf(512)]
    args = (right, right3, other0, other1)
    right, other0, other1 = call(add_first_kernel, "add_first", outs, args, alias={2: 1, 3: 2})
    right = shift_z(right, 1)
    (left,) = call(add_kernel, "add_left", [bf(128)], (left, left2))
    left = shift_z(left, -1)
    (right,) = call(add_kernel, "add_right", [bf(128)], (right, right2))
    right = shift_z(right, 1)
    (left,) = call(add_kernel, "add_left", [bf(128)], (left, left1))
    left = shift_z(left, -1)
    (right,) = call(add_kernel, "add_right", [bf(128)], (right, right1, done))
    right = shift_z(right, 1)
    (passage_grad,) = call(last_add_kernel, "last_add", [f32(128)], (coef, right, left, own))

    args = (where, p_all, coef, w0_own, w1_own, swap_core(other0), swap_core(other1))
    outs = [f32(256)] + [bf(256)] * 3
    keep, *sent = call(
        keep_queries_kernel, "keep_queries", outs, args, scratch=[pltpu.VMEM((1024, 1024), BF)], mib=20, smem=1
    )
    moved = [shift_plane(v, 1, k + 1) for k, v in enumerate(sent)]
    outs = [f32(64)] + [bf(64)] * 3
    keep, *sent = call(add_queries_kernel, "add_queries", outs, (keep, *moved))
    moved = [shift_plane(v, 0, k + 1) for k, v in enumerate(sent)]
    (query_grad,) = call(last_queries_kernel, "last_queries", [f32(64)], (coef, keep, *moved))
    return losses.reshape(512), query_grad, passage_grad


def solution(mesh):
    mesh = Mesh(mesh.devices.reshape(Y, Z, X, C), ("y", "z", "x", "core"))
    q_spec = P(("y", "z", "x", "core"), None)
    p_spec = P(("x", "core", "y", "z"), None)
    row_spec = P(("y", "z"))
    return jax.shard_map(
        body,
        mesh=mesh,
        in_specs=(q_spec, p_spec, row_spec),
        out_specs=(row_spec, q_spec, p_spec),
        check_vma=False,
    )
```

```python
import functools
import math

import jax
import jax.numpy as jnp
from jax import lax
from jax.experimental import pallas as pl
from jax.experimental.pallas import tpu as pltpu
from jax.sharding import Mesh, PartitionSpec as P

D = 1024
NQ = 16384
SCALE = 3.0 / math.sqrt(D)
TO_EXP2 = SCALE * math.log2(math.e)
X, Y, Z, C = 4, 4, 8, 2
PLANE = ("y", "x", "core")
BF, F32 = jnp.bfloat16, jnp.float32
MIB = 1 << 20
LARGEST = 46000.0
NEAR = ((0, 0, 128), (-3, 0, 128), (3, 0, 128), (-2, 0, 128), (2, 0, 128), (-1, 0, 128), (1, 0, 128))
FAR = ((4, 0, 64), (4, 64, 64))
N_NEAR, N_FAR = 896, 128
TILE = 16
VMEM = pl.BlockSpec(memory_space=pltpu.VMEM)
SMEM = pl.BlockSpec(memory_space=pltpu.SMEM)


def call(kernel, name, outs, args, scratch=(), mib=8, smem=0, alias=None):
    return pl.pallas_call(
        kernel,
        out_shape=[jax.ShapeDtypeStruct(s, t) for s, t in outs],
        in_specs=[SMEM] * smem + [VMEM] * (len(args) - smem),
        out_specs=[VMEM] * len(outs),
        scratch_shapes=list(scratch),
        input_output_aliases=alias or {},
        compiler_params=pltpu.CompilerParams(vmem_limit_bytes=mib * MIB),
        cost_estimate=pl.CostEstimate(flops=1000, bytes_accessed=1024, transcendentals=0),
        name=name,
    )(*args)


def shift_z(v, k):
    return lax.ppermute(v, "z", [(i, (i + k) % Z) for i in range(Z)])


def shift_x(v, k):
    return lax.ppermute(v, "x", [(i, (i + k) % X) for i in range(X)])


def shift_y(v, k):
    return lax.ppermute(v, "y", [(i, (i + k) % Y) for i in range(Y)])


def swap_core(v):
    return lax.ppermute(v, "core", [(0, 1), (1, 0)])


def shift_plane(v, stage, k):
    pairs = []
    for y in range(Y):
        for x in range(X):
            for c in range(C):
                y2, x2 = (y, (x + k) % X) if c == stage else ((y + k) % Y, x)
                pairs.append(((y * X + x) * C + c, (y2 * X + x2) * C + c))
    return lax.ppermute(v, PLANE, pairs)


def encode(v):
    v2 = v * v
    v4 = v2 * v2
    v8 = v4 * v4
    return jnp.where(v < 0, -v8, v8).astype(BF)


def decode(code):
    y = code.astype(F32)
    size = jnp.abs(y)
    v = jnp.exp2(jnp.log2(jnp.maximum(size, 1e-37)) * 0.125)
    v = jnp.where(size < 1e-37, 0.0, v)
    return jnp.where(y < 0, -v, v)


def axes_of(where, c):
    x, y = where[0], where[1]
    return jnp.where(c == 0, x, y), jnp.where(c == 0, y, x)


def largest(v):
    v = jnp.max(jnp.abs(v).astype(F32), axis=0, keepdims=True)
    return jnp.max(v, axis=1, keepdims=True)


def rows_like(tile):
    return lax.broadcasted_iota(jnp.int32, tile.shape, 0)


def pack_passages_kernel(passages, queries, out):
    out[:128, :] = passages[...]
    out[128:, :] = jnp.broadcast_to(largest(queries[...]), (TILE, D)).astype(BF)


def pack_queries_kernel(where, queries, positives, out):
    out[:64, :] = queries[...]
    out[64:, :] = jnp.zeros((TILE, D), BF)
    pos = positives[pl.ds(where[0], 1), :]
    pos = jnp.where(where[3] == 0, pos, jnp.concatenate([pos[:, 64:], pos[:, :64]], axis=1))
    tile = jnp.zeros((TILE, 128), F32)
    for i, part in enumerate((lax.shift_right_logical(pos, 8), jnp.bitwise_and(pos, 255))):
        tile = jnp.where(rows_like(tile) == i, part.astype(F32), tile)
    out[64:, :128] = tile.astype(BF)


def round1_kernel(q0, q1, q2, q3, out):
    tile = jnp.zeros((TILE, 128), F32)
    for i, ref in enumerate((q0, q1, q2, q3)):
        out[i * 64 : (i + 1) * 64, :] = ref[:64, :]
        part = ref[64:, :128].astype(F32)
        tile = jnp.where(rows_like(tile) == i, part[0:1, :], tile)
        tile = jnp.where(rows_like(tile) == 4 + i, part[1:2, :], tile)
    out[256:, :] = jnp.zeros((TILE, D), BF)
    out[256:, :128] = tile.astype(BF)


def cut_kernel(z_right, z_left, far_right, far_left):
    far_right[:64, :] = z_right[:64, :]
    far_right[64:, :] = z_right[128:, :]
    far_left[...] = z_left[64:, :]


def round2_kernel(q_right, q_left, z_right, z_left, right, left):
    right[:128, :] = q_right[:128, :]
    right[128:, :] = q_right[256:, :]
    left[...] = q_left[128:, :]


def round3_kernel(where, own, right, left, right2, left2, far0, far1, out, positives, scratch):
    first, second = axes_of(where, where[3])
    for i, (ref, part, n) in enumerate(((own, 0, 4), (right, 0, 4), (left, 0, 4), (right2, 0, 2), (left2, 2, 2))):
        a = lax.rem(second + (0, 3, 1, 2, 2)[i], 4)
        tile = ref[n * 64 :, :128].astype(F32)
        for j in range(part, part + n):
            b = lax.rem(first + (0, 3, 1, 2)[j], 4)
            at = pl.ds(pl.multiple_of((a * 4 + b) * 64, 64), 64)
            out[at, :] = ref[(j - part) * 64 : (j - part + 1) * 64, :]
            pos = tile[j : j + 1, :] * 256.0 + tile[4 + j : 5 + j, :]
            scratch[pl.ds(a * 4 + b, 1), :] = pos.astype(jnp.int32)
    positives[...] = jnp.zeros((8, 256), jnp.int32)
    for a in range(4):
        for b in range(4):
            positives[a : a + 1, b * 64 : b * 64 + 64] = scratch[a * 4 + b : a * 4 + b + 1, :64]


def losses_kernel(where, coef, out, done):
    done[...] = jnp.zeros((8, 128), F32)
    y, c = where[1], where[3]
    v = coef[:, 512:768]
    core0, core1 = jnp.where(c == 0, v[:4], v[4:]), jnp.where(c == 0, v[4:], v[:4])
    for x in range(4):
        a, b = core0[0:1, x * 64 : x * 64 + 64], core1[x : x + 1, :64]
        for k in range(1, 4):
            a = jnp.where(y == k, core0[k : k + 1, x * 64 : x * 64 + 64], a)
            b = jnp.where(y == k, core1[x : x + 1, k * 64 : k * 64 + 64], b)
        out[x : x + 1, :64] = a
        out[x : x + 1, 64:] = b


def first_passage(where, offset):
    x, y, z, c = where[0], where[1], where[2], where[3]
    return (((x * C + c) * Y + y) * Z + lax.rem(z + offset + Z, Z)) * 128


def softmax(where, rows, raw, positives, exps, at):
    top = jnp.max(raw[...], axis=0, keepdims=True)
    total = jnp.zeros_like(top)
    pos_score = jnp.zeros_like(top)
    row = 0
    for offset, start, n in rows:
        part = raw[row : row + n, :]
        e = jnp.exp2((part - top) * TO_EXP2)
        exps[row : row + n, at] = e
        total += jnp.sum(e, axis=0, keepdims=True)
        hit = lax.broadcasted_iota(jnp.int32, part.shape, 0) == positives - (first_passage(where, offset) + start)
        pos_score += jnp.sum(jnp.where(hit, part, 0.0), axis=0, keepdims=True)
        row += n
    return top * SCALE, total, pos_score * SCALE


def product(p, q):
    return lax.dot_general(p, q, (((1,), (1,)), ((), ())), preferred_element_type=F32)


def score_blocks(where, q, passages, positives, first, raws, exps, stats):
    raws[0][...] = product(passages[...], q[0:256, :])
    for i in range(4):
        if i < 3:
            raws[(i + 1) % 2][...] = product(passages[...], q[(i + 1) * 256 : (i + 2) * 256, :])
        at, row = slice(i * 256, (i + 1) * 256), slice(first + i, first + i + 1)
        top, total, pos_score = softmax(where, NEAR + FAR, raws[i % 2], positives[row, :], exps, at)
        stats[row, 0:256] = top
        stats[row, 256:512] = total
        stats[row, 512:768] = pos_score


def own_scores_kernel(where, q, positives, *refs):
    pieces, (exps, stats, passages, *raws) = refs[: len(NEAR) + 2], refs[len(NEAR) + 2 :]
    largest_q, row = None, 0
    for ref in pieces:
        n = ref.shape[0] - TILE
        passages[row : row + n, :] = ref[:n, :]
        v = ref[n : n + 1, :128].astype(F32)
        largest_q = v if largest_q is None else jnp.maximum(largest_q, v)
        row += n
    stats[0:4, 768:] = jnp.broadcast_to(largest_q, (4, 128))
    stats[4:8, 768:] = jnp.broadcast_to(largest(passages[...]), (4, 128))
    score_blocks(where, q, passages, positives, 0, raws, exps, stats)


def other_scores_kernel(where, q, pos_own, pos_other, passages, own_stats, exps, stats, positives, *raws):
    positives[:4, :] = pos_own[:4, :]
    positives[4:, :] = pos_other[:4, :]
    stats[0:4, :] = own_stats[0:4, :]
    stats[4:8, 768:] = own_stats[4:8, 768:]
    score_blocks(where, q, passages, positives, 4, raws, exps, stats)


def merge_stats(parts):
    top = functools.reduce(jnp.maximum, [p[:, 0:256] for p in parts])
    totals = [p[:, 256:512] * jnp.exp(p[:, 0:256] - top) for p in parts]
    pos_scores = [p[:, 512:768] for p in parts]
    if len(parts) == 4:
        join = lambda v: (v[0] + v[3]) + (v[1] + v[2])
    else:
        join = lambda v: v[0] + v[1]
    rest = functools.reduce(jnp.maximum, [p[:, 768:] for p in parts])
    return top, join(totals), join(pos_scores), rest


def merge_kernel(*refs):
    out = refs[-1]
    top, total, pos_score, rest = merge_stats([r[...] for r in refs[:-1]])
    out[:, 0:256] = top
    out[:, 256:512] = total
    out[:, 512:768] = pos_score
    out[:, 768:] = rest


def finish_kernel(local, one, two, out):
    two = jnp.concatenate(
        [jnp.concatenate([two[4:8, :768], two[0:4, :768]], axis=0), two[:, 768:]], axis=1
    )
    top, total, pos_score, rest = merge_stats([one[...], two])
    lse = top + jnp.log(total)
    out[:, 0:256] = jnp.exp(local[:, 0:256] - lse)
    out[:, 256:512] = jnp.zeros_like(lse)
    out[:, 512:768] = lse - pos_score
    bound_p = (NQ * SCALE) * jnp.maximum(rest[0:1, :], 1e-30)
    bound_q = (2.0 * SCALE) * jnp.maximum(rest[4:5, :], 1e-30)
    out[0:1, 768:] = LARGEST / bound_p
    out[1:2, 768:] = bound_p / LARGEST
    out[2:3, 768:] = LARGEST / bound_q
    out[3:4, 768:] = bound_q / LARGEST
    out[4:8, 768:] = jnp.zeros((4, 128), F32)


def weigh(where, rows, exps, positives, coef, first, weights):
    for i in range(4):
        at = slice(i * 256, (i + 1) * 256)
        factor = coef[first + i : first + i + 1, 0:256]
        pos = positives[first + i : first + i + 1, :]
        row = 0
        for offset, start, n, r in rows:
            hit = lax.broadcasted_iota(jnp.int32, (n, 256), 0) == pos - (first_passage(where, offset) + start)
            weights[row : row + n, at] = ((exps[r : r + n, at] * factor - hit.astype(F32)) * SCALE).astype(BF)
            row += n


def scaled_terms(w_own, w_other, q_own, q_other, scale, at):
    g = jnp.dot(w_own[...], q_own[:, at], preferred_element_type=F32)
    return (g + jnp.dot(w_other[...], q_other[:, at], preferred_element_type=F32)) * scale


BLOCKS = [(o, s, n, 128 * i) for i, (o, s, n) in enumerate(NEAR)]
FAR_BLOCKS = [(o, s, n, N_NEAR + s) for o, s, n in FAR]


def first_terms_kernel(
    where, own_exps, other_exps, q_own, q_other, positives, coef,
    right, left, term_right, w_own, w_other, *_,
):
    rows = FAR_BLOCKS + BLOCKS[1:3]
    weigh(where, rows, own_exps, positives, coef, 0, w_own)
    weigh(where, rows, other_exps, positives, coef, 4, w_other)
    for j in range(4):
        at = slice(j * 256, (j + 1) * 256)
        g = scaled_terms(w_own, w_other, q_own, q_other, coef[0:1, 768:769], at)
        right[:, at] = encode(g[:128])
        left[:, at] = encode(g[128:256])
        term_right[:, at] = g[256:]


def other_terms_kernel(
    where, own_exps, other_exps, q_own, q_other, positives, coef, *outs
):
    grads, (w_own, w_other) = outs[:5], outs[5:]
    rows = [BLOCKS[0], *BLOCKS[3:]]
    weigh(where, rows, own_exps, positives, coef, 0, w_own)
    weigh(where, rows, other_exps, positives, coef, 4, w_other)
    for j in range(4):
        at = slice(j * 256, (j + 1) * 256)
        g = scaled_terms(w_own, w_other, q_own, q_other, coef[0:1, 768:769], at)
        for i, ref in enumerate(grads):
            ref[:, at] = g[i * 128 : (i + 1) * 128]


def add_first_kernel(received, term, other0, other1, out, *_):
    out[...] = encode(term[...] + decode(received[...]))


def add_kernel(received, term, *refs):
    out = refs[-1]
    out[...] = encode(term[...] + decode(received[...]))


def last_add_kernel(coef, from_left, from_right, term, out):
    out[...] = (term[...] + (decode(from_left[...]) + decode(from_right[...]))) * coef[1:2, 768:769]


GROUPS = ((1, 0, 128), (0, 128, 384), (1, 128, 640), (0, 0, 128))


def query_terms(own, where, passages, coef, w0, w1, w):
    _, second = axes_of(where, where[3] if own else 1 - where[3])
    for i in range(4):
        at = pl.ds(pl.multiple_of(lax.rem(second + i, 4) * 256, 256), 256)
        row = 0
        for k, u, v in GROUPS:
            w[row : row + v - u, i * 256 : (i + 1) * 256] = (w0, w1)[k][u:v, at]
            row += v - u
    g = lax.dot_general(w[...], passages[...], (((0,), (0,)), ((), ())), preferred_element_type=F32)
    return g * coef[2:3, 768:769]


def row_of(where, b):
    first, _ = axes_of(where, where[3])
    return pl.ds(pl.multiple_of(lax.rem(b - first + 4, 4) * 64, 64), 64)


def send_queries_kernel(where, passages, coef, w0, w1, out0, out1, w):
    g = encode(query_terms(False, where, passages, coef, w0, w1, w))
    out0[...] = g[:512, :]
    out1[...] = g[512:, :]


def keep_queries_kernel(where, passages, coef, w0, w1, other0, other1, keep, next_, direct, relay, term_left, w, quarter):
    terms = query_terms(True, where, passages, coef, w0, w1, w)
    for i, ref in enumerate((keep, next_, quarter, term_left)):
        g = terms[i * 256 : (i + 1) * 256, :] + decode((other0, other1)[i // 2][i % 2 * 256 : (i % 2 + 1) * 256, :])
        g = encode(g) if i in (1, 2) else g
        for b in range(4):
            ref[row_of(where, b), :] = g[b * 64 : (b + 1) * 64, :]
    direct[...] = quarter[:128, :]
    relay[...] = quarter[128:, :]


def relay_queries_kernel(received, term, out):
    out[:128, :] = encode(term[:128, :])
    out[128:, :] = encode(term[128:, :] + decode(received[...]))


def add_queries_kernel(own, a, b, c, keep, *sent):
    total = own[...] + (decode(a[...]) + decode(c[...]))
    total = jnp.concatenate([total[:128, :] + decode(b[...]), total[128:, :]], axis=0)
    keep[...] = total[:64, :]
    for i, ref in enumerate(sent):
        ref[...] = encode(total[(i + 1) * 64 : (i + 2) * 64, :])


def last_queries_kernel(coef, own, a, b, c, out):
    total = (own[...] + decode(b[...])) + (decode(a[...]) + decode(c[...]))
    out[...] = total * coef[3:4, 768:769]


def body(queries, passages, positives):
    x, y, z, c = (lax.axis_index(a) for a in ("x", "y", "z", "core"))
    where = jnp.stack([x, y, z, c]).astype(jnp.int32)
    bf = lambda n: ((n, D), BF)
    f32 = lambda n: ((n, D), F32)

    (packed,) = call(pack_passages_kernel, "pack_passages", [bf(144)], (passages, queries))
    z1r, z1l = shift_z(packed, 1), shift_z(packed, -1)
    z2r, z2l = shift_z(z1r, 1), shift_z(z1l, -1)
    z3r, z3l = shift_z(z2r, 1), shift_z(z2l, -1)
    far0, far1 = call(cut_kernel, "cut", [bf(80)] * 2, (z3r, z3l))
    far0, far1 = shift_z(far0, 1), shift_z(far1, -1)
    args = (where, queries, positives.reshape(4, 128))
    (q,) = call(pack_queries_kernel, "pack_queries", [bf(80)], args, smem=1)
    (q,) = call(round1_kernel, "round1", [bf(272)], (q, *(shift_plane(q, 0, k) for k in (1, -1, 2))))
    q_right, q_left = shift_plane(q, 1, 1), shift_plane(q, 1, -1)
    q_right2, q_left2 = call(round2_kernel, "round2", [bf(144)] * 2, (q_right, q_left, z3r, z3l))
    q_right2, q_left2 = shift_plane(q_right2, 1, 1), shift_plane(q_left2, 1, -1)
    args = (where, q, q_right, q_left, q_right2, q_left2, far0, far1)
    outs = [bf(1024), ((8, 256), jnp.int32)]
    scratch = [pltpu.VMEM((16, 128), jnp.int32)]
    q_own, pos_own = call(round3_kernel, "round3", outs, args, scratch=scratch, smem=1)
    q_other, pos_other = swap_core(q_own), swap_core(pos_own)

    raws = [pltpu.VMEM((1024, 256), F32)] * 2
    outs = [((1024, 1024), F32), ((8, 896), F32), bf(1024)]
    args = (where, q_own, pos_own, packed, z3r, z3l, z2r, z2l, z1r, z1l, far0, far1)
    own_exps, stats, p_all = call(own_scores_kernel, "own_scores", outs, args, scratch=raws, mib=16, smem=1)
    outs = [((1024, 1024), F32), ((8, 896), F32), ((8, 256), jnp.int32)]
    args = (where, q_other, pos_own, pos_other, p_all, stats)
    other_exps, stats, pos = call(other_scores_kernel, "other_scores", outs, args, scratch=raws, mib=16, smem=1)
    local = stats

    for shift in (shift_x, shift_y):
        args = [stats] + [shift(stats, k) for k in (1, -1, 2)]
        (stats,) = call(merge_kernel, "merge", [((8, 896), F32)], args)
    (coef,) = call(finish_kernel, "finish", [((8, 896), F32)], (local, stats, swap_core(stats)))

    args = (where, own_exps, other_exps, q_own, q_other, pos, coef)
    outs = [bf(128), bf(128), f32(128), bf(384), bf(384), ((8, 896), F32)]
    right, left, right3, w0_own, w0_other, coef = call(
        first_terms_kernel, "first_terms", outs, args, mib=16, smem=1, alias={6: 5}
    )
    losses, done = call(losses_kernel, "losses", [((4, 128), F32), ((8, 128), F32)], (where, coef), smem=1)
    right, left = shift_z(right, 1), shift_z(left, -1)
    args = (where, own_exps, other_exps, q_own, q_other, pos, coef)
    outs = [f32(128)] * 5 + [bf(640)] * 2
    own, left2, right2, left1, right1, w1_own, w1_other = call(
        other_terms_kernel, "other_terms", outs, args, mib=16, smem=1
    )
    args = (where, p_all, coef, w0_other, w1_other)
    other0, other1 = call(
        send_queries_kernel, "send_queries", [bf(512)] * 2, args, scratch=[pltpu.VMEM((1024, 1024), BF)], mib=20, smem=1
    )
    outs = [bf(128), bf(512), bf(512)]
    args = (right, right3, other0, other1)
    right, other0, other1 = call(add_first_kernel, "add_first", outs, args, alias={2: 1, 3: 2})
    right = shift_z(right, 1)
    (left,) = call(add_kernel, "add_left", [bf(128)], (left, left2))
    left = shift_z(left, -1)
    (right,) = call(add_kernel, "add_right", [bf(128)], (right, right2))
    right = shift_z(right, 1)
    (left,) = call(add_kernel, "add_left", [bf(128)], (left, left1))
    left = shift_z(left, -1)
    (right,) = call(add_kernel, "add_right", [bf(128)], (right, right1, done))
    right = shift_z(right, 1)
    (passage_grad,) = call(last_add_kernel, "last_add", [f32(128)], (coef, right, left, own))

    args = (where, p_all, coef, w0_own, w1_own, swap_core(other0), swap_core(other1))
    outs = [f32(256), bf(256), bf(128), bf(128), f32(256)]
    scratch = [pltpu.VMEM((1024, 1024), BF), pltpu.VMEM((256, D), BF)]
    keep, next_, direct, relay, term_left = call(
        keep_queries_kernel, "keep_queries", outs, args, scratch=scratch, mib=20, smem=1
    )
    relay = shift_plane(relay, 1, -1)
    (relay,) = call(relay_queries_kernel, "relay_queries", [bf(256)], (relay, term_left))
    moved = [shift_plane(next_, 1, 1), shift_plane(direct, 1, 2), shift_plane(relay, 1, -1)]
    outs = [f32(64)] + [bf(64)] * 3
    keep, *sent = call(add_queries_kernel, "add_queries", outs, (keep, *moved))
    moved = [shift_plane(v, 0, k + 1) for k, v in enumerate(sent)]
    (query_grad,) = call(last_queries_kernel, "last_queries", [f32(64)], (coef, keep, *moved))
    return losses.reshape(512), query_grad, passage_grad


def solution(mesh):
    mesh = Mesh(mesh.devices.reshape(Y, Z, X, C), ("y", "z", "x", "core"))
    q_spec = P(("y", "z", "x", "core"), None)
    p_spec = P(("x", "core", "y", "z"), None)
    row_spec = P(("y", "z"))
    return jax.shard_map(
        body,
        mesh=mesh,
        in_specs=(q_spec, p_spec, row_spec),
        out_specs=(row_spec, q_spec, p_spec),
        check_vma=False,
    )
```
